128 devices in a mesh: dp: 16 (over y, x_lo, core), sp: 8 (over x_hi, z).
Axes of the slice: x: 4 (x_hi: 2, x_lo: 2; x = x_hi * 2 + x_lo), y: 4, z: 4, core: 2. Of those that a mesh axis runs over, the one named last changes fastest.
Arguments:
- tokens: bfloat16 [16384, 2048], P(('dp', 'sp')), may hold values from -6 to 6
- cotangent: bfloat16 [16384, 2048], P(('dp', 'sp')), may hold values from -6 to 6
- chosen: int32 [16384, 2], P(('dp', 'sp')), may hold values from 0 to 3, all different within a row; in each aligned block of 128 rows (0 to 127, 128 to 255, ...) at most 80 rows name the same one
- attn_gain: bfloat16 [2048], P('dp'), may hold values from 0.099609375 to 1.8984375
- w_query: bfloat16 [2048, 3072], P('dp'), may hold values from -0.125 to 0.125
- w_kv_down: bfloat16 [2048, 576], P('dp'), may hold values from -0.125 to 0.125
- kv_gain: bfloat16 [512], P('dp'), may hold values from 0.099609375 to 1.8984375
- w_kv_up: bfloat16 [512, 4096], P('dp'), may hold values from -0.25 to 0.25
- w_out: bfloat16 [2048, 2048], P('dp'), may hold values from -2 to 2
- ffn_gain: bfloat16 [2048], P('dp'), may hold values from 0.099609375 to 1.8984375
- w_router: bfloat16 [2048, 4], P('dp'), may hold values from -0.09375 to 0.09375
- shared_gate: bfloat16 [2048, 2, 1408], P('dp'), may hold values from -0.125 to 0.125
- shared_up: bfloat16 [2048, 2, 1408], P('dp'), may hold values from -0.125 to 0.125
- shared_down: bfloat16 [1408, 2, 2048], P('dp'), may hold values from -0.109375 to 0.109375
- expert_gate: bfloat16 [2048, 4, 1408], P('dp'), may hold values from -0.125 to 0.125
- expert_up: bfloat16 [2048, 4, 1408], P('dp'), may hold values from -0.125 to 0.125
- expert_down: bfloat16 [1408, 4, 2048], P('dp'), may hold values from -0.15625 to 0.15625
Outputs:
- mixed: bfloat16 [16384, 2048], P(('dp', 'sp'))
- tokens_grad: bfloat16 [16384, 2048], P(('dp', 'sp'))
- attn_gain_grad: float32 [2048], P('dp')
- w_query_grad: float32 [2048, 3072], P('dp')
- w_kv_down_grad: float32 [2048, 576], P('dp')
- kv_gain_grad: float32 [512], P('dp')
- w_kv_up_grad: float32 [512, 4096], P('dp')
- w_out_grad: float32 [2048, 2048], P('dp')
- ffn_gain_grad: float32 [2048], P('dp')
- w_router_grad: float32 [2048, 4], P('dp')
- shared_gate_grad: float32 [2048, 2, 1408], P('dp')
- shared_up_grad: float32 [2048, 2, 1408], P('dp')
- shared_down_grad: float32 [1408, 2, 2048], P('dp')
- expert_gate_grad: float32 [2048, 4, 1408], P('dp')
- expert_up_grad: float32 [2048, 4, 1408], P('dp')
- expert_down_grad: float32 [1408, 4, 2048], P('dp')
The draws below stay inside these ranges and needn't reach their ends.
Inputs may be any that keep to these rules, and one draw needn't show every extreme that they name: `chosen`: each row names 2 different experts. Among the rows of one device (aligned blocks of 128 rows) no expert is named by more than 80 rows, and in every draw some expert is named by exactly 80 rows of some device.
All inputs are finite; a program needn't handle non-finite values.
Results may differ from the reference program's by a relative error of at most 0.025.
Values may be sent and summed in bfloat16 or wider, within the bound.
A program may use at most 576 MiB of HBM per device.

```python
import math
import jax
import jax.numpy as jnp
import numpy as np
from jax import lax

D = 2048
HEADS = 16
NOPE = 128
ROPE = 64
VDIM = 128
RANK = 512
FE = 1408
NS = 2
EXPERTS = 4
TOP = 2
SEQ = 1024
TOK_DEV = 128
TOKENS = 16384
CAP = 80


def block_levels(own_key, extent, cuts, smallest, high):
    level, own = 1.0, jax.random.fold_in(own_key, 6)
    for position, blocks in cuts:
        steps = jnp.exp(jax.random.uniform(jax.random.fold_in(own, position), (blocks,), jnp.float32, smallest / len(cuts), high / len(cuts)))
        level = level * jnp.repeat(steps, extent[position] // blocks).reshape([-1 if axis == position else 1 for axis in range(len(extent))])
    return level


def deal_out(own_key, own, number, rows, number_of, top, limit, lean):
    ranking = jax.random.permutation(own_key, number_of)
    heavy_load, common = load_shares(number_of, rows * top, limit, lean, True), load_shares(number_of, rows * top, limit, lean, False)
    places = jnp.arange(number_of)

    def named(lengths, rotation):
        used = int((lengths > 0).sum())
        fixed = max(1, used // 4)
        shifted = fixed + (places - fixed + rotation * (used - fixed)) % max(1, number_of - fixed)
        return jnp.zeros((number_of,), jnp.int32).at[ranking[jnp.where(places < fixed, places, shifted)]].set(jnp.asarray(lengths, jnp.int32))

    lengths = jnp.where(number % 4 == 0, named(heavy_load, number // 4), named(common, number - number // 4 - 1))
    mixed = jax.random.permutation(jax.random.fold_in(own, 3), number_of)
    donor, receiver = mixed[0:number_of // 2 * 2:2], mixed[1:number_of // 2 * 2:2]
    margin = jnp.minimum(lengths[donor] - 1, limit - lengths[receiver]) // 2
    margin = jnp.where((donor == ranking[0]) | (receiver == ranking[0]) | (lengths[receiver] == 0), 0, jnp.maximum(margin, 0))
    shifted = jax.random.randint(jax.random.fold_in(own, 4), (number_of // 2,), 0, 1 << 20) % (margin + 1)
    lengths = lengths.at[donor].add(-shifted).at[receiver].add(shifted)
    members = jnp.searchsorted(jnp.cumsum(lengths), jnp.arange(rows * top), side="right").astype(jnp.int32)
    listing = members.reshape(top, rows).T
    listing = listing[jax.random.permutation(jax.random.fold_in(own, 1), rows)]
    rotation = jax.random.randint(jax.random.fold_in(own, 2), (rows, 1), 0, top)
    return jnp.take_along_axis(listing, (jnp.arange(top)[None, :] + rotation) % top, axis=1)


def load_shares(amount, total, most, slope, full):
    portions = [(1 << 20) // math.isqrt(rank ** slope) + 1 for rank in range(1, amount + 1)]
    largest = most if full else min(most, max(-(-total // amount), total * portions[0] // sum(portions)))
    least = 1 if total - largest >= amount - 1 else 0
    given, rest = [largest] + [least] * (amount - 1), total - largest - least * (amount - 1)
    while rest > 0:
        movable = [i for i in range(1, amount) if given[i] < largest] or [i for i in range(1, amount) if given[i] < most]
        whole, remaining = sum([portions[i] for i in movable]), rest
        for i in movable:
            extra = min(most - given[i], max(1, remaining * portions[i] // whole), rest)
            given[i] = given[i] + extra
            rest = rest - extra
    return np.array(given)


def gaussian(stream_key, extent, spread, most, cuts=(), kind=jnp.bfloat16):
    level = block_levels(stream_key, extent, cuts, -0.22, 0.18) if cuts else 1.0
    values = jax.random.normal(stream_key, extent, jnp.float32) * spread * level
    return jnp.minimum(jnp.maximum(values, -most), most).astype(kind)


def setup_inputs(seed: int = 0) -> dict:
    streams_of = jax.random.split(jax.random.key(seed), 18)
    tokens = gaussian(streams_of[0], (TOKENS, D), 1.0, 6.0, ((0, 128),))
    cotangent = gaussian(streams_of[1], (TOKENS, D), 1.0, 6.0, ((0, 128),))
    chosen_keys = jax.random.split(jax.random.fold_in(streams_of[2], 1), TOKENS // TOK_DEV)
    chosen_turns = jax.random.permutation(jax.random.fold_in(streams_of[2], 3), TOKENS // TOK_DEV)
    chosen = jax.vmap(lambda own, number: deal_out(jax.random.fold_in(streams_of[2], 2), own, number, TOK_DEV, EXPERTS, TOP, CAP, 2))(chosen_keys, chosen_turns).reshape((TOKENS, TOP))
    attn_gain = jnp.clip(1.0 + 0.18 * jax.random.normal(streams_of[3], (D,), jnp.float32), 0.099609375, 1.8984375).astype(jnp.bfloat16)
    w_query = gaussian(streams_of[4], (D, HEADS * (NOPE + ROPE)), D ** -0.5, 0.125, ((0, 16),))
    w_kv_down = gaussian(streams_of[5], (D, RANK + ROPE), D ** -0.5, 0.125, ((0, 16),))
    kv_gain = jnp.clip(1.0 + 0.18 * jax.random.normal(streams_of[6], (RANK,), jnp.float32), 0.099609375, 1.8984375).astype(jnp.bfloat16)
    w_kv_up = gaussian(streams_of[7], (RANK, HEADS * (NOPE + VDIM)), RANK ** -0.5, 0.25, ((0, 16),))
    w_out = gaussian(streams_of[8], (HEADS * VDIM, D), (max(1, HEADS * VDIM * 4 // SEQ)) ** -0.5, 2.0, ((0, 16),))
    ffn_gain = jnp.clip(1.0 + 0.18 * jax.random.normal(streams_of[9], (D,), jnp.float32), 0.099609375, 1.8984375).astype(jnp.bfloat16)
    w_router = gaussian(streams_of[10], (D, EXPERTS), (2 * D) ** -0.5, 0.09375, ((0, 16),))
    shared_gate = gaussian(streams_of[11], (D, NS, FE), D ** -0.5, 0.125, ((0, 16),))
    shared_up = gaussian(streams_of[12], (D, NS, FE), D ** -0.5, 0.125, ((0, 16),))
    shared_down = gaussian(streams_of[13], (FE, NS, D), (NS * FE) ** -0.5, 0.109375, ((0, 16),))
    expert_gate = gaussian(streams_of[14], (D, EXPERTS, FE), D ** -0.5, 0.125, ((0, 16),))
    expert_up = gaussian(streams_of[15], (D, EXPERTS, FE), D ** -0.5, 0.125, ((0, 16),))
    expert_down = gaussian(streams_of[16], (FE, EXPERTS, D), FE ** -0.5, 0.15625, ((0, 16),))
    return dict(tokens=tokens, cotangent=cotangent, chosen=chosen, attn_gain=attn_gain, w_query=w_query, w_kv_down=w_kv_down, kv_gain=kv_gain, w_kv_up=w_kv_up, w_out=w_out, ffn_gain=ffn_gain, w_router=w_router, shared_gate=shared_gate, shared_up=shared_up, shared_down=shared_down, expert_gate=expert_gate, expert_up=expert_up, expert_down=expert_down)


@jax.custom_vjp
def low(v):
    return lax.optimization_barrier(v.astype(jnp.bfloat16)).astype(jnp.float32)

@jax.custom_vjp
def low_back(v):
    return v

def low_keep(v):
    return (low(v), None)

def low_pass(kept, grad):
    return (grad,)

def back_keep(v):
    return (v, None)

def back_low(kept, grad):
    return (low(grad),)
low.defvjp(low_keep, low_pass)
low_back.defvjp(back_keep, back_low)
epsilon = 1e-06
highest = lax.Precision.HIGHEST

def product(left_side, right_side):
    return jnp.dot(left_side, right_side, precision=highest)

def rms_norm(values, gain_vec):
    return values * lax.rsqrt(lax.optimization_barrier(jnp.mean(values * values, axis=-1, keepdims=True)) + epsilon) * gain_vec

def rotate(values, cosine, sine):
    half_dim = values.shape[-1] // 2
    first_half = values[..., :half_dim]
    second_half = values[..., half_dim:]
    return jnp.concatenate([first_half * cosine - second_half * sine, second_half * cosine + first_half * sine], axis=-1)

def rope_tables(positions):
    half_dim = ROPE // 2
    inverse = 10000.0 ** (-jnp.arange(half_dim, dtype=jnp.float32) * 2.0 / ROPE)
    angles = positions[:, None] * inverse[None, :]
    return (jnp.cos(angles), jnp.sin(angles))

def swiglu(gate_in, up_in):
    return jax.nn.silu(gate_in) * up_in

def forward(params, resid_one, chosen_rows):
    attn_gain, w_query, w_kv_down, kv_gain, w_kv_up, w_out, ffn_gain, w_router, shared_gate, shared_up, shared_down, expert_gate, expert_up, expert_down = params
    positions = jnp.arange(SEQ).astype(jnp.float32)
    cosine, sine = rope_tables(positions)
    hidden_one = low(rms_norm(resid_one, attn_gain))
    query_pre = low_back(product(hidden_one, w_query)).reshape(SEQ, HEADS, NOPE + ROPE)
    query_rot = jnp.concatenate([query_pre[..., :NOPE], rotate(query_pre[..., NOPE:], cosine[:, None, :], sine[:, None, :])], axis=-1)
    query_all = low(low_back(query_rot))
    compressed = low_back(product(hidden_one, w_kv_down))
    latent = low(rms_norm(compressed[:, :RANK], kv_gain))
    key_rope = rotate(compressed[:, RANK:], cosine, sine)
    expanded = product(latent, w_kv_up).reshape(SEQ, HEADS, NOPE + VDIM)
    key_join = jnp.concatenate([expanded[..., :NOPE], jnp.broadcast_to(key_rope[:, None, :], (SEQ, HEADS, ROPE))], axis=-1)
    keys_all = low(low_back(key_join))
    values_all = low(low_back(expanded[..., NOPE:]))
    block_rows = min(512, SEQ)
    score_scale = (NOPE + ROPE) ** (-0.5)
    column_ids = jnp.arange(SEQ).astype(jnp.int32)

    def attend(begin_at):
        query_block = lax.dynamic_slice_in_dim(query_all, begin_at, block_rows, 0)
        raw_scores = low_back(jnp.einsum('qhc,khc->hqk', query_block, keys_all, precision=highest))
        row_ids = begin_at + jnp.arange(block_rows).astype(jnp.int32)
        allowed = column_ids[None, :] <= row_ids[:, None]
        scores = jnp.where(allowed[None], raw_scores * score_scale, -1000000000.0)
        prob_rows = low(jax.nn.softmax(scores, axis=-1))
        return jnp.einsum('hqk,khc->qhc', prob_rows, values_all, precision=highest)
    block_starts = (jnp.arange(SEQ // block_rows) * block_rows).astype(jnp.int32)
    head_out = lax.map(jax.checkpoint(attend), block_starts).reshape(SEQ, HEADS * VDIM)
    head_out = low(low_back(head_out))
    resid_two = resid_one + low_back(product(head_out, w_out))
    hidden_two = low(rms_norm(resid_two, ffn_gain))
    router = jax.nn.softmax(low_back(product(hidden_two, w_router)), axis=-1)
    expert_ids = jnp.arange(EXPERTS).astype(jnp.int32)
    picked = lax.optimization_barrier(jnp.sum((chosen_rows[:, :, None] == expert_ids[None, None, :]).astype(jnp.float32), axis=1))
    gate_dense = router * picked
    gate_shared = low_back(jnp.einsum('td,dsf->tsf', hidden_two, shared_gate, precision=highest))
    up_shared = low_back(jnp.einsum('td,dsf->tsf', hidden_two, shared_up, precision=highest))
    act_shared = low(swiglu(gate_shared, up_shared))
    shared_out = jnp.einsum('tsf,fsd->td', act_shared, shared_down, precision=highest)
    gate_routed = low_back(jnp.einsum('td,def->tef', hidden_two, expert_gate, precision=highest))
    up_routed = low_back(jnp.einsum('td,def->tef', hidden_two, expert_up, precision=highest))
    act_routed = low(swiglu(gate_routed, up_routed))
    routed_out = low_back(jnp.einsum('tef,fed->ted', act_routed, expert_down, precision=highest))
    return resid_two + shared_out + jnp.einsum('te,ted->td', gate_dense, routed_out, precision=highest)

def reference(tokens, cotangent, chosen, attn_gain, w_query, w_kv_down, kv_gain, w_kv_up, w_out, ffn_gain, w_router, shared_gate, shared_up, shared_down, expert_gate, expert_up, expert_down):
    params = tuple((weight.astype(jnp.float32) for weight in (attn_gain, w_query, w_kv_down, kv_gain, w_kv_up, w_out, ffn_gain, w_router, shared_gate, shared_up, shared_down, expert_gate, expert_up, expert_down)))
    seq_count = TOKENS // SEQ
    inputs_all = (tokens.astype(jnp.float32).reshape(seq_count, SEQ, D), cotangent.astype(jnp.float32).reshape(seq_count, SEQ, D), chosen.reshape(seq_count, SEQ, TOP))

    def per_sequence(totals, inputs):
        resid, upstream, chosen_rows = inputs
        result, pullback = jax.vjp(lambda weights, values: forward(weights, values, chosen_rows), params, resid)
        weight_grads, resid_grad = pullback(upstream)
        totals = jax.tree.map(jnp.add, totals, weight_grads)
        return (totals, (result.astype(jnp.bfloat16), resid_grad.astype(jnp.bfloat16)))
    zeros_all = jax.tree.map(jnp.zeros_like, params)
    grads, (mixed, tokens_grad) = lax.scan(per_sequence, zeros_all, inputs_all)
    return (mixed.reshape(TOKENS, D), tokens_grad.reshape(TOKENS, D), grads[0], grads[1], grads[2], grads[3], grads[4], grads[5], grads[6], grads[7], grads[8], grads[9], grads[10], grads[11], grads[12], grads[13])
```

```python
import functools

import jax
import jax.numpy as jnp
from jax import lax
from jax.experimental import pallas as pl
from jax.experimental.pallas import tpu as pltpu
from jax.sharding import PartitionSpec as P

D = 2048
HEADS = 16
NOPE = 128
ROPE = 64
QK = NOPE + ROPE
VDIM = 128
RANK = 512
FE = 1408
NS = 2
EXPERTS = 4
TOP = 2
SETS = NS + EXPERTS
DP = 16
SP = 8
ROWS = 128
SEQ = SP * ROWS
GROUP = DP * ROWS
HEADS_HERE = HEADS // SP
QW = HEADS_HERE * QK
KVW = HEADS_HERE * (NOPE + VDIM)
OW = HEADS_HERE * VDIM
SLICE = FE // DP
WIDE = SETS * SLICE
SCALE = QK ** (-0.5)
PACK = QW + RANK + ROPE + ROPE + OW + ROWS
GU_PART = 144
DN_PART = 80

epsilon = 1e-06
bf16 = jnp.bfloat16
f32 = jnp.float32


def mm(left, right, dims):
    return lax.dot_general(left, right, ((dims[0], dims[1]), ((), ())), preferred_element_type=f32)


def nn(left, right):
    return mm(left, right, ((1,), (0,)))


def nt(left, right):
    return mm(left, right, ((1,), (1,)))


def tn(left, right):
    return mm(left, right, ((0,), (0,)))


def rope_tables(positions):
    half_dim = ROPE // 2
    inverse = 10000.0 ** (-jnp.arange(half_dim, dtype=f32) * 2.0 / ROPE)
    angles = positions[:, None] * inverse[None, :]
    return (jnp.cos(angles), jnp.sin(angles))


def rotate(values, cosine, sine):
    first, second = values[..., : ROPE // 2], values[..., ROPE // 2 :]
    return jnp.concatenate([first * cosine - second * sine, second * cosine + first * sine], axis=-1)


def norm_back(values, scale, gain, grad):
    scaled = gain * grad
    total = jnp.sum(scaled * values, axis=-1, keepdims=True) / values.shape[-1]
    return scale * scaled - values * (scale * scale * scale) * total


def inverse_rms(values):
    return lax.rsqrt(jnp.mean(values * values, axis=-1, keepdims=True) + epsilon)


class Seat:
    def __init__(self, axis):
        own_dp, own_sp = lax.axis_index("dp"), lax.axis_index("sp")
        self.axis = axis
        if axis == "sp":
            self.pair, self.ring, self.core, self.cores = own_sp // 4, own_sp % 4, 0, 1
            self.own, self.size = own_sp, SP
            self.device = lambda index: (own_dp, index)
        else:
            self.ring, self.pair, self.core, self.cores = own_dp // 4, (own_dp // 2) % 2, own_dp % 2, 2
            self.own, self.size = own_dp, DP
            self.device = lambda index: (index, own_sp)

    def index(self, pair, ring, core=0):
        pair, ring = (self.pair + pair) % 2, (self.ring + ring) % 4
        if self.axis == "sp":
            return pair * 4 + ring
        return (ring * 2 + pair) * 2 + (self.core + core) % 2


def send(src, dst, send_sem, recv_sem, device):
    copy = pltpu.make_async_remote_copy(
        src_ref=src,
        dst_ref=dst,
        send_sem=send_sem,
        recv_sem=recv_sem,
        device_id=device,
        device_id_type=pl.DeviceIdType.MESH,
    )
    copy.start()
    return copy


def block_of(ref, start, size):
    return ref.at[pl.ds(pl.multiple_of(start, 16), size)]


def middle(rows):
    return (rows // 2 + 15) // 16 * 16


NEAR = ((0, 1), (0, -1), (1, 0))
ORDER = ((1, 2), (1, 1), (1, -1), (0, 2), (1, 0), (0, 1), (0, -1), (0, 0))


class Gather:
    def __init__(self, axis, rows, width):
        self.axis, self.rows, self.width = axis, rows, width
        self.count = SP if axis == "sp" else DP

    def in_spec(self):
        return pl.BlockSpec(memory_space=pl.ANY)

    def out(self):
        return (
            jax.ShapeDtypeStruct((self.count * self.rows, self.width), bf16),
            pl.BlockSpec(memory_space=pl.ANY),
        )

    def scratch(self):
        return [pltpu.SemaphoreType.DMA((16,)), pltpu.SemaphoreType.DMA((16,)), pltpu.SemaphoreType.DMA]

    def partners(self, seat):
        near = [seat.index(*n) for n in NEAR]
        return near + ([seat.index(0, 0, 1)] if seat.cores == 2 else [])

    def bind(self, src, out, scratch):
        self.src, self.dst = src, out
        self.send_sem, self.recv_sem, self.local_sem = scratch
        self.seat = Seat(self.axis)
        self.copies = {}

    def view(self, place, half=None):
        start = self.seat.index(*place) * self.rows
        if half is None:
            return block_of(self.dst, start, self.rows)
        cut = middle(self.rows)
        return block_of(self.dst, start + half * cut, (cut, self.rows - cut)[half])

    def go(self, number, src, dst, to):
        self.copies[number] = send(
            src,
            dst,
            self.send_sem.at[number],
            self.recv_sem.at[number],
            self.seat.device(self.seat.index(*to)),
        )

    def share(self, number, place, src=None):
        if self.seat.cores == 2:
            self.go(8 + number, self.view(place) if src is None else src, self.view(place), (0, 0, 1))

    def arrived(self, *numbers):
        for number in numbers:
            self.copies[number].wait_recv()

    def step(self, number):
        if number == 0:
            here = self.view((0, 0))
            self.local = pltpu.make_async_copy(self.src, here, self.local_sem)
            self.local.start()
            for k, to in enumerate(NEAR):
                self.go(k, self.src, here, to)
            self.share(0, (0, 0), self.src)
        elif number == 1:
            self.arrived(0, 1)
            self.go(3, self.view((0, -1), 0), self.view((0, -1), 0), (0, 1))
            self.go(4, self.view((0, 1), 1), self.view((0, 1), 1), (0, -1))
            self.share(1, (0, -1))
            self.share(2, (0, 1))
        elif number == 2:
            self.arrived(2)
            self.go(5, self.view((1, 0)), self.view((1, 0)), (0, 1))
            self.go(6, self.view((1, 0)), self.view((1, 0)), (0, -1))
            self.share(3, (1, 0))
        elif number == 3:
            self.arrived(3, 4)
            self.go(7, self.view((0, 2)), self.view((0, 2)), (1, 0))
            self.share(4, (0, 2))
        elif number == 4:
            self.arrived(5, 6, 7)
            self.share(5, (1, -1))
            self.share(6, (1, 1))
            self.share(7, (1, 2))
        else:
            if self.seat.cores == 2:
                self.arrived(*range(8, 16))
            for copy in self.copies.values():
                copy.wait_send()
            self.local.wait()


class Scatter:
    def __init__(self, axis, rows, width, kind=f32):
        self.axis, self.rows, self.width, self.kind = axis, rows, width, kind
        self.count = SP if axis == "sp" else DP

    def in_spec(self):
        return pl.BlockSpec(memory_space=pltpu.VMEM)

    def out(self):
        return (
            jax.ShapeDtypeStruct((self.rows, self.width), self.kind),
            pl.BlockSpec(memory_space=pltpu.VMEM),
        )

    def scratch(self):
        block, cut = (self.rows, self.width), middle(self.rows)
        first, second = (cut, self.width), (self.rows - cut, self.width)
        shapes = [block, block, block, first, second, block, block, block]
        shapes = shapes + [block] * 4
        if self.axis == "dp":
            shapes = shapes + [(8,) + block]
        return [pltpu.SemaphoreType.DMA((16,)), pltpu.SemaphoreType.DMA((16,))] + [
            pltpu.VMEM(shape, bf16) for shape in shapes
        ]

    partners = Gather.partners
    go = Gather.go
    arrived = Gather.arrived

    def bind(self, src, out, scratch):
        self.src, self.dst = src, out
        self.send_sem, self.recv_sem = scratch[:2]
        self.got, self.made = scratch[2:10], scratch[10:14]
        self.shared = scratch[14] if self.axis == "dp" else None
        self.seat = Seat(self.axis)
        self.copies = {}

    def part(self, place):
        if self.shared is None:
            return block_of(self.src, self.seat.index(*place) * self.rows, self.rows)
        return self.shared.at[ORDER.index(place)]

    def ready(self, place):
        if self.shared is not None:
            k = ORDER.index(place)
            self.arrived(8 + k)
            self.add(
                self.shared.at[k],
                [self.shared.at[k], block_of(self.src, self.seat.index(*place) * self.rows, self.rows)],
            )

    def add(self, dst, terms):
        rows = dst.shape[0]
        step = 16

        @pl.loop(0, rows // step)
        def _(i):
            at = pl.ds(pl.multiple_of(i * step, step), step)
            total = terms[0][at, :].astype(f32)
            for term in terms[1:]:
                total = total + term[at, :].astype(f32)
            dst[at, :] = total.astype(dst.dtype)

    def halves(self, ref):
        cut = middle(self.rows)
        return ref.at[pl.ds(0, cut)], ref.at[pl.ds(cut, self.rows - cut)]

    def step(self, number):
        if number == 0:
            if self.shared is not None:
                for k, place in enumerate(ORDER):
                    src = block_of(self.src, self.seat.index(*place, 1) * self.rows, self.rows)
                    self.go(8 + k, src, self.shared.at[k], (0, 0, 1))
            self.ready((1, 2))
            self.go(0, self.part((1, 2)), self.got[0], (1, 0))
            self.ready((1, 1))
            self.go(1, self.part((1, 1)), self.got[1], (0, 1))
            self.ready((1, -1))
            self.go(2, self.part((1, -1)), self.got[2], (0, -1))
            for place in ORDER[3:]:
                self.ready(place)
        elif number == 1:
            self.arrived(0)
            self.add(self.made[0], [self.part((0, 2)), self.got[0]])
            first, second = self.halves(self.made[0])
            self.go(3, first, self.got[3], (0, 1))
            self.go(4, second, self.got[4], (0, -1))
        elif number == 2:
            self.arrived(1, 2)
            self.add(self.made[1], [self.part((1, 0)), self.got[1], self.got[2]])
            self.go(5, self.made[1], self.got[5], (1, 0))
        elif number == 3:
            self.arrived(3, 4)
            for k, place, half in ((2, (0, 1), 0), (3, (0, -1), 1)):
                made, part = self.halves(self.made[k]), self.halves(self.part(place))
                self.add(made[half], [part[half], self.got[3 + half]])
                self.add(made[1 - half], [part[1 - half]])
                self.go(6 + half, self.made[k], self.got[6 + half], (0, 1 - 2 * half))
        elif number == 4:
            self.arrived(5, 6, 7)
            self.add(self.dst, [self.part((0, 0)), self.got[5], self.got[6], self.got[7]])
        else:
            for copy in self.copies.values():
                copy.wait_send()


class Swap:
    def __init__(self, axis, shape, take, put, kind="any"):
        self.axis, self.shape, self.take, self.put = axis, shape, take, put
        self.count = SP if axis == "sp" else DP

    def in_spec(self):
        return pl.BlockSpec(memory_space=pl.ANY)

    def out(self):
        return jax.ShapeDtypeStruct(self.shape, bf16), pl.BlockSpec(memory_space=pl.ANY)

    def scratch(self):
        sems = pltpu.SemaphoreType.DMA((self.count,))
        return [sems, sems, pltpu.SemaphoreType.DMA]

    def partners(self, seat):
        return [(seat.own + k) % seat.size for k in range(1, seat.size)]

    def bind(self, src, out, scratch):
        self.src, self.dst = src, out
        self.send_sem, self.recv_sem, self.local_sem = scratch
        self.seat = Seat(self.axis)

    def step(self, number):
        seat = self.seat
        if number == 0:
            here = self.put(self.dst, seat.own)
            self.local = pltpu.make_async_copy(self.take(self.src, seat.own), here, self.local_sem)
            self.local.start()
            self.copies = []
            for k in range(1, seat.size):
                to = (seat.own + k) % seat.size
                self.copies.append(
                    send(
                        self.take(self.src, to),
                        here,
                        self.send_sem.at[k],
                        self.recv_sem.at[k],
                        seat.device(to),
                    )
                )
        elif number == 5:
            for copy in self.copies:
                copy.wait_recv()
            for copy in self.copies:
                copy.wait_send()
            self.local.wait()


def exchange(name, number, ops, arrays, plan=None, chained=()):
    chained = dict(chained)
    plan = plan or [(op, step) for step in range(6) for op in range(len(ops))]
    counts = [len(op.scratch()) for op in ops]
    inputs = [k for k in range(len(ops)) if k not in chained]

    def body(*refs):
        given = dict(zip(inputs, refs[: len(inputs)]))
        outs = refs[len(inputs) : len(inputs) + len(ops)]
        rest = refs[len(inputs) + len(ops) :]
        for k, op in enumerate(ops):
            op.bind(given[k] if k in given else outs[chained[k]], outs[k], rest[: counts[k]])
            rest = rest[counts[k] :]
        barrier = pltpu.get_barrier_semaphore()
        total = 0
        for axis in ("sp", "dp"):
            mine = [op for op in ops if op.axis == axis]
            if not mine:
                continue
            seat = Seat(axis)
            widest = max(mine, key=lambda op: len(op.partners(seat)))
            for partner in widest.partners(seat):
                pl.semaphore_signal(
                    barrier,
                    inc=1,
                    device_id=seat.device(partner),
                    device_id_type=pl.DeviceIdType.MESH,
                )
                total += 1
        pl.semaphore_wait(barrier, total)
        for op, step in plan:
            ops[op].step(step)

    outs = [op.out() for op in ops]
    return pl.pallas_call(
        body,
        name=name,
        out_shape=[shape for shape, _ in outs],
        in_specs=[ops[k].in_spec() for k in inputs],
        out_specs=[spec for _, spec in outs],
        scratch_shapes=[entry for op in ops for entry in op.scratch()],
        compiler_params=pltpu.CompilerParams(
            collective_id=number, has_side_effects=True, vmem_limit_bytes=56 * 2**20
        ),
    )(*arrays)


def per_device(
    tokens,
    cotangent,
    chosen,
    attn_gain,
    w_query,
    w_kv_down,
    kv_gain,
    w_kv_up,
    w_out,
    ffn_gain,
    w_router,
    shared_gate,
    shared_up,
    shared_down,
    expert_gate,
    expert_up,
    expert_down,
):
    own_sp = lax.axis_index("sp")
    picks = jnp.any(chosen[:, :, None] == jnp.arange(EXPERTS, dtype=jnp.int32), axis=1).astype(bf16)
    pack = jnp.concatenate(
        [
            lax.dynamic_slice_in_dim(w_query, own_sp * QW, QW, 1),
            w_kv_down,
            attn_gain[:, None],
            ffn_gain[:, None],
            jnp.pad(kv_gain, (0, ROWS - kv_gain.shape[0]))[:, None],
            w_router,
            picks,
            jnp.zeros((ROWS, ROPE - 11), bf16),
            lax.dynamic_slice_in_dim(w_out, own_sp * OW, OW, 1),
            lax.dynamic_slice_in_dim(w_kv_up, own_sp * KVW, KVW, 1).reshape(ROWS, ROWS),
        ],
        axis=1,
    )
    at = QW + RANK + ROPE
    out_at = at + ROPE
    tok_all, pack, cot_all, out_w = exchange(
        "gather_tokens_weights",
        0,
        [
            Gather("sp", ROWS, D),
            Gather("dp", ROWS, PACK),
            Gather("dp", ROWS, D),
            Swap(
                "sp",
                (OW, D),
                lambda ref, j: ref.at[pl.ds(pl.multiple_of(j * OW, OW), OW), pl.ds(out_at, OW)],
                lambda ref, j: ref.at[:, pl.ds(pl.multiple_of(j * OW, OW), OW)],
            ),
        ],
        [tokens, pack, cotangent],
        plan=[(0, 0), (1, 0), (0, 1), (1, 1), (0, 2), (1, 2), (0, 3), (1, 3), (1, 4), (1, 5)]
        + [(2, 0), (3, 0), (0, 4), (2, 1), (0, 5), (2, 2), (2, 3), (3, 5), (2, 4), (2, 5)],
        chained=[(3, 1)],
    )
    qc_w = pack[:, :at]
    up_w = pack[:, out_at + OW :].reshape(RANK, KVW)
    gain_one = pack[:, at].astype(f32)
    gain_two = pack[:, at + 1].astype(f32)
    latent_gain = pack[:, at + 2].reshape(DP, ROWS)[:, : RANK // DP].reshape(RANK).astype(f32)
    router_w = pack[:, at + 3 : at + 7]
    picks_all = pack[:, at + 7 : at + 11].astype(f32)
    gate_up = jnp.stack(
        [
            jnp.concatenate([shared_gate, expert_gate], axis=1),
            jnp.concatenate([shared_up, expert_up], axis=1),
        ]
    )
    gate_up = gate_up.reshape(2, ROWS, SETS, DP, SLICE).transpose(3, 0, 2, 4, 1)
    gate_up = gate_up.reshape(DP, 2 * WIDE, ROWS)
    down = jnp.concatenate([shared_down, expert_down], axis=1).transpose(1, 0, 2).reshape(WIDE, D)

    cosine, sine = rope_tables(jnp.arange(SEQ, dtype=f32))
    resid_all = tok_all.astype(f32)
    scale_one = inverse_rms(resid_all)
    hidden_one = (resid_all * scale_one * gain_one).astype(bf16)
    qc = nn(hidden_one, qc_w)
    compressed = qc[:, QW : QW + RANK]
    scale_latent = inverse_rms(compressed)
    latent = (compressed * scale_latent * latent_gain).astype(bf16)
    key_rope = rotate(qc[:, QW + RANK :], cosine, sine).astype(bf16)
    expanded = nn(latent, up_w).astype(bf16)
    rows = jnp.arange(SEQ, dtype=jnp.int32)
    allowed = rows[None, :] <= rows[:, None]
    queries, keys, values, probs, heads = [], [], [], [], []
    for h in range(HEADS_HERE):
        raw = qc[:, h * QK : (h + 1) * QK]
        query = jnp.concatenate([raw[:, :NOPE], rotate(raw[:, NOPE:], cosine, sine)], axis=1).astype(bf16)
        base = h * (NOPE + VDIM)
        key = jnp.concatenate([expanded[:, base : base + NOPE], key_rope], axis=1)
        value = expanded[:, base + NOPE : base + NOPE + VDIM]
        scores = jnp.where(allowed, nt(query, key) * SCALE, -1e9)
        weights = jnp.exp(scores - jnp.max(scores, axis=-1, keepdims=True))
        prob = weights / jnp.sum(weights, axis=-1, keepdims=True)
        queries.append(query)
        keys.append(key)
        values.append(value)
        probs.append(prob)
        heads.append(nn(prob.astype(bf16), value).astype(bf16))
    head_out = jnp.concatenate(heads, axis=1)
    attn_proj, gate_up = exchange(
        "sum_projection",
        1,
        [
            Scatter("sp", ROWS, D),
            Swap(
                "dp",
                (2 * WIDE, D),
                lambda ref, j: ref.at[j],
                lambda ref, j: ref.at[:, pl.ds(pl.multiple_of(j * ROWS, ROWS), ROWS)],
            ),
        ],
        [nn(head_out, out_w).astype(bf16), gate_up],
    )
    resid_two = tokens.astype(f32) + attn_proj
    scale_two = inverse_rms(resid_two)
    hidden_two = (resid_two * scale_two * gain_two).astype(bf16)

    (hidden_all,) = exchange("gather_hidden", 2, [Gather("dp", ROWS, D)], [hidden_two])
    router_all = jax.nn.softmax(nn(hidden_all, router_w), axis=-1)
    gate_dense = router_all * picks_all
    column_set = jnp.arange(WIDE, dtype=jnp.int32) // SLICE

    def spread(per_expert, shared):
        out = jnp.full((GROUP, WIDE), shared, f32)
        for e in range(EXPERTS):
            out = jnp.where(column_set[None, :] == NS + e, per_expert[:, e : e + 1], out)
        return out

    gates = spread(gate_dense, 1.0)
    gate = nt(hidden_all, gate_up[:WIDE])
    up = nt(hidden_all, gate_up[WIDE:])
    sig = jax.nn.sigmoid(gate)
    silu = gate * sig
    act = silu * up
    act_gated = (act.astype(bf16).astype(f32) * gates).astype(bf16)
    mixed_part = nn(act_gated, down).astype(bf16)
    act_grad_raw = nt(cot_all, down)
    reached = act * act_grad_raw
    prob_grad = jnp.stack(
        [
            jnp.sum(jnp.where(column_set[None, :] == NS + e, reached, 0.0), axis=1)
            for e in range(EXPERTS)
        ],
        axis=1,
    )
    act_grad = act_grad_raw * gates
    gate_grad = (act_grad * up * sig * (1.0 + gate * (1.0 - sig))).astype(bf16)
    up_grad = (act_grad * silu).astype(bf16)
    hidden_grad_part = (nn(gate_grad, gate_up[:WIDE]) + nn(up_grad, gate_up[WIDE:])).astype(bf16)
    hidden_grad_part = jnp.concatenate(
        [hidden_grad_part, prob_grad.astype(bf16), jnp.zeros((GROUP, ROWS - EXPERTS), bf16)], axis=1
    )
    (hidden_grad,) = exchange(
        "sum_hidden_grad", 3, [Scatter("dp", ROWS, D + ROWS)], [hidden_grad_part]
    )
    prob_grad = hidden_grad[:, D : D + EXPERTS]
    hidden_grad = hidden_grad[:, :D]

    def parts(grad, size):
        return jnp.pad(grad, ((0, SP * size - grad.shape[0]), (0, 0))).reshape(SP, size, D)

    gate_up_grad = jnp.concatenate([tn(gate_grad, hidden_all), tn(up_grad, hidden_all)]).astype(bf16)
    down_grad = tn(act_gated, cot_all).astype(bf16)
    ffn_grad = jnp.concatenate([parts(gate_up_grad, GU_PART), parts(down_grad, DN_PART)], axis=1)
    ffn_grad = ffn_grad.reshape(SP * (GU_PART + DN_PART), D)

    logits = nn(hidden_two, router_w)
    router = jax.nn.softmax(logits, axis=-1)
    prob_grad = prob_grad * picks.astype(f32)
    logit_grad = (
        router * (prob_grad - jnp.sum(router * prob_grad, axis=-1, keepdims=True))
    ).astype(bf16)
    hidden_grad = hidden_grad + nt(logit_grad, router_w)
    router_grad = tn(hidden_two, logit_grad)
    gain_two_grad = jnp.sum(hidden_grad * resid_two * scale_two, axis=0)
    upstream = cotangent.astype(f32)
    resid_two_grad = upstream + norm_back(resid_two, scale_two, gain_two, hidden_grad)
    proj_grad = resid_two_grad.astype(bf16)

    proj_grad_all, mixed = exchange(
        "gather_projection_grad",
        4,
        [Gather("sp", ROWS, D), Scatter("dp", ROWS, D)],
        [proj_grad, mixed_part],
    )
    mixed = (resid_two + mixed).astype(bf16)
    out_w_grad = tn(head_out, proj_grad_all)
    head_grad = nt(proj_grad_all, out_w).astype(bf16)
    query_grads, expanded_grads, rope_grad = [], [], 0.0
    for h in range(HEADS_HERE):
        piece = head_grad[:, h * VDIM : (h + 1) * VDIM]
        prob = probs[h]
        dprob = nt(piece, values[h])
        delta = jnp.sum(prob * dprob, axis=-1, keepdims=True)
        score_grad = (prob * (dprob - delta) * SCALE).astype(bf16)
        query_grad = nn(score_grad, keys[h]).astype(bf16).astype(f32)
        key_grad = tn(score_grad, queries[h]).astype(bf16)
        value_grad = tn(prob.astype(bf16), piece).astype(bf16)
        query_grads.append(query_grad[:, :NOPE].astype(bf16))
        query_grads.append(rotate(query_grad[:, NOPE:], cosine, -sine).astype(bf16))
        expanded_grads.append(key_grad[:, :NOPE])
        expanded_grads.append(value_grad)
        rope_grad = rope_grad + key_grad[:, NOPE:].astype(f32)
    query_pre_grad = jnp.concatenate(query_grads, axis=1)
    expanded_grad = jnp.concatenate(expanded_grads, axis=1)
    up_w_grad = tn(latent, expanded_grad)
    latent_grad = nt(expanded_grad, up_w)
    latent_in_grad = norm_back(compressed, scale_latent, latent_gain, latent_grad)
    latent_gain_grad = jnp.sum(latent_grad * compressed * scale_latent, axis=0)
    compressed_grad = jnp.concatenate(
        [latent_in_grad, rotate(rope_grad, cosine, -sine)], axis=1
    ).astype(bf16)
    qc_grad = jnp.concatenate([query_pre_grad, compressed_grad], axis=1)
    qc_w_grad = tn(hidden_one, qc_grad)
    hidden_one_grad = nt(qc_grad, qc_w)
    gain_one_grad = jnp.sum(hidden_one_grad * resid_all * scale_one, axis=0)
    (out_cols_grad,) = exchange(
        "swap_projection_weight_grad",
        5,
        [
            Swap(
                "sp",
                (D, OW),
                lambda ref, j: ref.at[:, pl.ds(pl.multiple_of(j * OW, OW), OW)],
                lambda ref, j: ref.at[pl.ds(pl.multiple_of(j * OW, OW), OW)],
            )
        ],
        [out_w_grad.astype(bf16)],
    )
    latent_gain_grad = jnp.pad(
        latent_gain_grad.reshape(DP, RANK // DP), ((0, 0), (0, ROWS - RANK // DP))
    ).reshape(D)
    grads = jnp.concatenate(
        [
            qc_w_grad.astype(bf16),
            gain_one_grad.astype(bf16)[:, None],
            gain_two_grad.astype(bf16)[:, None],
            latent_gain_grad.astype(bf16)[:, None],
            router_grad.astype(bf16),
            jnp.zeros((D, ROPE - 7), bf16),
            out_cols_grad,
            up_w_grad.astype(bf16).reshape(D, ROWS),
        ],
        axis=1,
    )
    grads, ffn_grad, hidden_one_grad = exchange(
        "sum_grads",
        6,
        [
            Scatter("dp", ROWS, PACK, bf16),
            Scatter("sp", GU_PART + DN_PART, D, bf16),
            Scatter("sp", ROWS, D),
        ],
        [grads, ffn_grad, hidden_one_grad.astype(bf16)],
    )
    grads, dn_total, gu_piece = exchange(
        "gather_grads",
        7,
        [
            Gather("sp", ROWS, PACK),
            Gather("sp", DN_PART, D),
            Swap(
                "dp",
                (DP, GU_PART, ROWS),
                lambda ref, j: ref.at[:, pl.ds(pl.multiple_of(j * ROWS, ROWS), ROWS)],
                lambda ref, j: ref.at[j],
            ),
        ],
        [grads, ffn_grad[GU_PART:], ffn_grad[:GU_PART]],
    )
    (gu_total,) = exchange(
        "gather_expert_grads",
        8,
        [Gather("sp", DP * GU_PART, ROWS)],
        [gu_piece.reshape(DP * GU_PART, ROWS)],
    )
    gu_total = gu_total.reshape(SP, DP, GU_PART, ROWS)
    grads = grads.reshape(SP, ROWS, PACK)
    resid_one = tokens.astype(f32)
    own_scale = inverse_rms(resid_one)
    tokens_grad = resid_two_grad + norm_back(resid_one, own_scale, gain_one, hidden_one_grad)
    tokens_grad = tokens_grad.astype(bf16)

    def side_by_side(block, width):
        return block.astype(f32).transpose(1, 0, 2).reshape(-1, SP * width)

    query_total = side_by_side(grads[:, :, :QW], QW)
    tail = jnp.sum(grads[:, :, QW:out_at].astype(f32), axis=0)
    down_total, tail = tail[:, : RANK + ROPE], tail[:, RANK + ROPE :]
    out_total = side_by_side(grads[:, :, out_at : out_at + OW], OW)
    up_total = side_by_side(grads[:, :, out_at + OW :].reshape(SP, RANK // DP, KVW), KVW)

    gu_total = gu_total.transpose(0, 2, 1, 3).reshape(SP * GU_PART, DP, ROWS)[: 2 * WIDE]
    gu_total = gu_total.reshape(2, SETS, SLICE, DP, ROWS).transpose(0, 4, 1, 3, 2)
    gu_total = gu_total.reshape(2, ROWS, SETS, FE).astype(f32)
    dn_total = dn_total[:WIDE].reshape(SETS, SLICE, D).transpose(1, 0, 2).astype(f32)
    return (
        mixed,
        tokens_grad,
        tail[:, 0],
        query_total,
        down_total,
        tail[: RANK // DP, 2],
        up_total,
        out_total,
        tail[:, 1],
        tail[:, 3:7],
        gu_total[0, :, :NS],
        gu_total[1, :, :NS],
        dn_total[:, :NS],
        gu_total[0, :, NS:],
        gu_total[1, :, NS:],
        dn_total[:, NS:],
    )


def solution(mesh):
    rows = P(("dp", "sp"), None)
    vec, mat, cube = P("dp"), P("dp", None), P("dp", None, None)
    return jax.shard_map(
        per_device,
        mesh=mesh,
        in_specs=(rows, rows, rows, vec, mat, mat, vec, mat, mat, vec, mat) + (cube,) * 6,
        out_specs=(rows, rows, vec, mat, mat, vec, mat, mat, vec, mat) + (cube,) * 6,
        check_vma=False,
    )
```

```python
import functools

import jax
import jax.numpy as jnp
from jax import lax
from jax.experimental import pallas as pl
from jax.experimental.pallas import tpu as pltpu
from jax.sharding import PartitionSpec as P

D = 2048
HEADS = 16
NOPE = 128
ROPE = 64
QK = NOPE + ROPE
VDIM = 128
RANK = 512
FE = 1408
NS = 2
EXPERTS = 4
TOP = 2
SETS = NS + EXPERTS
DP = 16
SP = 8
ROWS = 128
SEQ = SP * ROWS
GROUP = DP * ROWS
HEADS_HERE = HEADS // SP
QW = HEADS_HERE * QK
KVW = HEADS_HERE * (NOPE + VDIM)
OW = HEADS_HERE * VDIM
SLICE = FE // DP
CORE_W = 1024
UP_AT = CORE_W + OW
MISC_AT = CORE_W - ROWS
PICK_LANE, GAIN_ONE, GAIN_TWO, GAIN_KV, ROUTER_LANE = 64, 68, 69, 70, 80
ROOM = 96
HALF = SETS * ROOM
FULL = 640
CHUNK = 2 * ROWS
TILE = 512
SCALE = QK ** (-0.5)
PACK = QW + RANK + ROPE + ROPE + OW + ROWS
GU_PART = 2 * HALF // SP
DN_PART = FULL // SP

epsilon = 1e-06
bf16 = jnp.bfloat16
f32 = jnp.float32


def mm(left, right, dims):
    return lax.dot_general(left, right, ((dims[0], dims[1]), ((), ())), preferred_element_type=f32)


def nn(left, right):
    return mm(left, right, ((1,), (0,)))


def nt(left, right):
    return mm(left, right, ((1,), (1,)))


def tn(left, right):
    return mm(left, right, ((0,), (0,)))


def rope_tables(positions):
    half_dim = ROPE // 2
    inverse = 10000.0 ** (-jnp.arange(half_dim, dtype=f32) * 2.0 / ROPE)
    angles = positions[:, None] * inverse[None, :]
    return (jnp.cos(angles), jnp.sin(angles))


def rotate(values, cosine, sine):
    first, second = values[..., : ROPE // 2], values[..., ROPE // 2 :]
    return jnp.concatenate([first * cosine - second * sine, second * cosine + first * sine], axis=-1)


def norm_back(values, scale, gain, grad):
    scaled = gain * grad
    total = jnp.sum(scaled * values, axis=-1, keepdims=True) / values.shape[-1]
    return scale * scaled - values * (scale * scale * scale) * total


def inverse_rms(values):
    return lax.rsqrt(jnp.mean(values * values, axis=-1, keepdims=True) + epsilon)


class Seat:
    def __init__(self, axis):
        own_dp, own_sp = lax.axis_index("dp"), lax.axis_index("sp")
        self.axis = axis
        if axis == "sp":
            self.pair, self.ring, self.core, self.cores = own_sp // 4, own_sp % 4, 0, 1
            self.own, self.size = own_sp, SP
            self.device = lambda index: (own_dp, index)
        else:
            self.ring, self.pair, self.core, self.cores = own_dp // 4, (own_dp // 2) % 2, own_dp % 2, 2
            self.own, self.size = own_dp, DP
            self.device = lambda index: (index, own_sp)

    def index(self, pair, ring, core=0):
        pair, ring = (self.pair + pair) % 2, (self.ring + ring) % 4
        if self.axis == "sp":
            return pair * 4 + ring
        return (ring * 2 + pair) * 2 + (self.core + core) % 2


def remote(src, dst, send_sem, recv_sem, device):
    return pltpu.make_async_remote_copy(
        src_ref=src,
        dst_ref=dst,
        send_sem=send_sem,
        recv_sem=recv_sem,
        device_id=device,
        device_id_type=pl.DeviceIdType.MESH,
    )


def block_of(ref, start, size):
    return ref.at[pl.ds(pl.multiple_of(start, 16), size)]


def middle(rows):
    return (rows // 2 + 15) // 16 * 16


NEAR = ((0, 1), (0, -1), (1, 0))
SHARE = ((0, 0), (0, -1), (0, 1), (1, 0), (0, 2), (1, -1), (1, 1), (1, 2))
ORDER = ((1, 2), (1, 1), (1, -1), (0, 2), (1, 0), (0, 1), (0, -1), (0, 0))


class Gather:
    def __init__(self, axis, rows, width, spare=False):
        self.axis, self.rows, self.width, self.spare = axis, rows, width, spare
        self.count = SP if axis == "sp" else DP

    def in_spec(self):
        return pl.BlockSpec(memory_space=pl.ANY)

    def out(self):
        return (
            jax.ShapeDtypeStruct((self.count * self.rows, self.width), bf16),
            pl.BlockSpec(memory_space=pl.ANY),
        )

    def scratch(self):
        return [pltpu.SemaphoreType.DMA((17,)), pltpu.SemaphoreType.DMA((17,)), pltpu.SemaphoreType.DMA]

    def partners(self, seat):
        near = [seat.index(*n) for n in NEAR]
        return near + ([seat.index(0, 0, 1)] if seat.cores == 2 else [])

    def bind(self, src, out, scratch):
        self.src, self.dst = src, out
        self.send_sem, self.recv_sem, self.local_sem = scratch
        self.seat = Seat(self.axis)

    def view(self, place, half=None):
        start = self.seat.index(*place) * self.rows
        if half is None:
            return block_of(self.dst, start, self.rows)
        cut = middle(self.rows)
        return block_of(self.dst, start + half * cut, (cut, self.rows - cut)[half])

    def table(self, number):
        if number in (0, 1, 2, 8):
            return self.src, self.view((0, 0)), {0: (0, 1), 1: (0, -1), 2: (1, 0), 8: (0, 0, 1)}[number]
        if 8 <= number < 16:
            here = self.view(SHARE[number - 8])
            return here, here, (0, 0, 1)
        place, half, to = {
            7: ((1, -1), 0, (0, 1)),
            16: ((1, 1), 1, (0, -1)),
        }[number] if self.spare and number in (7, 16) else {
            3: ((0, -1), 0, (0, 1)),
            4: ((0, 1), 1, (0, -1)),
            5: ((1, 0), None, (0, 1)),
            6: ((1, 0), None, (0, -1)),
            7: ((0, 2), None, (1, 0)),
        }[number]
        here = self.view(place, half)
        return here, here, to

    def copy(self, number):
        src, dst, to = self.table(number)
        return remote(
            src,
            dst,
            self.send_sem.at[number],
            self.recv_sem.at[number],
            self.seat.device(self.seat.index(*to)),
        )

    def go(self, *numbers):
        for number in numbers:
            self.copy(number).start()

    def share(self, *numbers):
        if self.seat.cores == 2:
            self.go(*[8 + number for number in numbers])

    def arrived(self, *numbers):
        for number in numbers:
            self.copy(number).wait_recv()

    def local(self):
        return pltpu.make_async_copy(self.src, self.view((0, 0)), self.local_sem)

    def step(self, number, shared=True):
        if number == 0:
            self.local().start()
            self.go(0, 1, 2)
            self.share(0)
        elif number == 1:
            self.arrived(0, 1)
            self.go(3, 4)
            self.share(1, 2)
        elif number == 2:
            self.arrived(2)
            self.go(5, 6)
            self.share(3)
        elif number == 3:
            self.arrived(3, 4)
            if not self.spare:
                self.go(7)
            self.share(4)
        elif number == 4:
            self.arrived(5, 6)
            if self.spare:
                self.go(7, 16)
                self.share(5, 6)
                self.arrived(7, 16)
                self.share(7)
            else:
                self.arrived(7)
                self.share(5, 6, 7)
        else:
            numbers = list(range(8)) + [16] * self.spare
            if self.seat.cores == 2:
                numbers = numbers + list(range(8, 16))
                if shared:
                    self.arrived(*range(8, 16))
            for number in numbers:
                self.copy(number).wait_send()
            if shared:
                self.local().wait()


class Scatter:
    def __init__(self, axis, rows, width, kind=f32):
        self.axis, self.rows, self.width, self.kind = axis, rows, width, kind
        self.count = SP if axis == "sp" else DP

    def in_spec(self):
        return pl.BlockSpec(memory_space=pltpu.VMEM)

    def out(self):
        return (
            jax.ShapeDtypeStruct((self.rows, self.width), self.kind),
            pl.BlockSpec(memory_space=pltpu.VMEM),
        )

    def scratch(self):
        block, cut = (self.rows, self.width), middle(self.rows)
        first, second = (cut, self.width), (self.rows - cut, self.width)
        shapes = [block, block, block, first, second, block, block, block]
        shapes = shapes + [(8 if self.axis == "dp" else 4,) + block]
        return [pltpu.SemaphoreType.DMA((16,)), pltpu.SemaphoreType.DMA((16,))] + [
            pltpu.VMEM(shape, bf16) for shape in shapes
        ]

    partners = Gather.partners
    copy = Gather.copy
    go = Gather.go
    arrived = Gather.arrived

    def bind(self, src, out, scratch):
        self.src, self.dst = src, out
        self.send_sem, self.recv_sem = scratch[:2]
        self.got, self.made = scratch[2:10], scratch[10]
        self.seat = Seat(self.axis)

    def given(self, *place):
        return block_of(self.src, self.seat.index(*place) * self.rows, self.rows)

    def slot(self, place):
        if self.axis == "dp":
            return self.made.at[ORDER.index(place)]
        return self.made.at[((0, 2), (1, 0), (0, 1), (0, -1)).index(place)]

    def part(self, place):
        return self.slot(place) if self.axis == "dp" else self.given(*place)

    def ready(self, *places):
        if self.axis == "dp":
            for place in places:
                self.arrived(8 + ORDER.index(place))
                self.add(self.slot(place), [self.slot(place), self.given(*place)])

    def add(self, dst, terms):
        rows = dst.shape[0]
        step = 16

        @pl.loop(0, rows // step)
        def _(i):
            at = pl.ds(pl.multiple_of(i * step, step), step)
            total = terms[0][at, :].astype(f32)
            for term in terms[1:]:
                total = total + term[at, :].astype(f32)
            dst[at, :] = total.astype(dst.dtype)

    def halves(self, ref):
        cut = middle(self.rows)
        return ref.at[pl.ds(0, cut)], ref.at[pl.ds(cut, self.rows - cut)]

    def table(self, number):
        if number >= 8:
            return self.given(*ORDER[number - 8], 1), self.made.at[number - 8], (0, 0, 1)
        src, to = {
            0: (lambda: self.part((1, 2)), (1, 0)),
            1: (lambda: self.part((1, 1)), (0, 1)),
            2: (lambda: self.part((1, -1)), (0, -1)),
            3: (lambda: self.halves(self.slot((0, 2)))[0], (0, 1)),
            4: (lambda: self.halves(self.slot((0, 2)))[1], (0, -1)),
            5: (lambda: self.slot((1, 0)), (1, 0)),
            6: (lambda: self.slot((0, 1)), (0, 1)),
            7: (lambda: self.slot((0, -1)), (0, -1)),
        }[number]
        return src(), self.got[number], to

    def step(self, number):
        if number == 0:
            if self.axis == "dp":
                self.go(*range(8, 16))
            self.ready((1, 2))
            self.go(0)
            self.ready((1, 1))
            self.go(1)
            self.ready((1, -1))
            self.go(2)
        elif number == 1:
            self.ready((0, 2))
            self.arrived(0)
            self.add(self.slot((0, 2)), [self.part((0, 2)), self.got[0]])
            self.go(3, 4)
        elif number == 2:
            self.ready((1, 0))
            self.arrived(1, 2)
            self.add(self.slot((1, 0)), [self.part((1, 0)), self.got[1], self.got[2]])
            self.go(5)
        elif number == 3:
            self.ready((0, 1), (0, -1))
            self.arrived(3, 4)
            for place, half in (((0, 1), 0), ((0, -1), 1)):
                made, part = self.halves(self.slot(place)), self.halves(self.part(place))
                self.add(made[half], [part[half], self.got[3 + half]])
                if self.axis == "sp":
                    self.add(made[1 - half], [part[1 - half]])
                self.go(6 + half)
        elif number == 4:
            self.ready((0, 0))
            self.arrived(5, 6, 7)
            self.add(self.dst, [self.part((0, 0)), self.got[5], self.got[6], self.got[7]])
        else:
            for number in range(16 if self.axis == "dp" else 8):
                self.copy(number).wait_send()


class Swap:
    def __init__(self, axis, shape, take, put, kind="any"):
        self.axis, self.shape, self.take, self.put = axis, shape, take, put
        self.count = SP if axis == "sp" else DP

    def in_spec(self):
        return pl.BlockSpec(memory_space=pl.ANY)

    def out(self):
        return jax.ShapeDtypeStruct(self.shape, bf16), pl.BlockSpec(memory_space=pl.ANY)

    def scratch(self):
        sems = pltpu.SemaphoreType.DMA((self.count,))
        return [sems, sems, pltpu.SemaphoreType.DMA]

    def partners(self, seat):
        return [(seat.own + k) % seat.size for k in range(1, seat.size)]

    def bind(self, src, out, scratch):
        self.src, self.dst = src, out
        self.send_sem, self.recv_sem, self.local_sem = scratch
        self.seat = Seat(self.axis)

    def copy(self, k):
        to = (self.seat.own + k) % self.seat.size
        return remote(
            self.take(self.src, to),
            self.put(self.dst, self.seat.own),
            self.send_sem.at[k],
            self.recv_sem.at[k],
            self.seat.device(to),
        )

    def local(self):
        own = self.seat.own
        return pltpu.make_async_copy(self.take(self.src, own), self.put(self.dst, own), self.local_sem)

    def step(self, number):
        if number == 0:
            self.local().start()

            @pl.loop(1, self.seat.size)
            def _(k):
                self.copy(k).start()

        elif number == 5:

            @pl.loop(1, self.seat.size)
            def _(k):
                self.copy(k).wait_recv()
                self.copy(k).wait_send()

            self.local().wait()


def meet(ops):
    barrier = pltpu.get_barrier_semaphore()
    total = 0
    for axis in ("sp", "dp"):
        mine = [op for op in ops if op.axis == axis]
        if not mine:
            continue
        seat = Seat(axis)
        widest = max(mine, key=lambda op: len(op.partners(seat)))
        for partner in widest.partners(seat):
            pl.semaphore_signal(
                barrier, inc=1, device_id=seat.device(partner), device_id_type=pl.DeviceIdType.MESH
            )
            total += 1
    pl.semaphore_wait(barrier, total)


def exchange(name, number, ops, arrays, plan=None, chained=()):
    chained = dict(chained)
    plan = plan or [(op, step) for step in range(6) for op in range(len(ops))]
    counts = [len(op.scratch()) for op in ops]
    inputs = [k for k in range(len(ops)) if k not in chained]

    def body(*refs):
        given = dict(zip(inputs, refs[: len(inputs)]))
        outs = refs[len(inputs) : len(inputs) + len(ops)]
        rest = refs[len(inputs) + len(ops) :]
        for k, op in enumerate(ops):
            op.bind(given[k] if k in given else outs[chained[k]], outs[k], rest[: counts[k]])
            rest = rest[counts[k] :]
        meet(ops)
        for op, step in plan:
            ops[op].step(step)

    outs = [op.out() for op in ops]
    return pl.pallas_call(
        body,
        name=name,
        out_shape=[shape for shape, _ in outs],
        in_specs=[ops[k].in_spec() for k in inputs],
        out_specs=[spec for _, spec in outs],
        scratch_shapes=[entry for op in ops for entry in op.scratch()],
        compiler_params=pltpu.CompilerParams(
            collective_id=number, has_side_effects=True, vmem_limit_bytes=56 * 2**20
        ),
    )(*arrays)


def expert_kernel(
    hidden_own,
    weights,
    router_t,
    down,
    cot_all,
    picks,
    sum_out,
    mixed_out,
    weights_grad,
    down_grad,
    hidden,
    gate_up,
    down_w,
    sums,
    cot,
    cot_column,
    act_t,
    grads_t,
    gates_up,
    raw,
    acts,
    wide,
    stage,
    made_wide,
    made_down,
    load_sem,
    cot_sem,
    out_sem,
    *rest,
):
    gather, scatter = Gather("dp", ROWS, D), Scatter("dp", ROWS, D + ROWS)
    gather.bind(hidden_own, hidden, rest[:3])
    scatter.bind(sums, sum_out, rest[3:])
    loads = [
        pltpu.make_async_copy(weights.at[pl.ds(0, HALF)], gate_up.at[pl.ds(0, HALF)], load_sem.at[0]),
        pltpu.make_async_copy(weights.at[pl.ds(HALF, HALF)], gate_up.at[pl.ds(FULL, HALF)], load_sem.at[1]),
        pltpu.make_async_copy(down, down_w, load_sem.at[2]),
    ]
    for load in loads:
        load.start()
    meet([gather])
    gather.step(0)
    gate_up[pl.ds(HALF, 16), :] = router_t[...]
    gate_up[pl.ds(HALF + 16, FULL - HALF - 16), :] = jnp.zeros((FULL - HALF - 16, D), bf16)
    gate_up[pl.ds(FULL + HALF, FULL - HALF), :] = jnp.zeros((FULL - HALF, D), bf16)

    def at_least(i, k):
        return (i + 8 - k) // 8

    def rows_of(i):
        pair = i // 3 - i // 4 + i // 5 - i // 6
        ring = 3 * at_least(i, 1) - 2 * at_least(i, 2) - at_least(i, 3) + 2 * at_least(i, 4)
        ring = ring + at_least(i, 5) - 2 * at_least(i, 6) + at_least(i, 7)
        seat = gather.seat
        chip = ((seat.ring + ring) % 4) * 2 + (seat.pair + pair) % 2
        return pl.ds(pl.multiple_of(chip * CHUNK, CHUNK), CHUNK)

    def fetch(i):
        return pltpu.make_async_copy(cot_all.at[rows_of(i)], cot.at[i % 2], cot_sem.at[i % 2])

    def put(i):
        return pltpu.make_async_copy(stage.at[i % 2], mixed_out.at[rows_of(i)], out_sem.at[i % 2])

    fetch(0).start()
    for load in loads:
        load.wait()
    gather.local().wait()

    @pl.loop(0, 8)
    def _(i):
        @pl.when(i < 7)
        def _():
            fetch(i + 1).start()

        for step, when in ((1, 1), (2, 1), (3, 3), (4, 5)):

            @pl.when(i == when)
            def _():
                gather.step(step)

        rows = rows_of(i)
        sibling = rows.start + (1 - gather.seat.core) * ROWS
        landed = block_of(hidden, sibling, ROWS)
        remote(
            landed,
            landed,
            gather.send_sem.at[8 + i],
            gather.recv_sem.at[8 + i],
            gather.seat.device(gather.seat.index(0, 0, 1)),
        ).wait_recv()
        block = hidden[rows, :]

        @pl.loop(0, 2 * FULL // 256)
        def _(n):
            at = pl.ds(pl.multiple_of(n * 256, 256), 256)
            gates_up[:, at] = nt(block, gate_up[at, :])

        fetch(i).wait()
        cot_block = cot[i % 2]
        raw[...] = nt(cot_block, down_w[...])

        @pl.loop(0, CHUNK // 16)
        def _(k):
            at = pl.ds(pl.multiple_of(k * 16, 16), 16)
            lane = lax.broadcasted_iota(jnp.int32, (16, ROWS), 1)
            valid = (lane >= PICK_LANE) & (lane < PICK_LANE + EXPERTS)
            logits = jnp.where(valid, gates_up[at, FULL - ROWS : FULL], -1e30)
            top = jnp.max(logits, axis=1, keepdims=True)
            router = jnp.where(valid, jnp.exp(logits - top), 0.0)
            router = router / jnp.sum(router, axis=1, keepdims=True)
            chosen_rows = pl.ds(pl.multiple_of(rows.start + k * 16, 16), 16)
            dense = router * picks[chosen_rows, :].astype(f32)
            column = lax.broadcasted_iota(jnp.int32, (16, FULL), 1)
            gates = jnp.ones((16, FULL), f32)
            inside = []
            for e in range(EXPERTS):
                low, high = (NS + e) * ROOM, (NS + e + 1) * ROOM
                inside.append((column >= low) & (column < high))
                one = jnp.sum(jnp.where(lane == PICK_LANE + e, dense, 0.0), axis=1, keepdims=True)
                gates = jnp.where(inside[e], one, gates)
            gate, up, raw_grad = gates_up[at, :FULL], gates_up[at, FULL:], raw[at, :]
            sig = 1.0 / (1.0 + jnp.exp(-gate))
            silu = gate * sig
            act = silu * up
            acts[at, :] = (act.astype(bf16).astype(f32) * gates).astype(bf16)
            reached = act * raw_grad
            prob_grad = jnp.zeros((16, ROWS), f32)
            for e in range(EXPERTS):
                one = jnp.sum(jnp.where(inside[e], reached, 0.0), axis=1, keepdims=True)
                prob_grad = jnp.where(lane == PICK_LANE + e, one, prob_grad)
            sums[chosen_rows, D:] = prob_grad.astype(bf16)
            act_grad = raw_grad * gates
            wide[at, :FULL] = (act_grad * up * sig * (1.0 + gate * (1.0 - sig))).astype(bf16)
            wide[at, FULL:] = (act_grad * silu).astype(bf16)

        @pl.when(i >= 2)
        def _():
            put(i - 2).wait()

        @pl.loop(0, D // TILE)
        def _(n):
            at = pl.ds(pl.multiple_of(n * TILE, TILE), TILE)
            stage[i % 2, :, at] = nn(acts[...], down_w[:, at]).astype(bf16)
            sums[rows, at] = nn(wide[...], gate_up[:, at]).astype(bf16)

        put(i).start()
        act_t[:, rows] = acts[...].T
        grads_t[:, rows] = wide[...].T

    put(6).wait()
    put(7).wait()

    def columns(n):
        return pl.ds(pl.multiple_of(n * 256, 256), 256)

    def fetch_column(n):
        return pltpu.make_async_copy(cot_all.at[:, columns(n)], cot_column.at[n % 2], cot_sem.at[n % 2])

    def stores(n):
        k = n % 2
        return (
            pltpu.make_async_copy(made_wide.at[k], weights_grad.at[:, columns(n)], out_sem.at[k]),
            pltpu.make_async_copy(made_down.at[k], down_grad.at[:, columns(n)], out_sem.at[2 + k]),
        )

    def weight_grads(first, last):
        @pl.loop(first, last)
        def _(n):
            @pl.when(n < D // 256 - 1)
            def _():
                fetch_column(n + 1).start()

            @pl.when(n >= 2)
            def _():
                for store in stores(n - 2):
                    store.wait()

            made = nn(grads_t[...], hidden[:, columns(n)]).astype(bf16)
            made_wide[n % 2, :HALF, :] = made[:HALF]
            made_wide[n % 2, HALF:, :] = made[FULL : FULL + HALF]
            fetch_column(n).wait()
            made_down[n % 2] = nn(act_t[...], cot_column[n % 2]).astype(bf16)
            for store in stores(n):
                store.start()

    fetch_column(0).start()
    scatter.step(0)
    weight_grads(0, 4)
    scatter.step(1)
    scatter.step(2)
    weight_grads(4, 6)
    scatter.step(3)
    weight_grads(6, 8)
    scatter.step(4)
    for n in (6, 7):
        for store in stores(n):
            store.wait()
    gather.step(5, shared=False)
    scatter.step(5)


def experts(hidden_own, weights, router_t, down, cot_all, picks):
    any_spec, vmem = pl.BlockSpec(memory_space=pl.ANY), pl.BlockSpec(memory_space=pltpu.VMEM)
    gather, scatter = Gather("dp", ROWS, D), Scatter("dp", ROWS, D + ROWS)
    flops = 2 * GROUP * D * FULL * 9
    return pl.pallas_call(
        expert_kernel,
        name="experts",
        out_shape=[
            jax.ShapeDtypeStruct((ROWS, D + ROWS), f32),
            jax.ShapeDtypeStruct((GROUP, D), bf16),
            jax.ShapeDtypeStruct((2 * HALF, D), bf16),
            jax.ShapeDtypeStruct((FULL, D), bf16),
        ],
        in_specs=[any_spec, any_spec, vmem, any_spec, any_spec, vmem],
        out_specs=[vmem, any_spec, any_spec, any_spec],
        scratch_shapes=[
            pltpu.VMEM((GROUP, D), bf16),
            pltpu.VMEM((2 * FULL, D), bf16),
            pltpu.VMEM((FULL, D), bf16),
            pltpu.VMEM((GROUP, D + ROWS), bf16),
            pltpu.VMEM((2, CHUNK, D), bf16),
            pltpu.VMEM((2, GROUP, 256), bf16),
            pltpu.VMEM((FULL, GROUP), bf16),
            pltpu.VMEM((2 * FULL, GROUP), bf16),
            pltpu.VMEM((CHUNK, 2 * FULL), f32),
            pltpu.VMEM((CHUNK, FULL), f32),
            pltpu.VMEM((CHUNK, FULL), bf16),
            pltpu.VMEM((CHUNK, 2 * FULL), bf16),
            pltpu.VMEM((2, CHUNK, D), bf16),
            pltpu.VMEM((2, 2 * HALF, 256), bf16),
            pltpu.VMEM((2, FULL, 256), bf16),
            pltpu.SemaphoreType.DMA((3,)),
            pltpu.SemaphoreType.DMA((2,)),
            pltpu.SemaphoreType.DMA((4,)),
        ]
        + gather.scratch()
        + scatter.scratch(),
        compiler_params=pltpu.CompilerParams(
            collective_id=2, has_side_effects=True, vmem_limit_bytes=61 * 2**20
        ),
        cost_estimate=pl.CostEstimate(flops=flops, bytes_accessed=40 * 2**20, transcendentals=GROUP * FULL),
    )(hidden_own, weights, router_t, down, cot_all, picks)


def wait_all(copies):
    for copy in copies:
        copy.wait()


def swap_halves(values):
    lane = lax.broadcasted_iota(jnp.int32, values.shape, 1) % ROPE
    return jnp.where(lane < ROPE // 2, pltpu.roll(values, 96, 1), pltpu.roll(values, 32, 1))


def attention_ops():
    return (
        Gather("sp", ROWS, D, spare=True),
        Gather("dp", ROWS, PACK),
        Swap(
            "sp",
            (OW, D),
            lambda ref, j: ref.at[pl.ds(pl.multiple_of(j * OW, OW), OW), pl.ds(CORE_W, OW)],
            lambda ref, j: ref.at[:, pl.ds(pl.multiple_of(j * OW, OW), OW)],
        ),
        Gather("dp", ROWS, D, spare=True),
        Swap(
            "dp",
            (2 * HALF, D),
            lambda ref, j: ref.at[j],
            lambda ref, j: ref.at[:, pl.ds(pl.multiple_of(j * ROWS, ROWS), ROWS)],
        ),
        Scatter("sp", ROWS, D),
    )


def attention_kernel(
    tokens,
    pack,
    cotangent,
    pieces,
    cosine,
    sine,
    attn_sum,
    cot_all,
    gate_up,
    tok_out,
    weights_out,
    hidden_out,
    compressed_out,
    latent_out,
    query_out,
    key_out,
    value_out,
    head_out,
    out_w_out,
    misc_out,
    total_out,
    tok,
    weights,
    hidden,
    qc,
    latent,
    up_w,
    query,
    key,
    value,
    heads,
    out_w,
    misc_t,
    totals,
    sums,
    save_sem,
    *rest,
):
    ops = attention_ops()
    tok_op, pack_op, out_op, cot_op, piece_op, sum_op = ops
    bound = ((tokens, tok), (pack, weights), (weights, out_w), (cotangent, cot_all), (pieces, gate_up), (sums, attn_sum))
    for op, (src, dst) in zip(ops, bound):
        count = len(op.scratch())
        op.bind(src, dst, rest[:count])
        rest = rest[count:]
    meet(ops)
    tok_op.step(0)
    pack_op.step(0)
    for step in (1, 2, 3):
        tok_op.step(step)
        pack_op.step(step)
    pack_op.step(4)
    tok_op.step(4)
    pack_op.step(5)
    out_op.step(0)
    cot_op.step(0)
    piece_op.step(0)
    tok_op.step(5)
    saves = [
        pltpu.make_async_copy(src, dst, save_sem.at[k])
        for k, (src, dst) in enumerate(
            (
                (tok, tok_out),
                (weights, weights_out),
                (hidden, hidden_out),
                (qc.at[:, pl.ds(QW, RANK)], compressed_out),
                (latent, latent_out),
                (query, query_out),
                (key, key_out),
                (value, value_out),
                (heads, head_out),
                (out_w, out_w_out),
                (misc_t, misc_out),
                (totals, total_out),
            )
        )
    ]
    saves[0].start()
    saves[1].start()
    misc_t[...] = weights[:, MISC_AT:CORE_W].astype(f32).T
    saves[10].start()
    up = weights[:, UP_AT:].reshape(DP, 4, RANK // DP, ROWS)
    for k in range(4):
        up_w[:, k * ROWS : (k + 1) * ROWS] = up[:, k].reshape(RANK, ROWS)
    row = lax.broadcasted_iota(jnp.int32, (D, RANK), 0)
    column = lax.broadcasted_iota(jnp.int32, (D, RANK), 1)
    each = RANK // DP
    compact = ((row % ROWS < each) & (row // ROWS * each + row % ROWS == column)).astype(bf16)
    kv_gain = nn(misc_t[GAIN_KV - 6 : GAIN_KV + 2, :].astype(bf16), compact)[6:7]
    gain = misc_t[GAIN_ONE : GAIN_ONE + 1, :]

    @pl.loop(0, SEQ // 16)
    def _(k):
        at = pl.ds(pl.multiple_of(k * 16, 16), 16)
        values = tok[at, :].astype(f32)
        hidden[at, :] = (values * inverse_rms(values) * gain).astype(bf16)

    saves[2].start()
    cot_op.step(1)

    @pl.loop(0, SEQ // 256)
    def _(k):
        at = pl.ds(pl.multiple_of(k * 256, 256), 256)
        qc[at, :] = nn(hidden[at, :], weights[:, :CORE_W])

    saves[3].start()
    cot_op.step(2)

    @pl.loop(0, SEQ // 128)
    def _(k):
        at = pl.ds(pl.multiple_of(k * 128, 128), 128)
        inner = qc[at, QW : QW + RANK]
        latent[at, :] = (inner * inverse_rms(inner) * kv_gain).astype(bf16)
        ropes, key_rope = qc[at, 2 * NOPE : QW], qc[at, MISC_AT:CORE_W]
        cos, sin = cosine[at, :], sine[at, :]
        ropes = (ropes * cos + swap_halves(ropes) * sin).astype(bf16)
        key_rope = key_rope * cos + swap_halves(key_rope) * sin
        lane = lax.broadcasted_iota(jnp.int32, key_rope.shape, 1)
        key_rope = jnp.where(lane < ROPE, key_rope, 0.0)
        expanded = nn(latent[at, :], up_w[...]).astype(bf16)
        for h in range(HEADS_HERE):
            query[h, at, :NOPE] = qc[at, h * NOPE : (h + 1) * NOPE].astype(bf16)
            query[h, at, NOPE:] = ropes
            turned = key_rope if h == 0 else pltpu.roll(key_rope, ROPE, 1)
            key[h, at, NOPE:] = turned.astype(bf16)
            base = h * (NOPE + VDIM)
            key[h, at, :NOPE] = expanded[:, base : base + NOPE]
            value[h, at, :] = expanded[:, base + NOPE : base + NOPE + VDIM]

    for k in (4, 5, 6, 7):
        saves[k].start()
    for h in range(HEADS_HERE):
        for i in range(SEQ // 256):
            at, seen = pl.ds(i * 256, 256), (i + 1) * 256
            scores = nt(query[h, at, :], key[h, :seen, :]) * SCALE
            row = lax.broadcasted_iota(jnp.int32, scores.shape, 0) + i * 256
            column = lax.broadcasted_iota(jnp.int32, scores.shape, 1)
            scores = jnp.where(column <= row, scores, -1e9)
            top = jnp.max(scores, axis=1, keepdims=True)
            parts = jnp.exp(scores - top)
            total = jnp.sum(parts, axis=1, keepdims=True)
            probs = (parts / total).astype(bf16)
            heads[at, h * VDIM : (h + 1) * VDIM] = nn(probs, value[h, :seen, :]).astype(bf16)
            totals[h, at, :] = jnp.broadcast_to(top + jnp.log(total), (256, ROWS))

    saves[8].start()
    saves[11].start()
    out_op.step(5)
    saves[9].start()

    @pl.loop(0, D // TILE)
    def _(n):
        at = pl.ds(pl.multiple_of(n * TILE, TILE), TILE)
        sums[:, at] = nn(heads[...], out_w[:, at]).astype(bf16)

    sum_op.step(0)
    cot_op.step(3)
    sum_op.step(1)
    sum_op.step(2)
    cot_op.step(4)
    sum_op.step(3)
    sum_op.step(4)
    wait_all(saves)
    sum_op.step(5)
    cot_op.step(5)
    piece_op.step(5)


def attention(tokens, pack, cotangent, pieces, cosine, sine):
    any_spec, vmem = pl.BlockSpec(memory_space=pl.ANY), pl.BlockSpec(memory_space=pltpu.VMEM)
    kept = [
        ((SEQ, D), bf16),
        ((D, PACK), bf16),
        ((SEQ, D), bf16),
        ((SEQ, RANK), f32),
        ((SEQ, RANK), bf16),
        ((HEADS_HERE, SEQ, 2 * NOPE), bf16),
        ((HEADS_HERE, SEQ, 2 * NOPE), bf16),
        ((HEADS_HERE, SEQ, VDIM), bf16),
        ((SEQ, OW), bf16),
        ((OW, D), bf16),
        ((ROWS, D), f32),
        ((HEADS_HERE, SEQ, ROWS), f32),
    ]
    made = [((ROWS, D), f32), ((GROUP, D), bf16), ((2 * HALF, D), bf16)]
    scratch = kept[:3] + [((SEQ, CORE_W), f32), kept[4], ((RANK, KVW), bf16)] + kept[5:] + [((SEQ, D), bf16)]
    return pl.pallas_call(
        attention_kernel,
        name="attention",
        out_shape=[jax.ShapeDtypeStruct(*shape) for shape in made + kept],
        in_specs=[any_spec] * 4 + [vmem] * 2,
        out_specs=[vmem] + [any_spec] * (len(made) + len(kept) - 1),
        scratch_shapes=[pltpu.VMEM(*shape) for shape in scratch]
        + [pltpu.SemaphoreType.DMA((len(kept),))]
        + [entry for op in attention_ops() for entry in op.scratch()],
        compiler_params=pltpu.CompilerParams(
            collective_id=0, has_side_effects=True, vmem_limit_bytes=60 * 2**20
        ),
        cost_estimate=pl.CostEstimate(
            flops=2 * SEQ * D * (CORE_W + OW), bytes_accessed=60 * 2**20, transcendentals=SEQ * SEQ
        ),
    )(tokens, pack, cotangent, pieces, cosine, sine)


def per_device(
    tokens,
    cotangent,
    chosen,
    attn_gain,
    w_query,
    w_kv_down,
    kv_gain,
    w_kv_up,
    w_out,
    ffn_gain,
    w_router,
    shared_gate,
    shared_up,
    shared_down,
    expert_gate,
    expert_up,
    expert_down,
):
    own_sp = lax.axis_index("sp")
    picks = jnp.any(chosen[:, :, None] == jnp.arange(EXPERTS, dtype=jnp.int32), axis=1).astype(bf16)
    own_query = lax.dynamic_slice_in_dim(w_query, own_sp * QW, QW, 1)
    own_up = lax.dynamic_slice_in_dim(w_kv_up, own_sp * KVW, KVW, 1)
    pack = jnp.concatenate(
        [
            own_query[:, :NOPE],
            own_query[:, QK : QK + NOPE],
            own_query[:, NOPE:QK],
            own_query[:, QK + NOPE :],
            w_kv_down,
            picks,
            attn_gain[:, None],
            ffn_gain[:, None],
            jnp.pad(kv_gain, (0, ROWS - kv_gain.shape[0]))[:, None],
            jnp.zeros((ROWS, 9), bf16),
            w_router,
            jnp.zeros((ROWS, 44), bf16),
            lax.dynamic_slice_in_dim(w_out, own_sp * OW, OW, 1),
            own_up.reshape(RANK // DP, 4, ROWS).transpose(1, 0, 2).reshape(ROWS, ROWS),
        ],
        axis=1,
    )
    gate_up = jnp.stack(
        [
            jnp.concatenate([shared_gate, expert_gate], axis=1),
            jnp.concatenate([shared_up, expert_up], axis=1),
        ]
    )
    gate_up = gate_up.reshape(2, ROWS, SETS, DP, SLICE).transpose(3, 0, 2, 4, 1)
    gate_up = jnp.pad(gate_up, ((0, 0),) * 3 + ((0, ROOM - SLICE), (0, 0)))
    gate_up = gate_up.reshape(DP, 2 * HALF, ROWS)
    down = jnp.concatenate([shared_down, expert_down], axis=1).transpose(1, 0, 2)
    down = jnp.pad(down, ((0, 0), (0, ROOM - SLICE), (0, 0))).reshape(HALF, D)
    down = jnp.pad(down, ((0, FULL - HALF), (0, 0)))

    cosine, sine = rope_tables(jnp.arange(SEQ, dtype=f32))
    cosine = jnp.concatenate([cosine] * 4, axis=1)
    sine = jnp.concatenate([-sine, sine] * 2, axis=1)
    (
        attn_proj,
        cot_all,
        gate_up,
        tok_all,
        weights,
        hidden_one,
        compressed,
        latent,
        queries,
        keys,
        values,
        head_out,
        out_w,
        misc,
        log_totals,
    ) = attention(tokens, pack, cotangent, gate_up, cosine, sine)
    gain_one, gain_two = misc[GAIN_ONE], misc[GAIN_TWO]
    latent_gain = misc[GAIN_KV].reshape(DP, ROWS)[:, : RANK // DP].reshape(RANK)
    router_t = misc[ROUTER_LANE : ROUTER_LANE + 16].astype(bf16)
    router_w = router_t[:EXPERTS]
    picks_all = weights[:, MISC_AT:CORE_W]
    resid_two = tokens.astype(f32) + attn_proj
    scale_two = inverse_rms(resid_two)
    hidden_two = (resid_two * scale_two * gain_two).astype(bf16)

    hidden_grad, mixed_part, gate_up_grad, down_grad = experts(
        hidden_two, gate_up, router_t, down, cot_all, picks_all
    )
    prob_grad = hidden_grad[:, D + PICK_LANE : D + PICK_LANE + EXPERTS]
    hidden_grad = hidden_grad[:, :D]

    logits = nt(hidden_two, router_w)
    router = jax.nn.softmax(logits, axis=-1)
    prob_grad = prob_grad * picks.astype(f32)
    logit_grad = (
        router * (prob_grad - jnp.sum(router * prob_grad, axis=-1, keepdims=True))
    ).astype(bf16)
    hidden_grad = hidden_grad + nn(logit_grad, router_w)
    router_grad = tn(hidden_two, logit_grad)
    gain_two_grad = jnp.sum(hidden_grad * resid_two * scale_two, axis=0)
    upstream = cotangent.astype(f32)
    resid_two_grad = upstream + norm_back(resid_two, scale_two, gain_two, hidden_grad)
    proj_grad = resid_two_grad.astype(bf16)

    proj_grad_all, mixed, gate_up_grad, down_grad = exchange(
        "gather_projection_grad",
        4,
        [
            Gather("sp", ROWS, D, spare=True),
            Scatter("dp", ROWS, D),
            Scatter("sp", GU_PART, D, bf16),
            Scatter("sp", DN_PART, D, bf16),
        ],
        [proj_grad, mixed_part, gate_up_grad, down_grad],
    )
    mixed = (resid_two + mixed).astype(bf16)
    out_w_grad = tn(head_out, proj_grad_all)
    head_grad = nt(proj_grad_all, out_w).astype(bf16)
    rows = jnp.arange(SEQ, dtype=jnp.int32)
    allowed = rows[None, :] <= rows[:, None]
    low = jnp.arange(ROWS) < ROPE
    rope_grad, nope_grads, expanded_grads, key_rope_grad = 0.0, [], [], 0.0
    for h in range(HEADS_HERE):
        piece = head_grad[:, h * VDIM : (h + 1) * VDIM]
        prob = jnp.exp(jnp.where(allowed, nt(queries[h], keys[h]) * SCALE, -1e9) - log_totals[h, :, :1])
        dprob = nt(piece, values[h])
        delta = jnp.sum(prob * dprob, axis=-1, keepdims=True)
        score_grad = (prob * (dprob - delta) * SCALE).astype(bf16)
        query_grad = nn(score_grad, keys[h]).astype(bf16)
        key_grad = tn(score_grad, queries[h]).astype(bf16)
        value_grad = tn(prob.astype(bf16), piece).astype(bf16)
        nope_grads.append(query_grad[:, :NOPE])
        rope_grad = rope_grad + query_grad[:, NOPE:].astype(f32)
        expanded_grads += [key_grad[:, :NOPE], value_grad]
        own = key_grad[:, NOPE + h * ROPE : NOPE + (h + 1) * ROPE].astype(f32)
        key_rope_grad = key_rope_grad + own

    def unrotate(values, cos, sin):
        flipped = values.reshape(SEQ, -1, 2, ROPE // 2)[:, :, ::-1].reshape(values.shape)
        return values * cos - flipped * sin

    rope_grad = unrotate(rope_grad, cosine, sine).astype(bf16)
    key_rope_grad = unrotate(key_rope_grad, cosine[:, :ROPE], sine[:, :ROPE]).astype(bf16)
    expanded_grad = jnp.concatenate(expanded_grads, axis=1)
    up_w = weights[:, UP_AT:].reshape(DP, 4, RANK // DP, ROWS).transpose(0, 2, 1, 3).reshape(RANK, KVW)
    up_w_grad = tn(latent, expanded_grad)
    latent_grad = nt(expanded_grad, up_w)
    scale_latent = inverse_rms(compressed)
    latent_in_grad = norm_back(compressed, scale_latent, latent_gain, latent_grad)
    latent_gain_grad = jnp.sum(latent_grad * compressed * scale_latent, axis=0)
    qc_grad = jnp.concatenate(
        nope_grads
        + [rope_grad, latent_in_grad.astype(bf16), key_rope_grad, jnp.zeros((SEQ, ROPE), bf16)],
        axis=1,
    )
    qc_w_grad = tn(hidden_one, qc_grad)
    hidden_one_grad = nt(qc_grad, weights[:, :CORE_W])
    resid_all = tok_all.astype(f32)
    gain_one_grad = jnp.sum(hidden_one_grad * resid_all * inverse_rms(resid_all), axis=0)

    (out_cols_grad,) = exchange(
        "swap_projection_weight_grad",
        5,
        [
            Swap(
                "sp",
                (D, OW),
                lambda ref, j: ref.at[:, pl.ds(pl.multiple_of(j * OW, OW), OW)],
                lambda ref, j: ref.at[pl.ds(pl.multiple_of(j * OW, OW), OW)],
            )
        ],
        [out_w_grad.astype(bf16)],
    )
    latent_gain_grad = jnp.pad(
        latent_gain_grad.reshape(DP, RANK // DP), ((0, 0), (0, ROWS - RANK // DP))
    ).reshape(D)
    grads = jnp.concatenate(
        [
            qc_w_grad[:, : QW + RANK + ROPE].astype(bf16),
            gain_one_grad.astype(bf16)[:, None],
            gain_two_grad.astype(bf16)[:, None],
            latent_gain_grad.astype(bf16)[:, None],
            router_grad.astype(bf16),
            jnp.zeros((D, ROPE - 7), bf16),
            out_cols_grad,
            up_w_grad.astype(bf16).reshape(D, ROWS),
        ],
        axis=1,
    )
    grads, hidden_one_grad, _, gu_total, dn_total = exchange(
        "sum_grads",
        6,
        [
            Scatter("dp", ROWS, PACK, bf16),
            Scatter("sp", ROWS, D),
            Swap(
                "dp",
                (DP * GU_PART, ROWS),
                lambda ref, j: ref.at[:, pl.ds(pl.multiple_of(j * ROWS, ROWS), ROWS)],
                lambda ref, j: ref.at[pl.ds(pl.multiple_of(j * GU_PART, GU_PART), GU_PART)],
            ),
            Gather("sp", DP * GU_PART, ROWS),
            Gather("sp", DN_PART, D),
        ],
        [grads, hidden_one_grad.astype(bf16), gate_up_grad, down_grad],
        plan=[(2, 0), (0, 0), (1, 0), (4, 0), (2, 5), (3, 0)]
        + [(op, step) for step in range(1, 6) for op in (1, 0, 4, 3)],
        chained=[(3, 2)],
    )
    (grads,) = exchange("gather_grads", 7, [Gather("sp", ROWS, PACK)], [grads])
    gu_total = gu_total.reshape(SP, DP, GU_PART, ROWS)
    grads = grads.reshape(SP, ROWS, PACK)
    resid_one = tokens.astype(f32)
    own_scale = inverse_rms(resid_one)
    tokens_grad = resid_two_grad + norm_back(resid_one, own_scale, gain_one, hidden_one_grad)
    tokens_grad = tokens_grad.astype(bf16)

    def side_by_side(block, width):
        return block.astype(f32).transpose(1, 0, 2).reshape(-1, SP * width)

    query_total = grads[:, :, :QW]
    query_total = jnp.concatenate(
        [
            query_total[:, :, :NOPE],
            query_total[:, :, 2 * NOPE : 2 * NOPE + ROPE],
            query_total[:, :, NOPE : 2 * NOPE],
            query_total[:, :, 2 * NOPE + ROPE :],
        ],
        axis=2,
    )
    query_total = side_by_side(query_total, QW)
    tail = jnp.sum(grads[:, :, QW:CORE_W].astype(f32), axis=0)
    down_total, tail = tail[:, : RANK + ROPE], tail[:, RANK + ROPE :]
    out_total = side_by_side(grads[:, :, CORE_W:UP_AT], OW)
    up_total = side_by_side(grads[:, :, UP_AT:].reshape(SP, RANK // DP, KVW), KVW)

    gu_total = gu_total.transpose(0, 2, 1, 3).reshape(2, SETS, ROOM, DP, ROWS)[:, :, :SLICE]
    gu_total = gu_total.transpose(0, 4, 1, 3, 2).reshape(2, ROWS, SETS, FE).astype(f32)
    dn_total = dn_total[:HALF].reshape(SETS, ROOM, D)[:, :SLICE].transpose(1, 0, 2).astype(f32)
    return (
        mixed,
        tokens_grad,
        tail[:, 0],
        query_total,
        down_total,
        tail[: RANK // DP, 2],
        up_total,
        out_total,
        tail[:, 1],
        tail[:, 3:7],
        gu_total[0, :, :NS],
        gu_total[1, :, :NS],
        dn_total[:, :NS],
        gu_total[0, :, NS:],
        gu_total[1, :, NS:],
        dn_total[:, NS:],
    )


def solution(mesh):
    rows = P(("dp", "sp"), None)
    vec, mat, cube = P("dp"), P("dp", None), P("dp", None, None)
    return jax.shard_map(
        per_device,
        mesh=mesh,
        in_specs=(rows, rows, rows, vec, mat, mat, vec, mat, mat, vec, mat) + (cube,) * 6,
        out_specs=(rows, rows, vec, mat, mat, vec, mat, mat, vec, mat) + (cube,) * 6,
        check_vma=False,
    )
```

```python
import functools

import jax
import jax.numpy as jnp
import numpy as np
from jax import lax
from jax.experimental import pallas as pl
from jax.experimental.pallas import tpu as pltpu
from jax.sharding import PartitionSpec as P

D = 2048
HEADS = 16
NOPE = 128
ROPE = 64
QK = NOPE + ROPE
VDIM = 128
RANK = 512
FE = 1408
NS = 2
EXPERTS = 4
TOP = 2
SETS = NS + EXPERTS
DP = 16
SP = 8
ROWS = 128
SEQ = SP * ROWS
GROUP = DP * ROWS
HEADS_HERE = HEADS // SP
QW = HEADS_HERE * QK
KVW = HEADS_HERE * (NOPE + VDIM)
OW = HEADS_HERE * VDIM
SLICE = FE // DP
CORE_W = 1024
UP_AT = CORE_W
GRAD_UP_AT = CORE_W + OW
MISC_AT = CORE_W - ROWS
PICK_LANE, GAIN_ONE, GAIN_TWO, GAIN_KV, ROUTER_LANE = 64, 68, 69, 70, 80
ROOM = 96
HALF = SETS * ROOM
FULL = 640
CHUNK = 2 * ROWS
TILE = 512
SCALE = QK ** (-0.5)
PACK = QW + RANK + ROPE + ROPE + ROWS
GRAD_PACK = PACK + OW
GU_PART = 2 * HALF // SP
RELAY = 2 * HALF // SP
UNITS = ROOM // SP
DN_PART = FULL // SP

epsilon = 1e-06
bf16 = jnp.bfloat16
f32 = jnp.float32


def mm(left, right, dims):
    return lax.dot_general(left, right, ((dims[0], dims[1]), ((), ())), preferred_element_type=f32)


def nn(left, right):
    return mm(left, right, ((1,), (0,)))


def nt(left, right):
    return mm(left, right, ((1,), (1,)))


def tn(left, right):
    return mm(left, right, ((0,), (0,)))


def rope_tables():
    inverse = 10000.0 ** (-np.arange(ROPE // 2, dtype=np.float64) * 2.0 / ROPE)
    angles = np.arange(SEQ, dtype=np.float64)[:, None] * inverse[None, :]
    cosine, sine = np.cos(angles), np.sin(angles)
    cosine = np.concatenate([cosine] * 4, axis=1)
    sine = np.concatenate([-sine, sine] * 2, axis=1)
    return jnp.asarray(cosine, f32), jnp.asarray(sine, f32)


def norm_back(values, scale, gain, grad):
    scaled = gain * grad
    total = jnp.sum(scaled * values, axis=-1, keepdims=True) / values.shape[-1]
    return scale * scaled - values * (scale * scale * scale) * total


def inverse_rms(values):
    return lax.rsqrt(jnp.mean(values * values, axis=-1, keepdims=True) + epsilon)


class Seat:
    def __init__(self, axis):
        own_dp, own_sp = lax.axis_index("dp"), lax.axis_index("sp")
        self.axis = axis
        if axis == "sp":
            self.pair, self.ring, self.core, self.cores = own_sp // 4, own_sp % 4, 0, 1
            self.own, self.size = own_sp, SP
            self.device = lambda index: (own_dp, index)
        else:
            self.ring, self.pair, self.core, self.cores = own_dp // 4, (own_dp // 2) % 2, own_dp % 2, 2
            self.own, self.size = own_dp, DP
            self.device = lambda index: (index, own_sp)

    def index(self, pair, ring, core=0):
        pair, ring = (self.pair + pair) % 2, (self.ring + ring) % 4
        if self.axis == "sp":
            return pair * 4 + ring
        return (ring * 2 + pair) * 2 + (self.core + core) % 2


def remote(src, dst, send_sem, recv_sem, device):
    return pltpu.make_async_remote_copy(
        src_ref=src,
        dst_ref=dst,
        send_sem=send_sem,
        recv_sem=recv_sem,
        device_id=device,
        device_id_type=pl.DeviceIdType.MESH,
    )


def block_of(ref, start, size):
    return ref.at[pl.ds(pl.multiple_of(start, 16), size)]


def middle(rows):
    return (rows // 2 + 15) // 16 * 16


NEAR = ((0, 1), (0, -1), (1, 0))
SHARE = ((0, 0), (0, -1), (0, 1), (1, 0), (0, 2), (1, -1), (1, 1), (1, 2))
ORDER = ((1, 2), (1, 1), (1, -1), (0, 2), (1, 0), (0, 1), (0, -1), (0, 0))


class Gather:
    def __init__(self, axis, rows, width, spare=False):
        self.axis, self.rows, self.width, self.spare = axis, rows, width, spare
        self.count = SP if axis == "sp" else DP

    def in_spec(self):
        return pl.BlockSpec(memory_space=pl.ANY)

    def out(self):
        return (
            jax.ShapeDtypeStruct((self.count * self.rows, self.width), bf16),
            pl.BlockSpec(memory_space=pl.ANY),
        )

    def scratch(self):
        return [pltpu.SemaphoreType.DMA((17,)), pltpu.SemaphoreType.DMA((17,)), pltpu.SemaphoreType.DMA]

    def partners(self, seat):
        near = [seat.index(*n) for n in NEAR]
        return near + ([seat.index(0, 0, 1)] if seat.cores == 2 else [])

    def bind(self, src, out, scratch):
        self.src, self.dst = src, out
        self.send_sem, self.recv_sem, self.local_sem = scratch
        self.seat = Seat(self.axis)

    def view(self, place, half=None):
        start = self.seat.index(*place) * self.rows
        if half is None:
            return block_of(self.dst, start, self.rows)
        cut = middle(self.rows)
        return block_of(self.dst, start + half * cut, (cut, self.rows - cut)[half])

    def table(self, number):
        if number in (0, 1, 2, 8):
            return self.src, self.view((0, 0)), {0: (0, 1), 1: (0, -1), 2: (1, 0), 8: (0, 0, 1)}[number]
        if 8 <= number < 16:
            here = self.view(SHARE[number - 8])
            return here, here, (0, 0, 1)
        place, half, to = {
            7: ((1, -1), 0, (0, 1)),
            16: ((1, 1), 1, (0, -1)),
        }[number] if self.spare and number in (7, 16) else {
            3: ((0, -1), 0, (0, 1)),
            4: ((0, 1), 1, (0, -1)),
            5: ((1, 0), None, (0, 1)),
            6: ((1, 0), None, (0, -1)),
            7: ((0, 2), None, (1, 0)),
        }[number]
        here = self.view(place, half)
        return here, here, to

    def copy(self, number):
        src, dst, to = self.table(number)
        return remote(
            src,
            dst,
            self.send_sem.at[number],
            self.recv_sem.at[number],
            self.seat.device(self.seat.index(*to)),
        )

    def go(self, *numbers):
        for number in numbers:
            self.copy(number).start()

    def share(self, *numbers):
        if self.seat.cores == 2:
            self.go(*[8 + number for number in numbers])

    def arrived(self, *numbers):
        for number in numbers:
            self.copy(number).wait_recv()

    def local(self):
        return pltpu.make_async_copy(self.src, self.view((0, 0)), self.local_sem)

    def step(self, number, shared=True):
        if number == 0:
            self.local().start()
            self.go(0, 1, 2)
            self.share(0)
        elif number == 1:
            self.arrived(0, 1)
            self.go(3, 4)
            self.share(1, 2)
        elif number == 2:
            self.arrived(2)
            self.go(5, 6)
            self.share(3)
        elif number == 3:
            self.arrived(3, 4)
            if not self.spare:
                self.go(7)
            self.share(4)
        elif number == 4:
            self.arrived(5, 6)
            if self.spare:
                self.go(7, 16)
                self.share(5, 6)
                self.arrived(7, 16)
                self.share(7)
            else:
                self.arrived(7)
                self.share(5, 6, 7)
        else:
            numbers = list(range(8)) + [16] * self.spare
            if self.seat.cores == 2:
                numbers = numbers + list(range(8, 16))
                if shared:
                    self.arrived(*range(8, 16))
            for number in numbers:
                self.copy(number).wait_send()
            if shared:
                self.local().wait()


class Scatter:
    def __init__(self, axis, rows, width, kind=f32, spare=False):
        self.axis, self.rows, self.width, self.kind, self.spare = axis, rows, width, kind, spare
        self.count = SP if axis == "sp" else DP

    def in_spec(self):
        return pl.BlockSpec(memory_space=pltpu.VMEM)

    def out(self):
        return (
            jax.ShapeDtypeStruct((self.rows, self.width), self.kind),
            pl.BlockSpec(memory_space=pltpu.VMEM),
        )

    def scratch(self):
        block, cut = (self.rows, self.width), middle(self.rows)
        first, second = (cut, self.width), (self.rows - cut, self.width)
        shapes = [block, block, block, first, second, block, block, block]
        shapes = shapes + [(8 if self.axis == "dp" else 5,) + block]
        return [pltpu.SemaphoreType.DMA((17,)), pltpu.SemaphoreType.DMA((17,))] + [
            pltpu.VMEM(shape, bf16) for shape in shapes
        ]

    partners = Gather.partners
    copy = Gather.copy
    go = Gather.go
    arrived = Gather.arrived

    def bind(self, src, out, scratch):
        self.src, self.dst = src, out
        self.send_sem, self.recv_sem = scratch[:2]
        self.got, self.made = scratch[2:10], scratch[10]
        self.seat = Seat(self.axis)

    def given(self, *place):
        return block_of(self.src, self.seat.index(*place) * self.rows, self.rows)

    def slot(self, place):
        if self.axis == "dp":
            return self.made.at[ORDER.index(place)]
        kept = ((1, 0), (0, 1), (0, -1)) + (((1, 1), (1, -1)) if self.spare else ((0, 2),))
        return self.made.at[kept.index(place)]

    def part(self, place):
        return self.slot(place) if self.axis == "dp" else self.given(*place)

    def ready(self, *places):
        if self.axis == "dp":
            for place in places:
                self.arrived(8 + ORDER.index(place))
                self.add(self.slot(place), [self.slot(place), self.given(*place)])

    def add(self, dst, terms):
        rows = dst.shape[0]
        step = 16

        @pl.loop(0, rows // step)
        def _(i):
            at = pl.ds(pl.multiple_of(i * step, step), step)
            total = terms[0][at, :].astype(f32)
            for term in terms[1:]:
                total = total + term[at, :].astype(f32)
            dst[at, :] = total.astype(dst.dtype)

    def add_half(self, place, half, term):
        made, part = self.halves(self.slot(place)), self.halves(self.part(place))
        self.add(made[half], [part[half], term])
        if self.axis == "sp":
            self.add(made[1 - half], [part[1 - half]])

    def halves(self, ref):
        cut = middle(self.rows)
        return ref.at[pl.ds(0, cut)], ref.at[pl.ds(cut, self.rows - cut)]

    def table(self, number):
        if 8 <= number < 16:
            return self.given(*ORDER[number - 8], 1), self.made.at[number - 8], (0, 0, 1)
        if self.spare and number in (0, 1, 2, 3, 4, 16):
            if number in (1, 2):
                return self.slot((1, 3 - 2 * number)), self.got[number], (0, 3 - 2 * number)
            half = 0 if number in (0, 3) else 1
            src = self.halves(self.part((1, 2) if number in (0, 16) else (0, 2)))[half]
            dst = self.halves(self.got[0])[half] if number in (0, 16) else self.got[number]
            return src, dst, (0, 1 - 2 * half)
        src, to = {
            0: (lambda: self.part((1, 2)), (1, 0)),
            1: (lambda: self.part((1, 1)), (0, 1)),
            2: (lambda: self.part((1, -1)), (0, -1)),
            3: (lambda: self.halves(self.slot((0, 2)))[0], (0, 1)),
            4: (lambda: self.halves(self.slot((0, 2)))[1], (0, -1)),
            5: (lambda: self.slot((1, 0)), (1, 0)),
            6: (lambda: self.slot((0, 1)), (0, 1)),
            7: (lambda: self.slot((0, -1)), (0, -1)),
        }[number]
        return src(), self.got[number], to

    def step(self, number):
        if number == 0:
            if self.axis == "dp":
                self.go(*range(8, 16))
            self.ready((1, 2))
            if self.spare:
                self.go(0, 16)
                self.ready((0, 2))
                self.go(3, 4)
                self.ready((1, 1), (1, -1))
                return
            self.go(0)
            self.ready((1, 1))
            self.go(1)
            self.ready((1, -1))
            self.go(2)
        elif number == 1 and self.spare:
            self.arrived(0, 16)
            for place, half in (((1, 1), 0), ((1, -1), 1)):
                self.add_half(place, half, self.halves(self.got[0])[half])
                self.go(1 + half)
        elif number == 1:
            self.ready((0, 2))
            self.arrived(0)
            self.add(self.slot((0, 2)), [self.part((0, 2)), self.got[0]])
            self.go(3, 4)
        elif number == 2:
            self.ready((1, 0))
            self.arrived(1, 2)
            self.add(self.slot((1, 0)), [self.part((1, 0)), self.got[1], self.got[2]])
            self.go(5)
        elif number == 3:
            self.ready((0, 1), (0, -1))
            self.arrived(3, 4)
            for place, half in (((0, 1), 0), ((0, -1), 1)):
                self.add_half(place, half, self.got[3 + half])
                self.go(6 + half)
        elif number == 4:
            self.ready((0, 0))
            self.arrived(5, 6, 7)
            self.add(self.dst, [self.part((0, 0)), self.got[5], self.got[6], self.got[7]])
        else:
            numbers = list(range(16 if self.axis == "dp" else 8)) + [16] * self.spare
            for number in numbers:
                self.copy(number).wait_send()


class Swap:
    def __init__(self, axis, shape, take, put, kind="any"):
        self.axis, self.shape, self.take, self.put = axis, shape, take, put
        self.count = SP if axis == "sp" else DP

    def in_spec(self):
        return pl.BlockSpec(memory_space=pl.ANY)

    def out(self):
        return jax.ShapeDtypeStruct(self.shape, bf16), pl.BlockSpec(memory_space=pl.ANY)

    def scratch(self):
        sems = pltpu.SemaphoreType.DMA((self.count,))
        return [sems, sems, pltpu.SemaphoreType.DMA]

    def partners(self, seat):
        return [(seat.own + k) % seat.size for k in range(1, seat.size)]

    def bind(self, src, out, scratch):
        self.src, self.dst = src, out
        self.send_sem, self.recv_sem, self.local_sem = scratch
        self.seat = Seat(self.axis)

    def copy(self, k):
        to = (self.seat.own + k) % self.seat.size
        return remote(
            self.take(self.src, to),
            self.put(self.dst, self.seat.own),
            self.send_sem.at[k],
            self.recv_sem.at[k],
            self.seat.device(to),
        )

    def local(self):
        own = self.seat.own
        return pltpu.make_async_copy(self.take(self.src, own), self.put(self.dst, own), self.local_sem)

    def step(self, number):
        if number == 0:
            self.local().start()

            @pl.loop(1, self.seat.size)
            def _(k):
                self.copy(k).start()

        elif number == 5:

            @pl.loop(1, self.seat.size)
            def _(k):
                self.copy(k).wait_recv()
                self.copy(k).wait_send()

            self.local().wait()


def meet(ops):
    barrier = pltpu.get_barrier_semaphore()
    total = 0
    for axis in ("sp", "dp"):
        mine = [op for op in ops if op.axis == axis]
        if not mine:
            continue
        seat = Seat(axis)
        widest = max(mine, key=lambda op: len(op.partners(seat)))
        for partner in widest.partners(seat):
            pl.semaphore_signal(
                barrier, inc=1, device_id=seat.device(partner), device_id_type=pl.DeviceIdType.MESH
            )
            total += 1
    pl.semaphore_wait(barrier, total)


def exchange(name, number, ops, arrays, plan=None, chained=()):
    chained = dict(chained)
    plan = plan or [(op, step) for step in range(6) for op in range(len(ops))]
    counts = [len(op.scratch()) for op in ops]
    inputs = [k for k in range(len(ops)) if k not in chained]

    def body(*refs):
        given = dict(zip(inputs, refs[: len(inputs)]))
        outs = refs[len(inputs) : len(inputs) + len(ops)]
        rest = refs[len(inputs) + len(ops) :]
        for k, op in enumerate(ops):
            op.bind(given[k] if k in given else outs[chained[k]], outs[k], rest[: counts[k]])
            rest = rest[counts[k] :]
        meet(ops)
        for op, step in plan:
            ops[op].step(step)

    outs = [op.out() for op in ops]
    return pl.pallas_call(
        body,
        name=name,
        out_shape=[shape for shape, _ in outs],
        in_specs=[ops[k].in_spec() for k in inputs],
        out_specs=[spec for _, spec in outs],
        scratch_shapes=[entry for op in ops for entry in op.scratch()],
        compiler_params=pltpu.CompilerParams(
            collective_id=number, has_side_effects=True, vmem_limit_bytes=56 * 2**20
        ),
    )(*arrays)


def expert_of(column):
    lane = jnp.zeros(column.shape, jnp.int32)
    for e in range(EXPERTS):
        low = (NS + e) * ROOM
        lane = jnp.where((column >= low) & (column < low + ROOM), PICK_LANE + e, lane)
    return lane


def two_terms(values):
    high = values.astype(bf16)
    return high, (values - high.astype(f32)).astype(bf16)


def expert_kernel(
    hidden_own,
    weights,
    router_t,
    down,
    cot_all,
    picks,
    sum_out,
    mixed_out,
    weights_grad,
    down_grad,
    hidden,
    gate_up,
    down_w,
    sums,
    stage,
    cot_column,
    acts,
    wide,
    gates_up,
    raw,
    gates,
    dense_terms,
    reached,
    spread,
    collect,
    made_wide,
    made_down,
    load_sem,
    in_sem,
    out_sem,
    *rest,
):
    gather, scatter = Gather("dp", ROWS, D), Scatter("dp", ROWS, D + ROWS)
    gather.bind(hidden_own, hidden, rest[:3])
    scatter.bind(sums, sum_out, rest[3:])
    loads = [
        pltpu.make_async_copy(down, down_w, load_sem.at[2]),
        pltpu.make_async_copy(weights, sums.at[pl.ds(0, 2 * HALF), pl.ds(0, D)], load_sem.at[0]),
    ]
    for load in loads:
        load.start()

    def chunk(i):
        return pl.ds(pl.multiple_of(i * CHUNK, CHUNK), CHUNK)

    def columns(n):
        return pl.ds(pl.multiple_of(n * 256, 256), 256)

    def fetch(i):
        return pltpu.make_async_copy(cot_all.at[chunk(i)], stage.at[i % 2], in_sem.at[i % 2])

    def put(i):
        return pltpu.make_async_copy(stage.at[i % 2], mixed_out.at[chunk(i)], in_sem.at[i % 2])

    def fetch_column(n):
        return pltpu.make_async_copy(cot_all.at[:, columns(n)], cot_column.at[n % 2], in_sem.at[2 + n % 2])

    def stores(n):
        k = n % 2
        return (
            pltpu.make_async_copy(made_wide.at[k], weights_grad.at[:, columns(n)], out_sem.at[k]),
            pltpu.make_async_copy(made_down.at[k], down_grad.at[:, columns(n)], out_sem.at[2 + k]),
        )

    fetch(0).start()
    fetch_column(0).start()
    meet([gather])
    gather.step(0)
    gate_up[pl.ds(HALF, 16), :] = router_t[...]
    gate_up[pl.ds(HALF + 16, FULL - HALF - 16), :] = jnp.zeros((FULL - HALF - 16, D), bf16)
    gate_up[pl.ds(FULL + HALF, FULL - HALF), :] = jnp.zeros((FULL - HALF, D), bf16)
    row = lax.broadcasted_iota(jnp.int32, (ROWS, FULL), 0)
    lane_of = expert_of(lax.broadcasted_iota(jnp.int32, (ROWS, FULL), 1))
    hot = (row == lane_of).astype(bf16)
    spread[:ROWS, :] = hot
    spread[ROWS:, :] = hot
    lane = lax.broadcasted_iota(jnp.int32, (FULL, ROWS), 1)
    hot = (lane == expert_of(lax.broadcasted_iota(jnp.int32, (FULL, ROWS), 0))).astype(bf16)
    collect[:FULL, :] = hot
    collect[FULL:, :] = hot
    loads[0].wait()

    @pl.loop(0, 8)
    def _(i):
        @pl.when(i < 7)
        def _():
            fetch(i + 1).start()

        fetch(i).wait()
        raw[chunk(i), :] = nt(stage[i % 2], down_w[...])

    loads[1].wait()
    for k in range(2 * SETS):
        for part in range(SP):
            units = sums[part * RELAY + k * UNITS : part * RELAY + (k + 1) * UNITS, :D]
            at = k // SETS * FULL + k % SETS * ROOM + part * UNITS
            gate_up[at : at + UNITS, :] = units
    gather.local().wait()

    def at_least(i, k):
        return (i + 8 - k) // 8

    def chip_of(i):
        pair = i // 3 - i // 4 + i // 5 - i // 6
        ring = 3 * at_least(i, 1) - 2 * at_least(i, 2) - at_least(i, 3) + 2 * at_least(i, 4)
        ring = ring + at_least(i, 5) - 2 * at_least(i, 6) + at_least(i, 7)
        seat = gather.seat
        return ((seat.ring + ring) % 4) * 2 + (seat.pair + pair) % 2

    @pl.loop(0, 8)
    def _(i):
        for step, when in ((1, 1), (2, 1), (3, 3), (4, 5)):

            @pl.when(i == when)
            def _():
                gather.step(step)

        chip = chip_of(i)
        rows = chunk(chip)
        landed = block_of(hidden, chip * CHUNK + (1 - gather.seat.core) * ROWS, ROWS)
        remote(
            landed,
            landed,
            gather.send_sem.at[8 + i],
            gather.recv_sem.at[8 + i],
            gather.seat.device(gather.seat.index(0, 0, 1)),
        ).wait_recv()
        gates_up[...] = nt(hidden[rows, :], gate_up[...])
        lane = lax.broadcasted_iota(jnp.int32, (CHUNK, ROWS), 1)
        valid = (lane >= PICK_LANE) & (lane < PICK_LANE + EXPERTS)
        logits = jnp.where(valid, gates_up[:, FULL - ROWS : FULL], -1e30)
        top = jnp.max(logits, axis=1, keepdims=True)
        router = jnp.where(valid, jnp.exp(logits - top), 0.0)
        router = router / jnp.sum(router, axis=1, keepdims=True)
        dense_terms[:, :ROWS], dense_terms[:, ROWS:] = two_terms(router * picks[rows, :].astype(f32))
        gates[...] = nn(dense_terms[...], spread[...])

        @pl.loop(0, CHUNK // 32)
        def _(k):
            at = pl.ds(pl.multiple_of(k * 32, 32), 32)
            there = pl.ds(pl.multiple_of(chip * CHUNK + k * 32, 32), 32)
            column = lax.broadcasted_iota(jnp.int32, (32, FULL), 1)
            factor = jnp.where(column < NS * ROOM, 1.0, gates[at, :])
            gate, up, raw_grad = gates_up[at, :FULL], gates_up[at, FULL:], raw[there, :]
            sig = 1.0 / (1.0 + jnp.exp(-gate))
            silu = gate * sig
            act = silu * up
            acts[there, :] = (act.astype(bf16).astype(f32) * factor).astype(bf16)
            reached[at, :FULL], reached[at, FULL:] = two_terms(act * raw_grad)
            act_grad = raw_grad * factor
            wide[there, :FULL] = (act_grad * up * sig * (1.0 + gate * (1.0 - sig))).astype(bf16)
            wide[there, FULL:] = (act_grad * silu).astype(bf16)

        sums[rows, D:] = nn(reached[...], collect[...]).astype(bf16)
        sums[rows, :D] = nn(wide[rows, :], gate_up[...]).astype(bf16)

    def weight_grads(first, last):
        @pl.loop(first, last)
        def _(n):
            @pl.when(n < D // 256 - 1)
            def _():
                fetch_column(n + 1).start()

            @pl.when(n >= 2)
            def _():
                for store in stores(n - 2):
                    store.wait()

            made = tn(wide[...], hidden[:, columns(n)]).astype(bf16)
            made_wide[n % 2, :HALF, :] = made[:HALF]
            made_wide[n % 2, HALF:, :] = made[FULL : FULL + HALF]
            fetch_column(n).wait()
            made_down[n % 2] = tn(acts[...], cot_column[n % 2]).astype(bf16)
            for store in stores(n):
                store.start()

    def outputs(first, last):
        @pl.loop(first, last)
        def _(i):
            @pl.when(i >= 2)
            def _():
                put(i - 2).wait()

            stage[i % 2] = nn(acts[chunk(i), :], down_w[...]).astype(bf16)
            put(i).start()

    scatter.step(0)
    outputs(0, 8)
    scatter.step(1)
    scatter.step(2)
    weight_grads(0, 3)
    scatter.step(3)
    weight_grads(3, 8)
    scatter.step(4)
    for i in (6, 7):
        put(i).wait()
        wait_all(stores(i))
    gather.step(5, shared=False)
    scatter.step(5)


def experts(*arrays):
    any_spec, vmem = pl.BlockSpec(memory_space=pl.ANY), pl.BlockSpec(memory_space=pltpu.VMEM)
    gather, scatter = Gather("dp", ROWS, D), Scatter("dp", ROWS, D + ROWS)
    flops = 2 * GROUP * D * FULL * 9
    return pl.pallas_call(
        expert_kernel,
        name="experts",
        out_shape=[
            jax.ShapeDtypeStruct((ROWS, D + ROWS), f32),
            jax.ShapeDtypeStruct((GROUP, D), bf16),
            jax.ShapeDtypeStruct((2 * HALF, D), bf16),
            jax.ShapeDtypeStruct((FULL, D), bf16),
        ],
        in_specs=[any_spec, any_spec, vmem, any_spec, any_spec, vmem],
        out_specs=[vmem, any_spec, any_spec, any_spec],
        scratch_shapes=[
            pltpu.VMEM((GROUP, D), bf16),
            pltpu.VMEM((2 * FULL, D), bf16),
            pltpu.VMEM((FULL, D), bf16),
            pltpu.VMEM((GROUP, D + ROWS), bf16),
            pltpu.VMEM((2, CHUNK, D), bf16),
            pltpu.VMEM((2, GROUP, 256), bf16),
            pltpu.VMEM((GROUP, FULL), bf16),
            pltpu.VMEM((GROUP, 2 * FULL), bf16),
            pltpu.VMEM((CHUNK, 2 * FULL), f32),
            pltpu.VMEM((GROUP, FULL), f32),
            pltpu.VMEM((CHUNK, FULL), f32),
            pltpu.VMEM((CHUNK, 2 * ROWS), bf16),
            pltpu.VMEM((CHUNK, 2 * FULL), bf16),
            pltpu.VMEM((2 * ROWS, FULL), bf16),
            pltpu.VMEM((2 * FULL, ROWS), bf16),
            pltpu.VMEM((2, 2 * HALF, 256), bf16),
            pltpu.VMEM((2, FULL, 256), bf16),
            pltpu.SemaphoreType.DMA((4,)),
            pltpu.SemaphoreType.DMA((4,)),
            pltpu.SemaphoreType.DMA((4,)),
        ]
        + gather.scratch()
        + scatter.scratch(),
        compiler_params=pltpu.CompilerParams(
            collective_id=2, has_side_effects=True, vmem_limit_bytes=61 * 2**20
        ),
        cost_estimate=pl.CostEstimate(flops=flops, bytes_accessed=40 * 2**20, transcendentals=GROUP * FULL),
    )(*arrays)


def wait_all(copies):
    for copy in copies:
        copy.wait()


def swap_halves(values):
    lane = lax.broadcasted_iota(jnp.int32, values.shape, 1) % ROPE
    return jnp.where(lane < ROPE // 2, pltpu.roll(values, 96, 1), pltpu.roll(values, 32, 1))


def causal(scores):
    rows, seen = scores.shape
    row = lax.broadcasted_iota(jnp.int32, (rows, rows), 0)
    column = lax.broadcasted_iota(jnp.int32, (rows, rows), 1)
    last = jnp.where(column <= row, scores[:, seen - rows :], -1e9)
    return last if seen == rows else jnp.concatenate([scores[:, : seen - rows], last], axis=1)


def attention_ops():
    return (
        Gather("sp", ROWS, D, spare=True),
        Gather("dp", ROWS, PACK),
        Gather("dp", ROWS, D, spare=True),
        Gather("dp", ROWS, D, spare=True),
        Swap(
            "dp",
            (RELAY, D),
            lambda ref, j: ref.at[j],
            lambda ref, j: ref.at[:, pl.ds(pl.multiple_of(j * ROWS, ROWS), ROWS)],
        ),
        Gather("sp", RELAY, D),
        Swap(
            "sp",
            (ROWS, D),
            lambda ref, j: ref.at[pl.ds(pl.multiple_of(j * ROWS, ROWS), ROWS)],
            lambda ref, j: ref.at[:, pl.ds(pl.multiple_of(j * OW, OW), OW)],
        ),
    )


def attention_kernel(
    tokens,
    pack,
    cotangent,
    shared_gate,
    expert_gate,
    shared_up,
    expert_up,
    shared_down,
    expert_down,
    out_own,
    cosine,
    sine,
    resid_two,
    hidden_two,
    cot_all,
    gate_up_part,
    gate_up,
    down_out,
    tok_out,
    weights_out,
    hidden_out,
    compressed_out,
    latent_out,
    query_out,
    key_out,
    value_out,
    head_out,
    out_w_out,
    misc_out,
    total_out,
    tok,
    weights,
    hidden,
    qc,
    latent,
    up_w,
    query,
    key,
    value,
    heads,
    out_w,
    misc_t,
    totals,
    tok_heads,
    pieces,
    down,
    gate_shared,
    gate_routed,
    up_shared,
    up_routed,
    down_shared,
    down_routed,
    save_sem,
    load_sem,
    *rest,
):
    ops = attention_ops()
    tok_op, pack_op, out_op, cot_op, piece_op, gate_up_op, head_op = ops
    bound = (
        (tokens, tok),
        (pack, weights),
        (out_own, out_w),
        (cotangent, cot_all),
        (pieces, gate_up_part),
        (gate_up_part, gate_up),
        (heads, tok_heads),
    )
    for op, (src, dst) in zip(ops, bound):
        count = len(op.scratch())
        op.bind(src, dst, rest[:count])
        rest = rest[count:]
    loads = [
        pltpu.make_async_copy(src, dst, load_sem.at[k])
        for k, (src, dst) in enumerate(
            (
                (shared_gate, gate_shared),
                (expert_gate, gate_routed),
                (shared_up, up_shared),
                (expert_up, up_routed),
                (shared_down, down_shared),
                (expert_down, down_routed),
            )
        )
    ]
    for load in loads:
        load.start()
    meet(ops)
    tok_op.step(0)
    pack_op.step(0)
    for step in (1, 2):
        tok_op.step(step)
        pack_op.step(step)

    wait_all(loads)
    row = lax.broadcasted_iota(jnp.int32, (DP * UNITS, FE), 0)
    column = lax.broadcasted_iota(jnp.int32, (DP * UNITS, FE), 1)
    group, unit = row // UNITS, row - row // UNITS * UNITS + tok_op.seat.own * UNITS
    pick = ((group * SLICE + unit == column) & (unit < SLICE)).astype(bf16)
    for k, (shared, routed) in enumerate(((gate_shared, gate_routed), (up_shared, up_routed))):
        for e in range(SETS):
            piece = shared[:, e, :] if e < NS else routed[:, e - NS, :]
            piece = nt(pick, piece).astype(bf16)
            at = (k * SETS + e) * UNITS
            for d in range(DP):
                pieces[d, at : at + UNITS, :] = piece[d * UNITS : (d + 1) * UNITS]
    piece_op.step(0)
    for e in range(SETS):
        part = down_shared[:, e, :] if e < NS else down_routed[:, e - NS, :]
        down[e * ROOM : e * ROOM + SLICE, :] = part
        down[e * ROOM + SLICE : (e + 1) * ROOM, :] = jnp.zeros((ROOM - SLICE, D), bf16)
    down[HALF:, :] = jnp.zeros((FULL - HALF, D), bf16)
    down_save = pltpu.make_async_copy(down, down_out, load_sem.at[0])
    down_save.start()
    tok_op.step(3)
    pack_op.step(3)
    pack_op.step(4)
    pack_op.step(5)
    out_op.step(0)
    tok_op.local().wait()
    saves = [
        pltpu.make_async_copy(src, dst, save_sem.at[k])
        for k, (src, dst) in enumerate(
            (
                (tok, tok_out),
                (weights, weights_out),
                (hidden, hidden_out),
                (qc.at[:, pl.ds(QW, RANK)], compressed_out),
                (latent, latent_out),
                (query, query_out),
                (key, key_out),
                (value, value_out),
                (heads, head_out),
                (out_w, out_w_out),
                (misc_t, misc_out),
                (totals, total_out),
            )
        )
    ]
    saves[1].start()
    misc_t[...] = weights[:, MISC_AT:CORE_W].astype(f32).T
    up = weights[:, UP_AT:].reshape(DP, 4, RANK // DP, ROWS)
    for k in range(4):
        up_w[:, k * ROWS : (k + 1) * ROWS] = up[:, k].reshape(RANK, ROWS)
    each = RANK // DP
    for d in range(DP):
        misc_t[0:1, d * each : (d + 1) * each] = misc_t[GAIN_KV : GAIN_KV + 1, d * ROWS : d * ROWS + each]
    kv_gain = misc_t[0:1, :RANK]
    saves[10].start()
    gain = misc_t[GAIN_ONE : GAIN_ONE + 1, :]

    def project(*places):
        for place in places:
            start = tok_op.seat.index(*place) * ROWS

            @pl.loop(0, ROWS // 32)
            def _(k):
                at = pl.ds(pl.multiple_of(start + k * 32, 32), 32)
                values = tok[at, :].astype(f32)
                hidden[at, :] = (values * inverse_rms(values) * gain).astype(bf16)

            at = pl.ds(pl.multiple_of(start, ROWS), ROWS)
            qc[at, :] = nn(hidden[at, :], weights[:, :CORE_W])

    project((0, 0), (0, -1), (0, 1), (1, 0), (0, 2))
    tok_op.step(4)
    piece_op.step(5)
    gate_up_op.step(0)
    out_op.step(1)
    out_op.step(2)
    cot_op.step(0)
    project((1, -1), (1, 1), (1, 2))
    tok_op.step(5, shared=False)
    for k in (0, 2, 3):
        saves[k].start()

    @pl.loop(0, SEQ // 256)
    def _(k):
        at = pl.ds(pl.multiple_of(k * 256, 256), 256)
        inner = qc[at, QW : QW + RANK]
        latent[at, :] = (inner * inverse_rms(inner) * kv_gain).astype(bf16)
        ropes, key_rope = qc[at, 2 * NOPE : QW], qc[at, MISC_AT:CORE_W]
        cos, sin = cosine[at, :], sine[at, :]
        ropes = (ropes * cos + swap_halves(ropes) * sin).astype(bf16)
        key_rope = key_rope * cos + swap_halves(key_rope) * sin
        lane = lax.broadcasted_iota(jnp.int32, key_rope.shape, 1)
        key_rope = jnp.where(lane < ROPE, key_rope, 0.0)
        expanded = nn(latent[at, :], up_w[...]).astype(bf16)
        for h in range(HEADS_HERE):
            query[h, at, :NOPE] = qc[at, h * NOPE : (h + 1) * NOPE].astype(bf16)
            query[h, at, NOPE:] = ropes
            turned = key_rope if h == 0 else pltpu.roll(key_rope, ROPE, 1)
            key[h, at, NOPE:] = turned.astype(bf16)
            base = h * (NOPE + VDIM)
            key[h, at, :NOPE] = expanded[:, base : base + NOPE]
            value[h, at, :] = expanded[:, base + NOPE : base + NOPE + VDIM]

    for k in (4, 5, 6, 7):
        saves[k].start()
    out_op.step(3)
    gate_up_op.step(1)
    gate_up_op.step(2)
    for h in range(HEADS_HERE):
        for i in range(SEQ // 256):
            at, seen = pl.ds(i * 256, 256), (i + 1) * 256
            scores = causal(nt(query[h, at, :], key[h, :seen, :]) * SCALE)
            top = jnp.max(scores, axis=1, keepdims=True)
            parts = jnp.exp(scores - top)
            total = jnp.sum(parts, axis=1, keepdims=True)
            probs = (parts * (1.0 / total)).astype(bf16)
            heads[at, h * VDIM : (h + 1) * VDIM] = nn(probs, value[h, :seen, :]).astype(bf16)
            totals[h, at, :] = jnp.broadcast_to(top + jnp.log(total), (256, ROWS))
        if h == 0:
            out_op.step(4)
            cot_op.step(1)
            cot_op.step(2)
    head_op.step(0)
    saves[8].start()
    saves[11].start()
    gate_up_op.step(3)
    out_op.step(5)
    saves[9].start()
    cot_op.step(3)
    gate_up_op.step(4)
    head_op.step(5)
    own = tok_op.view((0, 0))[...].astype(f32)
    resid = own + nn(tok_heads[...], out_w[...])
    resid_two[...] = resid
    hidden_two[...] = (resid * inverse_rms(resid) * misc_t[GAIN_TWO : GAIN_TWO + 1, :]).astype(bf16)
    cot_op.step(4)
    wait_all(saves + [down_save])
    cot_op.step(5)
    gate_up_op.step(5)


def attention(*arrays):
    any_spec, vmem = pl.BlockSpec(memory_space=pl.ANY), pl.BlockSpec(memory_space=pltpu.VMEM)
    kept = [
        ((SEQ, D), bf16),
        ((D, PACK), bf16),
        ((SEQ, D), bf16),
        ((SEQ, RANK), f32),
        ((SEQ, RANK), bf16),
        ((HEADS_HERE, SEQ, 2 * NOPE), bf16),
        ((HEADS_HERE, SEQ, 2 * NOPE), bf16),
        ((HEADS_HERE, SEQ, VDIM), bf16),
        ((SEQ, OW), bf16),
        ((D, D), bf16),
        ((ROWS, D), f32),
        ((HEADS_HERE, SEQ, ROWS), f32),
    ]
    made = [((ROWS, D), f32), ((ROWS, D), bf16), ((GROUP, D), bf16), ((RELAY, D), bf16), ((SP * RELAY, D), bf16), ((FULL, D), bf16)]
    scratch = kept[:3] + [((SEQ, CORE_W), f32), kept[4], ((RANK, KVW), bf16)] + kept[5:]
    scratch = scratch + [((ROWS, D), bf16), ((DP, RELAY, ROWS), bf16), ((FULL, D), bf16)]
    scratch = scratch + [(array.shape, bf16) for array in arrays[3:9]]
    return pl.pallas_call(
        attention_kernel,
        name="attention",
        out_shape=[jax.ShapeDtypeStruct(*shape) for shape in made + kept],
        in_specs=[any_spec] * 10 + [vmem] * 2,
        out_specs=[vmem] * 2 + [any_spec] * (len(made) + len(kept) - 2),
        scratch_shapes=[pltpu.VMEM(*shape) for shape in scratch]
        + [pltpu.SemaphoreType.DMA((len(kept),)), pltpu.SemaphoreType.DMA((6,))]
        + [entry for op in attention_ops() for entry in op.scratch()],
        compiler_params=pltpu.CompilerParams(
            collective_id=0, has_side_effects=True, vmem_limit_bytes=60 * 2**20
        ),
        cost_estimate=pl.CostEstimate(
            flops=2 * SEQ * D * (CORE_W + OW), bytes_accessed=60 * 2**20, transcendentals=SEQ * SEQ
        ),
    )(*arrays)


def attention_grad_ops():
    return (
        Gather("sp", ROWS, D, spare=True),
        Scatter("sp", GU_PART, D, bf16),
        Scatter("sp", DN_PART, D, bf16),
        Swap(
            "sp",
            (D, GRAD_PACK),
            lambda ref, j: ref.at[:, pl.ds(pl.multiple_of(j * OW, OW), OW)],
            lambda ref, j: ref.at[pl.ds(pl.multiple_of(j * OW, OW), OW), pl.ds(CORE_W, OW)],
        ),
        Swap(
            "sp",
            (SEQ, OW),
            lambda ref, j: ref.at[:, pl.ds(pl.multiple_of(j * OW, OW), OW)],
            lambda ref, j: ref.at[pl.ds(pl.multiple_of(j * ROWS, ROWS), ROWS)],
        ),
    )


def attention_grad_kernel(
    proj_own,
    tok_all,
    weights_all,
    hidden_all,
    compressed_all,
    latent_all,
    query_all,
    key_all,
    value_all,
    head_all,
    head_tok,
    misc_all,
    total_all,
    gate_up_all,
    down_all,
    cosine,
    sine,
    norm_rows,
    hidden_part,
    gate_up_sum,
    down_sum,
    grads,
    proj,
    weights,
    hidden,
    compressed,
    latent,
    query,
    key,
    value,
    heads,
    misc_t,
    totals,
    gate_up_grad,
    down_grad,
    up_w,
    out_w_grad,
    head_grad,
    key_grad,
    value_grad,
    rope_grad,
    expanded_grad,
    qc_grad,
    scale_one,
    misc_grad,
    up_grad,
    made_w,
    made_h,
    load_sem,
    out_sem,
    *rest,
):
    ops = attention_grad_ops()
    proj_op, gate_up_op, down_op, out_op, head_op = ops
    bound = (
        (proj_own, proj),
        (gate_up_grad, gate_up_sum),
        (down_grad, down_sum),
        (out_w_grad, grads),
        (head_tok, head_grad),
    )
    for op, (src, dst) in zip(ops, bound):
        count = len(op.scratch())
        op.bind(src, dst, rest[:count])
        rest = rest[count:]
    loads = [
        pltpu.make_async_copy(src, dst, load_sem.at[k])
        for k, (src, dst) in enumerate(
            (
                (head_all, heads),
                (query_all, query),
                (key_all, key),
                (value_all, value),
                (total_all, totals),
                (gate_up_all, gate_up_grad),
                (down_all, down_grad),
                (weights_all, weights),
                (compressed_all, compressed),
                (latent_all, latent),
                (misc_all, misc_t),
                (hidden_all, hidden),
            )
        )
    ]
    tok_load = pltpu.make_async_copy(tok_all, proj, load_sem.at[12])
    for load in loads:
        load.start()
    meet(ops)
    head_op.step(0)
    proj_op.step(0)
    wait_all(loads)
    up = weights[:, UP_AT:].reshape(DP, 4, RANK // DP, ROWS)
    for k in range(4):
        up_w[:, k * ROWS : (k + 1) * ROWS] = up[:, k].reshape(RANK, ROWS)
    head_op.step(5)
    for h in range(HEADS_HERE):
        for i in reversed(range(SEQ // 256)):
            at, seen = pl.ds(i * 256, 256), (i + 1) * 256
            piece = head_grad[at, h * VDIM : (h + 1) * VDIM]
            scores = causal(nt(query[h, at, :], key[h, :seen, :]) * SCALE)
            probs = jnp.exp(scores - totals[h, at, 0:1])
            dprob = nt(piece, value[h, :seen, :])
            delta = jnp.sum(probs * dprob, axis=1, keepdims=True)
            score_grad = (probs * (dprob - delta) * SCALE).astype(bf16)
            query_grad = nn(score_grad, key[h, :seen, :]).astype(bf16)
            qc_grad[at, h * NOPE : (h + 1) * NOPE] = query_grad[:, :NOPE]
            turned = query_grad[:, NOPE:].astype(f32)
            rope_grad[at, :] = turned if h == 0 else rope_grad[at, :] + turned
            from_query = tn(score_grad, query[h, at, :])
            from_out = tn(probs.astype(bf16), piece)
            if i == SEQ // 256 - 1:
                key_grad[h, :seen, :] = from_query
                value_grad[h, :seen, :] = from_out
            else:
                key_grad[h, :seen, :] += from_query
                value_grad[h, :seen, :] += from_out
            if (h, i) == (0, 2):
                proj_op.step(1)
                proj_op.step(2)
        if h == 0:
            proj_op.step(3)
            gate_up_op.step(0)
            down_op.step(0)
    proj_op.step(4)
    proj_op.step(5)
    out_w_grad[...] = tn(heads[...], proj[...]).astype(bf16)
    out_op.step(0)
    tok_load.start()
    gate_up_op.step(1)
    down_op.step(1)
    kv_gain = misc_t[0:1, :RANK]
    lane = lax.broadcasted_iota(jnp.int32, (128, ROWS), 1)

    @pl.loop(0, SEQ // 128)
    def _(k):
        at = pl.ds(pl.multiple_of(k * 128, 128), 128)
        cos, sin = cosine[at, :], sine[at, :]
        ropes = rope_grad[at, :]
        qc_grad[at, 2 * NOPE : QW] = (ropes * cos - swap_halves(ropes) * sin).astype(bf16)
        key_rope = jnp.zeros((128, ROWS), f32)
        for h in range(HEADS_HERE):
            base = h * (NOPE + VDIM)
            expanded_grad[at, base : base + NOPE] = key_grad[h, at, :NOPE].astype(bf16)
            expanded_grad[at, base + NOPE : base + NOPE + VDIM] = value_grad[h, at, :].astype(bf16)
            turned = key_grad[h, at, NOPE:].astype(bf16).astype(f32)
            turned = turned if h == 0 else pltpu.roll(turned, ROPE, 1)
            key_rope = key_rope + jnp.where(lane < ROPE, turned, 0.0)
        key_rope = key_rope * cos - swap_halves(key_rope) * sin
        qc_grad[at, MISC_AT:CORE_W] = jnp.where(lane < ROPE, key_rope, 0.0).astype(bf16)

    gate_up_op.step(2)
    down_op.step(2)
    made = tn(latent[...], expanded_grad[...]).astype(bf16)
    each = RANK // DP
    for d in range(DP):
        for k in range(4):
            at = pl.ds(d * ROWS + k * each, each)
            up_grad[at, :] = made[d * each : (d + 1) * each, k * ROWS : (k + 1) * ROWS]
    up_store = pltpu.make_async_copy(up_grad, grads.at[:, pl.ds(GRAD_UP_AT, ROWS)], out_sem.at[2])
    up_store.start()
    misc_grad[...] = jnp.zeros_like(misc_grad)
    misc_grad[64:72, :] = norm_rows[...]
    kv_total = jnp.zeros((1, RANK), f32)
    for k in range(SEQ // 256):
        at = pl.ds(k * 256, 256)
        inner = compressed[at, :]
        scale = inverse_rms(inner)
        latent_grad = nt(expanded_grad[at, :], up_w[...])
        kv_total = kv_total + jnp.sum(latent_grad * inner * scale, axis=0, keepdims=True)
        qc_grad[at, QW : QW + RANK] = norm_back(inner, scale, kv_gain, latent_grad).astype(bf16)
    for d in range(DP):
        misc_grad[66:67, d * ROWS : d * ROWS + each] = kv_total[:, d * each : (d + 1) * each]
    tok_load.wait()

    @pl.loop(0, SEQ // 32)
    def _(k):
        at = pl.ds(pl.multiple_of(k * 32, 32), 32)
        scale_one[at, :] = inverse_rms(proj[at, :].astype(f32))

    def put(n):
        at = pl.ds(pl.multiple_of(n * TILE, TILE), TILE)
        return pltpu.make_async_copy(made_h.at[n % 2], hidden_part.at[:, at], out_sem.at[n % 2])

    @pl.loop(0, D // TILE)
    def _(n):
        at = pl.ds(pl.multiple_of(n * TILE, TILE), TILE)

        @pl.when(n >= 2)
        def _():
            put(n - 2).wait()

        grad = nt(qc_grad[...], weights[at, :CORE_W])
        made_h[n % 2] = grad.astype(bf16)
        put(n).start()
        grad = grad * proj[:, at].astype(f32) * scale_one[...]
        misc_grad[64:65, at] = jnp.sum(grad, axis=0, keepdims=True)

    put(2).wait()
    put(3).wait()
    gate_up_op.step(3)
    down_op.step(3)

    def store(n):
        at = pl.ds(pl.multiple_of(n * TILE, TILE), TILE)
        return pltpu.make_async_copy(
            made_w.at[n % 2], grads.at[at, pl.ds(0, CORE_W)], out_sem.at[n % 2]
        )

    @pl.loop(0, D // TILE)
    def _(n):
        at = pl.ds(pl.multiple_of(n * TILE, TILE), TILE)

        @pl.when(n >= 2)
        def _():
            store(n - 2).wait()

        made = tn(hidden[:, at], qc_grad[...])
        made_w[n % 2, :, :MISC_AT] = made[:, :MISC_AT].astype(bf16)
        made_w[n % 2, :, MISC_AT:] = (made[:, MISC_AT:] + misc_grad[:, at].T).astype(bf16)
        store(n).start()

    store(2).wait()
    store(3).wait()
    up_store.wait()
    gate_up_op.step(4)
    down_op.step(4)
    out_op.step(5)
    gate_up_op.step(5)
    down_op.step(5)


def attention_grad(*arrays):
    any_spec, vmem = pl.BlockSpec(memory_space=pl.ANY), pl.BlockSpec(memory_space=pltpu.VMEM)
    scratch = [
        ((SEQ, D), bf16),
        ((D, PACK), bf16),
        ((SEQ, D), bf16),
        ((SEQ, RANK), f32),
        ((SEQ, RANK), bf16),
        ((HEADS_HERE, SEQ, 2 * NOPE), bf16),
        ((HEADS_HERE, SEQ, 2 * NOPE), bf16),
        ((HEADS_HERE, SEQ, VDIM), bf16),
        ((SEQ, OW), bf16),
        ((ROWS, D), f32),
        ((HEADS_HERE, SEQ, ROWS), f32),
        ((2 * HALF, D), bf16),
        ((FULL, D), bf16),
        ((RANK, KVW), bf16),
        ((OW, D), bf16),
        ((SEQ, OW), bf16),
        ((HEADS_HERE, SEQ, 2 * NOPE), f32),
        ((HEADS_HERE, SEQ, VDIM), f32),
        ((SEQ, ROWS), f32),
        ((SEQ, KVW), bf16),
        ((SEQ, CORE_W), bf16),
        ((SEQ, 1), f32),
        ((ROWS, D), f32),
        ((D, ROWS), bf16),
        ((2, TILE, CORE_W), bf16),
        ((2, SEQ, TILE), bf16),
    ]
    return pl.pallas_call(
        attention_grad_kernel,
        name="attention_grad",
        out_shape=[
            jax.ShapeDtypeStruct((SEQ, D), bf16),
            jax.ShapeDtypeStruct((GU_PART, D), bf16),
            jax.ShapeDtypeStruct((DN_PART, D), bf16),
            jax.ShapeDtypeStruct((D, GRAD_PACK), bf16),
        ],
        in_specs=[any_spec] * 15 + [vmem] * 3,
        out_specs=[any_spec, vmem, vmem, any_spec],
        scratch_shapes=[pltpu.VMEM(*shape) for shape in scratch]
        + [pltpu.SemaphoreType.DMA((13,)), pltpu.SemaphoreType.DMA((3,))]
        + [entry for op in attention_grad_ops() for entry in op.scratch()],
        compiler_params=pltpu.CompilerParams(
            collective_id=4, has_side_effects=True, vmem_limit_bytes=61 * 2**20
        ),
        cost_estimate=pl.CostEstimate(
            flops=6 * SEQ * D * CORE_W, bytes_accessed=60 * 2**20, transcendentals=SEQ * SEQ
        ),
    )(*arrays)


def per_device(
    tokens,
    cotangent,
    chosen,
    attn_gain,
    w_query,
    w_kv_down,
    kv_gain,
    w_kv_up,
    w_out,
    ffn_gain,
    w_router,
    shared_gate,
    shared_up,
    shared_down,
    expert_gate,
    expert_up,
    expert_down,
):
    own_sp = lax.axis_index("sp")
    picks = jnp.any(chosen[:, :, None] == jnp.arange(EXPERTS, dtype=jnp.int32), axis=1).astype(bf16)
    own_query = lax.dynamic_slice_in_dim(w_query, own_sp * QW, QW, 1)
    own_up = lax.dynamic_slice_in_dim(w_kv_up, own_sp * KVW, KVW, 1)
    pack = jnp.concatenate(
        [
            own_query[:, :NOPE],
            own_query[:, QK : QK + NOPE],
            own_query[:, NOPE:QK],
            own_query[:, QK + NOPE :],
            w_kv_down,
            picks,
            attn_gain[:, None],
            ffn_gain[:, None],
            jnp.pad(kv_gain, (0, ROWS - kv_gain.shape[0]))[:, None],
            jnp.zeros((ROWS, 9), bf16),
            w_router,
            jnp.zeros((ROWS, 44), bf16),
            own_up.reshape(RANK // DP, 4, ROWS).transpose(1, 0, 2).reshape(ROWS, ROWS),
        ],
        axis=1,
    )
    cosine, sine = rope_tables()
    (
        resid_two,
        hidden_two,
        cot_all,
        _,
        gate_up,
        down,
        tok_all,
        weights,
        hidden_one,
        compressed,
        latent,
        queries,
        keys,
        values,
        head_out,
        out_w,
        misc,
        log_totals,
    ) = attention(
        tokens,
        pack,
        cotangent,
        shared_gate,
        expert_gate,
        shared_up,
        expert_up,
        shared_down,
        expert_down,
        w_out,
        cosine,
        sine,
    )
    gain_one, gain_two = misc[GAIN_ONE], misc[GAIN_TWO]
    latent_gain = misc[GAIN_KV].reshape(DP, ROWS)[:, : RANK // DP].reshape(RANK)
    router_t = misc[ROUTER_LANE : ROUTER_LANE + 16].astype(bf16)
    router_w = router_t[:EXPERTS]
    picks_all = weights[:, MISC_AT:CORE_W]
    scale_two = inverse_rms(resid_two)

    hidden_grad, mixed_part, gate_up_grad, down_grad = experts(
        hidden_two, gate_up, router_t, down, cot_all, picks_all
    )
    prob_grad = hidden_grad[:, D + PICK_LANE : D + PICK_LANE + EXPERTS]
    hidden_grad = hidden_grad[:, :D]

    logits = nt(hidden_two, router_w)
    router = jax.nn.softmax(logits, axis=-1)
    prob_grad = prob_grad * picks.astype(f32)
    logit_grad = (
        router * (prob_grad - jnp.sum(router * prob_grad, axis=-1, keepdims=True))
    ).astype(bf16)
    hidden_grad = hidden_grad + nn(logit_grad, router_w)
    router_grad = tn(logit_grad, hidden_two)
    gain_two_grad = jnp.sum(hidden_grad * resid_two * scale_two, axis=0)
    upstream = cotangent.astype(f32)
    resid_two_grad = upstream + norm_back(resid_two, scale_two, gain_two, hidden_grad)
    proj_grad = resid_two_grad.astype(bf16)

    head_tok_grad = nt(proj_grad, out_w).astype(bf16)
    norm_rows = jnp.concatenate(
        [
            jnp.zeros((1, D), f32),
            gain_two_grad[None],
            jnp.zeros((1, D), f32),
            router_grad,
            jnp.zeros((1, D), f32),
        ]
    )
    hidden_one_grad, gate_up_grad, down_grad, grads = attention_grad(
        proj_grad,
        tok_all,
        weights,
        hidden_one,
        compressed,
        latent,
        queries,
        keys,
        values,
        head_out,
        head_tok_grad,
        misc,
        log_totals,
        gate_up_grad,
        down_grad,
        cosine,
        sine,
        norm_rows,
    )

    _, hidden_one_grad, _, gu_total, dn_total, mixed, grads = exchange(
        "sum_grads",
        6,
        [
            Scatter("dp", ROWS, GRAD_PACK, bf16, spare=True),
            Scatter("sp", ROWS, D),
            Swap(
                "dp",
                (DP * GU_PART, ROWS),
                lambda ref, j: ref.at[:, pl.ds(pl.multiple_of(j * ROWS, ROWS), ROWS)],
                lambda ref, j: ref.at[pl.ds(pl.multiple_of(j * GU_PART, GU_PART), GU_PART)],
            ),
            Gather("sp", DP * GU_PART, ROWS),
            Gather("sp", DN_PART, D, spare=True),
            Scatter("dp", ROWS, D, spare=True),
            Gather("sp", ROWS, GRAD_PACK),
        ],
        [grads, hidden_one_grad, gate_up_grad, down_grad, mixed_part],
        plan=[(2, 0), (0, 0), (1, 0), (2, 5), (3, 0), (4, 0)]
        + [(0, 1), (1, 1), (0, 2), (0, 3), (1, 2), (3, 1), (4, 1), (0, 4), (6, 0), (5, 0), (1, 3)]
        + [(3, 2), (4, 2), (5, 1), (1, 4), (3, 3), (4, 3), (6, 1), (6, 2), (5, 2), (5, 3)]
        + [(3, 4), (4, 4), (6, 3), (5, 4), (6, 4)]
        + [(op, 5) for op in (0, 1, 3, 4, 5, 6)],
        chained=[(3, 2), (6, 0)],
    )
    gu_total = gu_total.reshape(SP, DP, GU_PART, ROWS)
    grads = grads.reshape(SP, ROWS, GRAD_PACK)
    mixed = (resid_two + mixed).astype(bf16)
    resid_one = tokens.astype(f32)
    own_scale = inverse_rms(resid_one)
    tokens_grad = resid_two_grad + norm_back(resid_one, own_scale, gain_one, hidden_one_grad)
    tokens_grad = tokens_grad.astype(bf16)

    def side_by_side(block, width):
        return block.astype(f32).transpose(1, 0, 2).reshape(-1, SP * width)

    query_total = grads[:, :, :QW]
    query_total = jnp.concatenate(
        [
            query_total[:, :, :NOPE],
            query_total[:, :, 2 * NOPE : 2 * NOPE + ROPE],
            query_total[:, :, NOPE : 2 * NOPE],
            query_total[:, :, 2 * NOPE + ROPE :],
        ],
        axis=2,
    )
    query_total = side_by_side(query_total, QW)
    tail = jnp.sum(grads[:, :, QW:CORE_W].astype(f32), axis=0)
    down_total, tail = tail[:, : RANK + ROPE], tail[:, RANK + ROPE :]
    out_total = side_by_side(grads[:, :, CORE_W:GRAD_UP_AT], OW)
    up_total = grads[:, :, GRAD_UP_AT:].reshape(SP, 4, RANK // DP, ROWS).transpose(0, 2, 1, 3)
    up_total = side_by_side(up_total.reshape(SP, RANK // DP, KVW), KVW)

    gu_total = gu_total.transpose(0, 2, 1, 3).reshape(2, SETS, ROOM, DP, ROWS)[:, :, :SLICE]
    gu_total = gu_total.transpose(0, 4, 1, 3, 2).reshape(2, ROWS, SETS, FE).astype(f32)
    dn_total = dn_total[:HALF].reshape(SETS, ROOM, D)[:, :SLICE].transpose(1, 0, 2).astype(f32)
    return (
        mixed,
        tokens_grad,
        tail[:, 0],
        query_total,
        down_total,
        tail[: RANK // DP, 2],
        up_total,
        out_total,
        tail[:, 1],
        tail[:, 3:7],
        gu_total[0, :, :NS],
        gu_total[1, :, :NS],
        dn_total[:, :NS],
        gu_total[0, :, NS:],
        gu_total[1, :, NS:],
        dn_total[:, NS:],
    )


def solution(mesh):
    rows = P(("dp", "sp"), None)
    vec, mat, cube = P("dp"), P("dp", None), P("dp", None, None)
    return jax.shard_map(
        per_device,
        mesh=mesh,
        in_specs=(rows, rows, rows, vec, mat, mat, vec, mat, mat, vec, mat) + (cube,) * 6,
        out_specs=(rows, rows, vec, mat, mat, vec, mat, mat, vec, mat) + (cube,) * 6,
        check_vma=False,
    )
```

```python
import functools

import jax
import jax.numpy as jnp
import numpy as np
from jax import lax
from jax.experimental import pallas as pl
from jax.experimental.pallas import tpu as pltpu
from jax.sharding import PartitionSpec as P

D = 2048
HEADS = 16
NOPE = 128
ROPE = 64
QK = NOPE + ROPE
VDIM = 128
RANK = 512
FE = 1408
NS = 2
EXPERTS = 4
TOP = 2
SETS = NS + EXPERTS
DP = 16
SP = 8
ROWS = 128
SEQ = SP * ROWS
GROUP = DP * ROWS
HEADS_HERE = HEADS // SP
QW = HEADS_HERE * QK
KVW = HEADS_HERE * (NOPE + VDIM)
OW = HEADS_HERE * VDIM
SLICE = FE // DP
CORE_W = 1024
UP_AT = CORE_W
MISC_AT = CORE_W - ROWS
PICK_LANE, GAIN_ONE, GAIN_TWO, GAIN_KV, ROUTER_LANE = 64, 68, 69, 70, 80
ROOM = 96
HALF = SETS * ROOM
FULL = 640
CHUNK = 2 * ROWS
TILE = 512
SCALE = QK ** (-0.5)
PACK = QW + RANK + ROPE + ROPE + ROWS
GU_PART = 2 * HALF // SP
RELAY = 2 * HALF // SP
UNITS = ROOM // SP
DN_PART = FULL // SP

epsilon = 1e-06
bf16 = jnp.bfloat16
f32 = jnp.float32


def mm(left, right, dims):
    return lax.dot_general(left, right, ((dims[0], dims[1]), ((), ())), preferred_element_type=f32)


def nn(left, right):
    return mm(left, right, ((1,), (0,)))


def nt(left, right):
    return mm(left, right, ((1,), (1,)))


def tn(left, right):
    return mm(left, right, ((0,), (0,)))


def rope_tables():
    inverse = 10000.0 ** (-np.arange(ROPE // 2, dtype=np.float64) * 2.0 / ROPE)
    angles = np.arange(SEQ, dtype=np.float64)[:, None] * inverse[None, :]
    cosine, sine = np.cos(angles), np.sin(angles)
    cosine = np.concatenate([cosine] * 4, axis=1)
    sine = np.concatenate([-sine, sine] * 2, axis=1)
    return jnp.asarray(cosine, f32), jnp.asarray(sine, f32)


def norm_back(values, scale, gain, grad):
    scaled = gain * grad
    total = jnp.sum(scaled * values, axis=-1, keepdims=True) / values.shape[-1]
    return scale * scaled - values * (scale * scale * scale) * total


def inverse_rms(values):
    return lax.rsqrt(jnp.mean(values * values, axis=-1, keepdims=True) + epsilon)


class Seat:
    def __init__(self, axis):
        own_dp, own_sp = lax.axis_index("dp"), lax.axis_index("sp")
        self.axis = axis
        if axis == "sp":
            self.pair, self.ring, self.core, self.cores = own_sp // 4, own_sp % 4, 0, 1
            self.own, self.size = own_sp, SP
            self.device = lambda index: (own_dp, index)
        else:
            self.ring, self.pair, self.core, self.cores = own_dp // 4, (own_dp // 2) % 2, own_dp % 2, 2
            self.own, self.size = own_dp, DP
            self.device = lambda index: (index, own_sp)

    def index(self, pair, ring, core=0):
        pair, ring = (self.pair + pair) % 2, (self.ring + ring) % 4
        if self.axis == "sp":
            return pair * 4 + ring
        return (ring * 2 + pair) * 2 + (self.core + core) % 2


def remote(src, dst, send_sem, recv_sem, device):
    return pltpu.make_async_remote_copy(
        src_ref=src,
        dst_ref=dst,
        send_sem=send_sem,
        recv_sem=recv_sem,
        device_id=device,
        device_id_type=pl.DeviceIdType.MESH,
    )


def block_of(ref, start, size):
    return ref.at[pl.ds(pl.multiple_of(start, 16), size)]


def middle(rows):
    return (rows // 2 + 15) // 16 * 16


NEAR = ((0, 1), (0, -1), (1, 0))
SHARE = ((0, 0), (0, -1), (0, 1), (1, 0), (0, 2), (1, -1), (1, 1), (1, 2))
ORDER = ((1, 2), (1, 1), (1, -1), (0, 2), (1, 0), (0, 1), (0, -1), (0, 0))


class Gather:
    def __init__(self, axis, rows, width, spare=False):
        self.axis, self.rows, self.width, self.spare = axis, rows, width, spare
        self.count = SP if axis == "sp" else DP

    def in_spec(self):
        return pl.BlockSpec(memory_space=pl.ANY)

    def out(self):
        return (
            jax.ShapeDtypeStruct((self.count * self.rows, self.width), bf16),
            pl.BlockSpec(memory_space=pl.ANY),
        )

    def scratch(self):
        return [pltpu.SemaphoreType.DMA((17,)), pltpu.SemaphoreType.DMA((17,)), pltpu.SemaphoreType.DMA]

    def partners(self, seat):
        near = [seat.index(*n) for n in NEAR]
        return near + ([seat.index(0, 0, 1)] if seat.cores == 2 else [])

    def bind(self, src, out, scratch):
        self.src, self.dst = src, out
        self.send_sem, self.recv_sem, self.local_sem = scratch
        self.seat = Seat(self.axis)

    def view(self, place, half=None):
        start = self.seat.index(*place) * self.rows
        if half is None:
            return block_of(self.dst, start, self.rows)
        cut = middle(self.rows)
        return block_of(self.dst, start + half * cut, (cut, self.rows - cut)[half])

    def table(self, number):
        if number in (0, 1, 2, 8):
            return self.src, self.view((0, 0)), {0: (0, 1), 1: (0, -1), 2: (1, 0), 8: (0, 0, 1)}[number]
        if 8 <= number < 16:
            here = self.view(SHARE[number - 8])
            return here, here, (0, 0, 1)
        place, half, to = {
            7: ((1, -1), 0, (0, 1)),
            16: ((1, 1), 1, (0, -1)),
        }[number] if self.spare and number in (7, 16) else {
            3: ((0, -1), 0, (0, 1)),
            4: ((0, 1), 1, (0, -1)),
            5: ((1, 0), None, (0, 1)),
            6: ((1, 0), None, (0, -1)),
            7: ((0, 2), None, (1, 0)),
        }[number]
        here = self.view(place, half)
        return here, here, to

    def copy(self, number):
        src, dst, to = self.table(number)
        return remote(
            src,
            dst,
            self.send_sem.at[number],
            self.recv_sem.at[number],
            self.seat.device(self.seat.index(*to)),
        )

    def go(self, *numbers):
        for number in numbers:
            self.copy(number).start()

    def share(self, *numbers):
        if self.seat.cores == 2:
            self.go(*[8 + number for number in numbers])

    def arrived(self, *numbers):
        for number in numbers:
            self.copy(number).wait_recv()

    def local(self):
        return pltpu.make_async_copy(self.src, self.view((0, 0)), self.local_sem)

    def step(self, number, shared=True):
        if number == 0:
            self.local().start()
            self.go(0, 1, 2)
            self.share(0)
        elif number == 1:
            self.arrived(0, 1)
            self.go(3, 4)
            self.share(1, 2)
        elif number == 2:
            self.arrived(2)
            self.go(5, 6)
            self.share(3)
        elif number == 3:
            self.arrived(3, 4)
            if not self.spare:
                self.go(7)
            self.share(4)
        elif number == 4:
            self.arrived(5, 6)
            if self.spare:
                self.go(7, 16)
                self.share(5, 6)
                self.arrived(7, 16)
                self.share(7)
            else:
                self.arrived(7)
                self.share(5, 6, 7)
        else:
            numbers = list(range(8)) + [16] * self.spare
            if self.seat.cores == 2:
                numbers = numbers + list(range(8, 16))
                if shared:
                    self.arrived(*range(8, 16))
            for number in numbers:
                self.copy(number).wait_send()
            if shared:
                self.local().wait()


class Scatter:
    def __init__(self, axis, rows, width, kind=f32, spare=False):
        self.axis, self.rows, self.width, self.kind, self.spare = axis, rows, width, kind, spare
        self.count = SP if axis == "sp" else DP

    def in_spec(self):
        return pl.BlockSpec(memory_space=pltpu.VMEM)

    def out(self):
        return (
            jax.ShapeDtypeStruct((self.rows, self.width), self.kind),
            pl.BlockSpec(memory_space=pltpu.VMEM),
        )

    def scratch(self):
        block, cut = (self.rows, self.width), middle(self.rows)
        first, second = (cut, self.width), (self.rows - cut, self.width)
        shapes = [block, block, block, first, second, block, block, block]
        shapes = shapes + [(8 if self.axis == "dp" else 5,) + block]
        return [pltpu.SemaphoreType.DMA((17,)), pltpu.SemaphoreType.DMA((17,))] + [
            pltpu.VMEM(shape, bf16) for shape in shapes
        ]

    partners = Gather.partners
    copy = Gather.copy
    go = Gather.go
    arrived = Gather.arrived

    def sizes(self):
        rows, cut = self.rows, middle(self.rows)
        return [rows] * 3 + [cut, rows - cut] + [rows] * 3

    def bind(self, src, out, scratch):
        self.src, self.dst = src, out
        self.send_sem, self.recv_sem = scratch[:2]
        self.got, self.made = scratch[2:10], scratch[10]
        self.seat = Seat(self.axis)

    def given(self, *place):
        return block_of(self.src, self.seat.index(*place) * self.rows, self.rows)

    def slot(self, place):
        if self.axis == "dp":
            return self.made.at[ORDER.index(place)]
        kept = ((1, 0), (0, 1), (0, -1)) + (((1, 1), (1, -1)) if self.spare else ((0, 2),))
        k = kept.index(place)
        return self.made[k] if isinstance(self.made, list) else self.made.at[k]

    def part(self, place):
        return self.slot(place) if self.axis == "dp" else self.given(*place)

    def ready(self, *places):
        if self.axis == "dp":
            for place in places:
                self.arrived(8 + ORDER.index(place))
                self.add(self.slot(place), [self.slot(place), self.given(*place)])

    def add(self, dst, terms):
        rows = dst.shape[0]
        step = 16

        @pl.loop(0, rows // step)
        def _(i):
            at = pl.ds(pl.multiple_of(i * step, step), step)
            total = terms[0][at, :].astype(f32)
            for term in terms[1:]:
                total = total + term[at, :].astype(f32)
            dst[at, :] = total.astype(dst.dtype)

    def add_half(self, place, half, term):
        made, part = self.halves(self.slot(place)), self.halves(self.part(place))
        self.add(made[half], [part[half], term])
        if self.axis == "sp":
            self.add(made[1 - half], [part[1 - half]])

    def halves(self, ref):
        cut = middle(self.rows)
        return ref.at[pl.ds(0, cut)], ref.at[pl.ds(cut, self.rows - cut)]

    def table(self, number):
        if 8 <= number < 16:
            return self.given(*ORDER[number - 8], 1), self.made.at[number - 8], (0, 0, 1)
        if self.spare and number in (0, 1, 2, 3, 4, 16):
            if number in (1, 2):
                return self.slot((1, 3 - 2 * number)), self.got[number], (0, 3 - 2 * number)
            half = 0 if number in (0, 3) else 1
            src = self.halves(self.part((1, 2) if number in (0, 16) else (0, 2)))[half]
            dst = self.halves(self.got[0])[half] if number in (0, 16) else self.got[number]
            return src, dst, (0, 1 - 2 * half)
        src, to = {
            0: (lambda: self.part((1, 2)), (1, 0)),
            1: (lambda: self.part((1, 1)), (0, 1)),
            2: (lambda: self.part((1, -1)), (0, -1)),
            3: (lambda: self.halves(self.slot((0, 2)))[0], (0, 1)),
            4: (lambda: self.halves(self.slot((0, 2)))[1], (0, -1)),
            5: (lambda: self.slot((1, 0)), (1, 0)),
            6: (lambda: self.slot((0, 1)), (0, 1)),
            7: (lambda: self.slot((0, -1)), (0, -1)),
        }[number]
        return src(), self.got[number], to

    def step(self, number):
        if number == 0:
            if self.axis == "dp":
                self.go(*range(8, 16))
            self.ready((1, 2))
            if self.spare:
                self.go(0, 16)
                self.ready((0, 2))
                self.go(3, 4)
                self.ready((1, 1), (1, -1))
                return
            self.go(0)
            self.ready((1, 1))
            self.go(1)
            self.ready((1, -1))
            self.go(2)
        elif number == 1 and self.spare:
            self.arrived(0, 16)
            for place, half in (((1, 1), 0), ((1, -1), 1)):
                self.add_half(place, half, self.halves(self.got[0])[half])
                self.go(1 + half)
        elif number == 1:
            self.ready((0, 2))
            self.arrived(0)
            self.add(self.slot((0, 2)), [self.part((0, 2)), self.got[0]])
            self.go(3, 4)
        elif number == 2:
            self.ready((1, 0))
            self.arrived(1, 2)
            self.add(self.slot((1, 0)), [self.part((1, 0)), self.got[1], self.got[2]])
            self.go(5)
        elif number == 3:
            self.ready((0, 1), (0, -1))
            self.arrived(3, 4)
            for place, half in (((0, 1), 0), ((0, -1), 1)):
                self.add_half(place, half, self.got[3 + half])
                self.go(6 + half)
        elif number == 4:
            self.ready((0, 0))
            self.arrived(5, 6, 7)
            self.add(self.dst, [self.part((0, 0)), self.got[5], self.got[6], self.got[7]])
        else:
            numbers = list(range(16 if self.axis == "dp" else 8)) + [16] * self.spare
            for number in numbers:
                self.copy(number).wait_send()


class Swap:
    def __init__(self, axis, shape, take, put, kind="any"):
        self.axis, self.shape, self.take, self.put = axis, shape, take, put
        self.count = SP if axis == "sp" else DP

    def in_spec(self):
        return pl.BlockSpec(memory_space=pl.ANY)

    def out(self):
        return jax.ShapeDtypeStruct(self.shape, bf16), pl.BlockSpec(memory_space=pl.ANY)

    def scratch(self):
        sems = pltpu.SemaphoreType.DMA((self.count,))
        return [sems, sems, pltpu.SemaphoreType.DMA]

    def partners(self, seat):
        return [(seat.own + k) % seat.size for k in range(1, seat.size)]

    def bind(self, src, out, scratch):
        self.src, self.dst = src, out
        self.send_sem, self.recv_sem, self.local_sem = scratch
        self.seat = Seat(self.axis)

    def copy(self, k):
        to = (self.seat.own + k) % self.seat.size
        return remote(
            self.take(self.src, to),
            self.put(self.dst, self.seat.own),
            self.send_sem.at[k],
            self.recv_sem.at[k],
            self.seat.device(to),
        )

    def local(self):
        own = self.seat.own
        return pltpu.make_async_copy(self.take(self.src, own), self.put(self.dst, own), self.local_sem)

    def step(self, number):
        if number == 0:
            self.local().start()

            @pl.loop(1, self.seat.size)
            def _(k):
                self.copy(k).start()

        elif number == 5:

            @pl.loop(1, self.seat.size)
            def _(k):
                self.copy(k).wait_recv()
                self.copy(k).wait_send()

            self.local().wait()


def meet(ops):
    barrier = pltpu.get_barrier_semaphore()
    total = 0
    for axis in ("sp", "dp"):
        mine = [op for op in ops if op.axis == axis]
        if not mine:
            continue
        seat = Seat(axis)
        widest = max(mine, key=lambda op: len(op.partners(seat)))
        for partner in widest.partners(seat):
            pl.semaphore_signal(
                barrier, inc=1, device_id=seat.device(partner), device_id_type=pl.DeviceIdType.MESH
            )
            total += 1
    pl.semaphore_wait(barrier, total)


def exchange(name, number, ops, arrays, plan=None, chained=()):
    chained = dict(chained)
    plan = plan or [(op, step) for step in range(6) for op in range(len(ops))]
    counts = [len(op.scratch()) for op in ops]
    inputs = [k for k in range(len(ops)) if k not in chained]

    def body(*refs):
        given = dict(zip(inputs, refs[: len(inputs)]))
        outs = refs[len(inputs) : len(inputs) + len(ops)]
        rest = refs[len(inputs) + len(ops) :]
        for k, op in enumerate(ops):
            op.bind(given[k] if k in given else outs[chained[k]], outs[k], rest[: counts[k]])
            rest = rest[counts[k] :]
        meet(ops)
        for op, step in plan:
            ops[op].step(step)

    outs = [op.out() for op in ops]
    return pl.pallas_call(
        body,
        name=name,
        out_shape=[shape for shape, _ in outs],
        in_specs=[ops[k].in_spec() for k in inputs],
        out_specs=[spec for _, spec in outs],
        scratch_shapes=[entry for op in ops for entry in op.scratch()],
        compiler_params=pltpu.CompilerParams(
            collective_id=number, has_side_effects=True, vmem_limit_bytes=56 * 2**20
        ),
    )(*arrays)


def expert_of(column):
    lane = jnp.zeros(column.shape, jnp.int32)
    for e in range(EXPERTS):
        low = (NS + e) * ROOM
        lane = jnp.where((column >= low) & (column < low + ROOM), PICK_LANE + e, lane)
    return lane


def two_terms(values):
    high = values.astype(bf16)
    return high, (values - high.astype(f32)).astype(bf16)


def expert_kernel(
    hidden_own,
    weights,
    router_t,
    down,
    cot_all,
    picks,
    sum_out,
    mixed_out,
    gate_up_sum,
    down_sum,
    hidden,
    gate_up,
    down_w,
    sums,
    stage,
    cot_column,
    acts,
    wide,
    gates_up,
    raw,
    gates,
    dense_terms,
    reached,
    spread,
    collect,
    running,
    load_sem,
    in_sem,
    turn_sem,
    gate_up_sems,
    down_sems,
    *rest,
):
    gather, scatter = Gather("dp", ROWS, D), Scatter("dp", ROWS, D + ROWS)
    gather.bind(hidden_own, hidden, rest[:3])
    scatter.bind(sums, sum_out, rest[3:])
    gate_up_op, down_op = Scatter("sp", GU_PART, D, bf16), Scatter("sp", DN_PART, D, bf16)
    views, at = [], 0
    for size in gate_up_op.sizes() + down_op.sizes() + [DN_PART] * 4:
        views.append(hidden.at[pl.ds(at, size)])
        at += size
    gate_up_op.bind(gate_up, gate_up_sum, [gate_up_sems.at[0], gate_up_sems.at[1], *views[:8], running])
    down_op.bind(down_w, down_sum, [down_sems.at[0], down_sems.at[1], *views[8:16], views[16:]])
    loads = [
        pltpu.make_async_copy(down, down_w, load_sem.at[2]),
        pltpu.make_async_copy(weights, sums.at[pl.ds(0, 2 * HALF), pl.ds(0, D)], load_sem.at[0]),
    ]
    for load in loads:
        load.start()

    def chunk(i):
        return pl.ds(pl.multiple_of(i * CHUNK, CHUNK), CHUNK)

    def columns(n):
        return pl.ds(pl.multiple_of(n * 256, 256), 256)

    def fetch(i):
        return pltpu.make_async_copy(cot_all.at[chunk(i)], stage.at[i % 2], in_sem.at[i % 2])

    def put(i):
        return pltpu.make_async_copy(stage.at[i % 2], mixed_out.at[chunk(i)], in_sem.at[i % 2])

    def fetch_column(n):
        return pltpu.make_async_copy(cot_all.at[:, columns(n)], cot_column.at[n % 2], in_sem.at[2 + n % 2])

    fetch(0).start()
    fetch_column(0).start()
    meet([gather, gate_up_op])
    gather.step(0)
    gate_up[pl.ds(HALF, 16), :] = router_t[...]
    gate_up[pl.ds(HALF + 16, FULL - HALF - 16), :] = jnp.zeros((FULL - HALF - 16, D), bf16)
    gate_up[pl.ds(FULL + HALF, FULL - HALF), :] = jnp.zeros((FULL - HALF, D), bf16)
    row = lax.broadcasted_iota(jnp.int32, (ROWS, FULL), 0)
    lane_of = expert_of(lax.broadcasted_iota(jnp.int32, (ROWS, FULL), 1))
    hot = (row == lane_of).astype(bf16)
    spread[:ROWS, :] = hot
    spread[ROWS:, :] = hot
    lane = lax.broadcasted_iota(jnp.int32, (FULL, ROWS), 1)
    hot = (lane == expert_of(lax.broadcasted_iota(jnp.int32, (FULL, ROWS), 0))).astype(bf16)
    collect[:FULL, :] = hot
    collect[FULL:, :] = hot
    loads[0].wait()

    @pl.loop(0, 8)
    def _(i):
        @pl.when(i < 7)
        def _():
            fetch(i + 1).start()

        fetch(i).wait()
        raw[chunk(i), :] = nt(stage[i % 2], down_w[...])

    loads[1].wait()
    for k in range(2 * SETS):
        for part in range(SP):
            units = sums[part * RELAY + k * UNITS : part * RELAY + (k + 1) * UNITS, :D]
            at = k // SETS * FULL + k % SETS * ROOM + part * UNITS
            gate_up[at : at + UNITS, :] = units
    gather.local().wait()

    def at_least(i, k):
        return (i + 8 - k) // 8

    def chip_of(i):
        pair = i // 3 - i // 4 + i // 5 - i // 6
        ring = 3 * at_least(i, 1) - 2 * at_least(i, 2) - at_least(i, 3) + 2 * at_least(i, 4)
        ring = ring + at_least(i, 5) - 2 * at_least(i, 6) + at_least(i, 7)
        seat = gather.seat
        return ((seat.ring + ring) % 4) * 2 + (seat.pair + pair) % 2

    @pl.loop(0, 8)
    def _(i):
        for step, when in ((1, 1), (2, 1), (3, 3), (4, 5)):

            @pl.when(i == when)
            def _():
                gather.step(step)

        chip = chip_of(i)
        rows = chunk(chip)
        landed = block_of(hidden, chip * CHUNK + (1 - gather.seat.core) * ROWS, ROWS)
        remote(
            landed,
            landed,
            gather.send_sem.at[8 + i],
            gather.recv_sem.at[8 + i],
            gather.seat.device(gather.seat.index(0, 0, 1)),
        ).wait_recv()
        gates_up[...] = nt(hidden[rows, :], gate_up[...])
        lane = lax.broadcasted_iota(jnp.int32, (CHUNK, ROWS), 1)
        valid = (lane >= PICK_LANE) & (lane < PICK_LANE + EXPERTS)
        logits = jnp.where(valid, gates_up[:, FULL - ROWS : FULL], -1e30)
        top = jnp.max(logits, axis=1, keepdims=True)
        router = jnp.where(valid, jnp.exp(logits - top), 0.0)
        router = router / jnp.sum(router, axis=1, keepdims=True)
        dense_terms[:, :ROWS], dense_terms[:, ROWS:] = two_terms(router * picks[rows, :].astype(f32))
        gates[...] = nn(dense_terms[...], spread[...])

        @pl.loop(0, CHUNK // 32)
        def _(k):
            at = pl.ds(pl.multiple_of(k * 32, 32), 32)
            there = pl.ds(pl.multiple_of(chip * CHUNK + k * 32, 32), 32)
            column = lax.broadcasted_iota(jnp.int32, (32, FULL), 1)
            factor = jnp.where(column < NS * ROOM, 1.0, gates[at, :])
            gate, up, raw_grad = gates_up[at, :FULL], gates_up[at, FULL:], raw[there, :]
            sig = 1.0 / (1.0 + jnp.exp(-gate))
            silu = gate * sig
            act = silu * up
            acts[there, :] = (act.astype(bf16).astype(f32) * factor).astype(bf16)
            reached[at, :FULL], reached[at, FULL:] = two_terms(act * raw_grad)
            act_grad = raw_grad * factor
            wide[there, :FULL] = (act_grad * up * sig * (1.0 + gate * (1.0 - sig))).astype(bf16)
            wide[there, FULL:] = (act_grad * silu).astype(bf16)

        sums[rows, D:] = nn(reached[...], collect[...]).astype(bf16)
        sums[rows, :D] = nn(wide[rows, :], gate_up[...]).astype(bf16)

    def gate_up_grads(first, last):
        @pl.loop(first, last)
        def _(n):
            made = tn(wide[...], hidden[:, columns(n)]).astype(bf16)
            gate_up[:HALF, columns(n)] = made[:HALF]
            gate_up[HALF : 2 * HALF, columns(n)] = made[FULL : FULL + HALF]

    def down_grads(first, last):
        @pl.loop(first, last)
        def _(n):
            @pl.when(n < D // 256 - 1)
            def _():
                fetch_column(n + 1).start()

            fetch_column(n).wait()
            down_w[:, columns(n)] = tn(acts[...], cot_column[n % 2]).astype(bf16)

    def outputs(first, last):
        @pl.loop(first, last)
        def _(i):
            @pl.when(i >= 2)
            def _():
                put(i - 2).wait()

            stage[i % 2] = nn(acts[chunk(i), :], down_w[...]).astype(bf16)
            put(i).start()

    scatter.step(0)
    gate_up_grads(0, 6)
    scatter.step(1)
    gate_up_grads(6, 8)
    gather.step(5, shared=False)
    seat = gate_up_op.seat
    for partner in gate_up_op.partners(seat):
        pl.semaphore_signal(
            turn_sem, inc=1, device_id=seat.device(partner), device_id_type=pl.DeviceIdType.MESH
        )
    scatter.step(2)
    outputs(0, 4)
    scatter.step(3)
    pl.semaphore_wait(turn_sem, len(NEAR))
    gate_up_op.step(0)
    outputs(4, 8)
    put(6).wait()
    put(7).wait()
    down_grads(0, 8)
    down_op.step(0)
    gate_up_op.step(1)
    scatter.step(4)
    for step in (2, 3):
        gate_up_op.step(step)
        down_op.step(step - 1)
    down_op.step(3)
    gate_up_op.step(4)
    down_op.step(4)
    gate_up_op.step(5)
    down_op.step(5)
    scatter.step(5)


def experts(*arrays):
    any_spec, vmem = pl.BlockSpec(memory_space=pl.ANY), pl.BlockSpec(memory_space=pltpu.VMEM)
    gather, scatter = Gather("dp", ROWS, D), Scatter("dp", ROWS, D + ROWS)
    flops = 2 * GROUP * D * FULL * 9
    return pl.pallas_call(
        expert_kernel,
        name="experts",
        out_shape=[
            jax.ShapeDtypeStruct((ROWS, D + ROWS), f32),
            jax.ShapeDtypeStruct((GROUP, D), bf16),
            jax.ShapeDtypeStruct((GU_PART, D), bf16),
            jax.ShapeDtypeStruct((DN_PART, D), bf16),
        ],
        in_specs=[any_spec, any_spec, vmem, any_spec, any_spec, vmem],
        out_specs=[vmem, any_spec, vmem, vmem],
        scratch_shapes=[
            pltpu.VMEM((GROUP, D), bf16),
            pltpu.VMEM((2 * FULL, D), bf16),
            pltpu.VMEM((FULL, D), bf16),
            pltpu.VMEM((GROUP, D + ROWS), bf16),
            pltpu.VMEM((2, CHUNK, D), bf16),
            pltpu.VMEM((2, GROUP, 256), bf16),
            pltpu.VMEM((GROUP, FULL), bf16),
            pltpu.VMEM((GROUP, 2 * FULL), bf16),
            pltpu.VMEM((CHUNK, 2 * FULL), f32),
            pltpu.VMEM((GROUP, FULL), f32),
            pltpu.VMEM((CHUNK, FULL), f32),
            pltpu.VMEM((CHUNK, 2 * ROWS), bf16),
            pltpu.VMEM((CHUNK, 2 * FULL), bf16),
            pltpu.VMEM((2 * ROWS, FULL), bf16),
            pltpu.VMEM((2 * FULL, ROWS), bf16),
            pltpu.VMEM((4, GU_PART, D), bf16),
            pltpu.SemaphoreType.DMA((3,)),
            pltpu.SemaphoreType.DMA((4,)),
            pltpu.SemaphoreType.REGULAR,
            pltpu.SemaphoreType.DMA((2, 17)),
            pltpu.SemaphoreType.DMA((2, 17)),
        ]
        + gather.scratch()
        + scatter.scratch(),
        compiler_params=pltpu.CompilerParams(
            collective_id=2, has_side_effects=True, vmem_limit_bytes=61 * 2**20
        ),
        cost_estimate=pl.CostEstimate(flops=flops, bytes_accessed=40 * 2**20, transcendentals=GROUP * FULL),
    )(*arrays)


def wait_all(copies):
    for copy in copies:
        copy.wait()


def swap_halves(values):
    lane = lax.broadcasted_iota(jnp.int32, values.shape, 1) % ROPE
    return jnp.where(lane < ROPE // 2, pltpu.roll(values, 96, 1), pltpu.roll(values, 32, 1))


def causal(scores):
    rows, seen = scores.shape
    row = lax.broadcasted_iota(jnp.int32, (rows, rows), 0)
    column = lax.broadcasted_iota(jnp.int32, (rows, rows), 1)
    last = jnp.where(column <= row, scores[:, seen - rows :], -1e9)
    return last if seen == rows else jnp.concatenate([scores[:, : seen - rows], last], axis=1)


def attention_ops():
    return (
        Gather("sp", ROWS, D, spare=True),
        Gather("dp", ROWS, PACK),
        Gather("dp", ROWS, D, spare=True),
        Gather("dp", ROWS, D, spare=True),
        Swap(
            "dp",
            (RELAY, D),
            lambda ref, j: ref.at[j],
            lambda ref, j: ref.at[:, pl.ds(pl.multiple_of(j * ROWS, ROWS), ROWS)],
        ),
        Gather("sp", RELAY, D),
        Swap(
            "sp",
            (ROWS, D),
            lambda ref, j: ref.at[pl.ds(pl.multiple_of(j * ROWS, ROWS), ROWS)],
            lambda ref, j: ref.at[:, pl.ds(pl.multiple_of(j * OW, OW), OW)],
        ),
    )


def attention_kernel(
    tokens,
    pack,
    cotangent,
    shared_gate,
    expert_gate,
    shared_up,
    expert_up,
    shared_down,
    expert_down,
    out_own,
    cosine,
    sine,
    resid_two,
    hidden_two,
    cot_all,
    gate_up_part,
    gate_up,
    down_out,
    tok_out,
    weights_out,
    hidden_out,
    compressed_out,
    latent_out,
    query_out,
    key_out,
    value_out,
    head_out,
    out_w_out,
    misc_out,
    total_out,
    tok,
    weights,
    hidden,
    qc,
    latent,
    up_w,
    query,
    key,
    value,
    tok_heads,
    out_w,
    misc_t,
    totals,
    heads,
    pieces,
    down,
    gate_shared,
    gate_routed,
    up_shared,
    up_routed,
    down_shared,
    down_routed,
    save_sem,
    load_sem,
    *rest,
):
    ops = attention_ops()
    tok_op, pack_op, out_op, cot_op, piece_op, gate_up_op, head_op = ops
    bound = (
        (tokens, tok),
        (pack, weights),
        (out_own, out_w),
        (cotangent, cot_all),
        (pieces, gate_up_part),
        (gate_up_part, gate_up),
        (heads, tok_heads),
    )
    for op, (src, dst) in zip(ops, bound):
        count = len(op.scratch())
        op.bind(src, dst, rest[:count])
        rest = rest[count:]
    loads = [
        pltpu.make_async_copy(src, dst, load_sem.at[k])
        for k, (src, dst) in enumerate(
            (
                (shared_gate, gate_shared),
                (expert_gate, gate_routed),
                (shared_up, up_shared),
                (expert_up, up_routed),
                (shared_down, down_shared),
                (expert_down, down_routed),
            )
        )
    ]
    for load in loads:
        load.start()
    meet(ops)
    tok_op.step(0)
    pack_op.step(0)
    out_op.step(0)
    for step in (1, 2):
        tok_op.step(step)
        pack_op.step(step)

    wait_all(loads)
    row = lax.broadcasted_iota(jnp.int32, (DP * UNITS, FE), 0)
    column = lax.broadcasted_iota(jnp.int32, (DP * UNITS, FE), 1)
    group, unit = row // UNITS, row - row // UNITS * UNITS + tok_op.seat.own * UNITS
    pick = ((group * SLICE + unit == column) & (unit < SLICE)).astype(bf16)
    for k, (shared, routed) in enumerate(((gate_shared, gate_routed), (up_shared, up_routed))):
        for e in range(SETS):
            piece = shared[:, e, :] if e < NS else routed[:, e - NS, :]
            piece = nt(pick, piece).astype(bf16)
            at = (k * SETS + e) * UNITS
            for d in range(DP):
                pieces[d, at : at + UNITS, :] = piece[d * UNITS : (d + 1) * UNITS]
        if k == 0:
            tok_op.step(3)
            pack_op.step(3)
            out_op.step(1)
            out_op.step(2)
    piece_op.step(0)
    pack_op.step(4)
    pack_op.step(5)
    cot_op.step(0)
    tok_op.local().wait()
    saves = [
        pltpu.make_async_copy(src, dst, save_sem.at[k])
        for k, (src, dst) in enumerate(
            (
                (tok, tok_out),
                (weights, weights_out),
                (hidden, hidden_out),
                (qc.at[:, pl.ds(QW, RANK)], compressed_out),
                (latent, latent_out),
                (query, query_out),
                (key, key_out),
                (value, value_out),
                (tok_heads, head_out),
                (out_w, out_w_out),
                (misc_t, misc_out),
                (totals, total_out),
            )
        )
    ]
    saves[1].start()
    misc_t[...] = weights[:, MISC_AT:CORE_W].astype(f32).T
    up = weights[:, UP_AT:].reshape(DP, 4, RANK // DP, ROWS)
    for k in range(4):
        up_w[:, k * ROWS : (k + 1) * ROWS] = up[:, k].reshape(RANK, ROWS)
    each = RANK // DP
    for d in range(DP):
        misc_t[0:1, d * each : (d + 1) * each] = misc_t[GAIN_KV : GAIN_KV + 1, d * ROWS : d * ROWS + each]
    kv_gain = misc_t[0:1, :RANK]
    saves[10].start()
    gain = misc_t[GAIN_ONE : GAIN_ONE + 1, :]

    def project(*places):
        for place in places:
            start = tok_op.seat.index(*place) * ROWS

            @pl.loop(0, ROWS // 32)
            def _(k):
                at = pl.ds(pl.multiple_of(start + k * 32, 32), 32)
                values = tok[at, :].astype(f32)
                hidden[at, :] = (values * inverse_rms(values) * gain).astype(bf16)

            at = pl.ds(pl.multiple_of(start, ROWS), ROWS)
            qc[at, :] = nn(hidden[at, :], weights[:, :CORE_W])

    project((0, 0), (0, -1), (0, 1), (1, 0), (0, 2))
    tok_op.step(4)
    piece_op.step(5)
    gate_up_op.step(0)
    out_op.step(3)
    project((1, -1), (1, 1), (1, 2))
    tok_op.step(5, shared=False)
    for k in (0, 2, 3):
        saves[k].start()

    @pl.loop(0, SEQ // 256)
    def _(k):
        at = pl.ds(pl.multiple_of(k * 256, 256), 256)
        inner = qc[at, QW : QW + RANK]
        latent[at, :] = (inner * inverse_rms(inner) * kv_gain).astype(bf16)
        ropes, key_rope = qc[at, 2 * NOPE : QW], qc[at, MISC_AT:CORE_W]
        cos, sin = cosine[at, :], sine[at, :]
        ropes = (ropes * cos + swap_halves(ropes) * sin).astype(bf16)
        key_rope = key_rope * cos + swap_halves(key_rope) * sin
        lane = lax.broadcasted_iota(jnp.int32, key_rope.shape, 1)
        key_rope = jnp.where(lane < ROPE, key_rope, 0.0)
        expanded = nn(latent[at, :], up_w[...]).astype(bf16)
        for h in range(HEADS_HERE):
            query[h, at, :NOPE] = qc[at, h * NOPE : (h + 1) * NOPE].astype(bf16)
            query[h, at, NOPE:] = ropes
            turned = key_rope if h == 0 else pltpu.roll(key_rope, ROPE, 1)
            key[h, at, NOPE:] = turned.astype(bf16)
            base = h * (NOPE + VDIM)
            key[h, at, :NOPE] = expanded[:, base : base + NOPE]
            value[h, at, :] = expanded[:, base + NOPE : base + NOPE + VDIM]

    for k in (4, 5, 6, 7):
        saves[k].start()
    gate_up_op.step(1)
    gate_up_op.step(2)
    out_op.step(4)
    cot_op.step(1)
    cot_op.step(2)
    for h in range(HEADS_HERE):
        for i in range(SEQ // 256):
            at, seen = pl.ds(i * 256, 256), (i + 1) * 256
            scores = causal(nt(query[h, at, :], key[h, :seen, :]) * SCALE)
            top = jnp.max(scores, axis=1, keepdims=True)
            parts = jnp.exp(scores - top)
            total = jnp.sum(parts, axis=1, keepdims=True)
            probs = (parts * (1.0 / total)).astype(bf16)
            heads[at, h * VDIM : (h + 1) * VDIM] = nn(probs, value[h, :seen, :]).astype(bf16)
            totals[h, at, :] = jnp.broadcast_to(top + jnp.log(total), (256, ROWS))
        if h == 0:
            gate_up_op.step(3)
    head_op.step(0)
    saves[11].start()
    cot_op.step(3)
    for e in range(SETS):
        part = down_shared[:, e, :] if e < NS else down_routed[:, e - NS, :]
        down[e * ROOM : e * ROOM + SLICE, :] = part
        down[e * ROOM + SLICE : (e + 1) * ROOM, :] = jnp.zeros((ROOM - SLICE, D), bf16)
    down[HALF:, :] = jnp.zeros((FULL - HALF, D), bf16)
    down_save = pltpu.make_async_copy(down, down_out, load_sem.at[0])
    down_save.start()
    gate_up_op.step(4)
    out_op.step(5)
    saves[9].start()
    head_op.step(5)
    saves[8].start()
    own = tok_op.view((0, 0))[...].astype(f32)
    resid = own + nn(tok_heads[...], out_w[...])
    resid_two[...] = resid
    hidden_two[...] = (resid * inverse_rms(resid) * misc_t[GAIN_TWO : GAIN_TWO + 1, :]).astype(bf16)
    cot_op.step(4)
    wait_all(saves + [down_save])
    cot_op.step(5)
    gate_up_op.step(5)


def attention(*arrays):
    any_spec, vmem = pl.BlockSpec(memory_space=pl.ANY), pl.BlockSpec(memory_space=pltpu.VMEM)
    kept = [
        ((SEQ, D), bf16),
        ((D, PACK), bf16),
        ((SEQ, D), bf16),
        ((SEQ, RANK), f32),
        ((SEQ, RANK), bf16),
        ((HEADS_HERE, SEQ, 2 * NOPE), bf16),
        ((HEADS_HERE, SEQ, 2 * NOPE), bf16),
        ((HEADS_HERE, SEQ, VDIM), bf16),
        ((ROWS, D), bf16),
        ((D, D), bf16),
        ((ROWS, D), f32),
        ((HEADS_HERE, SEQ, ROWS), f32),
    ]
    made = [((ROWS, D), f32), ((ROWS, D), bf16), ((GROUP, D), bf16), ((RELAY, D), bf16), ((SP * RELAY, D), bf16), ((FULL, D), bf16)]
    scratch = kept[:3] + [((SEQ, CORE_W), f32), kept[4], ((RANK, KVW), bf16)] + kept[5:]
    scratch = scratch + [((SEQ, OW), bf16), ((DP, RELAY, ROWS), bf16), ((FULL, D), bf16)]
    scratch = scratch + [(array.shape, bf16) for array in arrays[3:9]]
    return pl.pallas_call(
        attention_kernel,
        name="attention",
        out_shape=[jax.ShapeDtypeStruct(*shape) for shape in made + kept],
        in_specs=[any_spec] * 10 + [vmem] * 2,
        out_specs=[vmem] * 2 + [any_spec] * (len(made) + len(kept) - 2),
        scratch_shapes=[pltpu.VMEM(*shape) for shape in scratch]
        + [pltpu.SemaphoreType.DMA((len(kept),)), pltpu.SemaphoreType.DMA((6,))]
        + [entry for op in attention_ops() for entry in op.scratch()],
        compiler_params=pltpu.CompilerParams(
            collective_id=0, has_side_effects=True, vmem_limit_bytes=60 * 2**20
        ),
        cost_estimate=pl.CostEstimate(
            flops=2 * SEQ * D * (CORE_W + OW), bytes_accessed=60 * 2**20, transcendentals=SEQ * SEQ
        ),
    )(*arrays)


def attention_grad_ops():
    return (
        Gather("dp", ROWS, D, spare=True),
        Swap(
            "dp",
            (DP * GU_PART, ROWS),
            lambda ref, j: ref.at[:, pl.ds(pl.multiple_of(j * ROWS, ROWS), ROWS)],
            lambda ref, j: ref.at[pl.ds(pl.multiple_of(j * GU_PART, GU_PART), GU_PART)],
        ),
        Gather("sp", DP * GU_PART, ROWS),
        Gather("sp", DN_PART, D),
        Swap(
            "dp",
            (GROUP, ROWS),
            lambda ref, j: ref.at[:, pl.ds(pl.multiple_of(j * ROWS, ROWS), ROWS)],
            lambda ref, j: ref.at[pl.ds(pl.multiple_of(j * ROWS, ROWS), ROWS)],
        ),
        Swap(
            "sp",
            (SEQ, OW),
            lambda ref, j: ref.at[:, pl.ds(pl.multiple_of(j * OW, OW), OW)],
            lambda ref, j: ref.at[pl.ds(pl.multiple_of(j * ROWS, ROWS), ROWS)],
        ),
    )


def attention_grad_kernel(
    proj_own,
    tok_all,
    weights_all,
    hidden_all,
    compressed_all,
    latent_all,
    query_all,
    key_all,
    value_all,
    head_all,
    head_tok,
    misc_all,
    total_all,
    gate_up_sum,
    down_sum,
    cosine,
    sine,
    norm_rows,
    hidden_part,
    gate_up_piece,
    gate_up_total,
    down_total,
    grads,
    proj_all,
    out_grad,
    tok,
    weights,
    hidden,
    compressed,
    latent,
    query,
    key,
    value,
    head_cols,
    misc_t,
    totals,
    up_w,
    head_grad,
    key_grad,
    value_grad,
    rope_grad,
    expanded_grad,
    qc_grad,
    scale_one,
    misc_grad,
    up_grad,
    made_w,
    made_h,
    load_sem,
    out_sem,
    *rest,
):
    ops = attention_grad_ops()
    proj_op, piece_op, gate_up_op, down_op, out_op, head_op = ops
    bound = (
        (proj_own, proj_all),
        (gate_up_sum, gate_up_piece),
        (gate_up_piece, gate_up_total),
        (down_sum, down_total),
        (head_all, head_cols),
        (head_tok, head_grad),
    )
    for op, (src, dst) in zip(ops, bound):
        count = len(op.scratch())
        op.bind(src, dst, rest[:count])
        rest = rest[count:]
    loads = [
        pltpu.make_async_copy(src, dst, load_sem.at[k])
        for k, (src, dst) in enumerate(
            (
                (tok_all, tok),
                (query_all, query),
                (key_all, key),
                (value_all, value),
                (total_all, totals),
                (weights_all, weights),
                (compressed_all, compressed),
                (latent_all, latent),
                (misc_all, misc_t),
                (hidden_all, hidden),
            )
        )
    ]
    for load in loads:
        load.start()
    meet(ops)
    head_op.step(0)
    piece_op.step(0)
    down_op.step(0)
    proj_op.step(0)
    out_op.step(0)
    wait_all(loads)

    @pl.loop(0, SEQ // 32)
    def _(k):
        at = pl.ds(pl.multiple_of(k * 32, 32), 32)
        scale_one[at, :] = inverse_rms(tok[at, :].astype(f32))

    up = weights[:, UP_AT:].reshape(DP, 4, RANK // DP, ROWS)
    for k in range(4):
        up_w[:, k * ROWS : (k + 1) * ROWS] = up[:, k].reshape(RANK, ROWS)
    head_op.step(5)
    piece_op.step(5)
    gate_up_op.step(0)
    for h in range(HEADS_HERE):
        for i in reversed(range(SEQ // 256)):
            at, seen = pl.ds(i * 256, 256), (i + 1) * 256
            piece = head_grad[at, h * VDIM : (h + 1) * VDIM]
            scores = causal(nt(query[h, at, :], key[h, :seen, :]) * SCALE)
            probs = jnp.exp(scores - totals[h, at, 0:1])
            dprob = nt(piece, value[h, :seen, :])
            delta = jnp.sum(probs * dprob, axis=1, keepdims=True)
            score_grad = (probs * (dprob - delta) * SCALE).astype(bf16)
            query_grad = nn(score_grad, key[h, :seen, :]).astype(bf16)
            qc_grad[at, h * NOPE : (h + 1) * NOPE] = query_grad[:, :NOPE]
            turned = query_grad[:, NOPE:].astype(f32)
            rope_grad[at, :] = turned if h == 0 else rope_grad[at, :] + turned
            from_query = tn(score_grad, query[h, at, :])
            from_out = tn(probs.astype(bf16), piece)
            if i == SEQ // 256 - 1:
                key_grad[h, :seen, :] = from_query
                value_grad[h, :seen, :] = from_out
            else:
                key_grad[h, :seen, :] += from_query
                value_grad[h, :seen, :] += from_out
        if h == 0:
            down_op.step(1)
            down_op.step(2)
            proj_op.step(1)
            proj_op.step(2)
    gate_up_op.step(1)
    gate_up_op.step(2)
    down_op.step(3)
    proj_op.step(3)
    kv_gain = misc_t[0:1, :RANK]
    lane = lax.broadcasted_iota(jnp.int32, (128, ROWS), 1)

    @pl.loop(0, SEQ // 128)
    def _(k):
        at = pl.ds(pl.multiple_of(k * 128, 128), 128)
        cos, sin = cosine[at, :], sine[at, :]
        ropes = rope_grad[at, :]
        qc_grad[at, 2 * NOPE : QW] = (ropes * cos - swap_halves(ropes) * sin).astype(bf16)
        key_rope = jnp.zeros((128, ROWS), f32)
        for h in range(HEADS_HERE):
            base = h * (NOPE + VDIM)
            expanded_grad[at, base : base + NOPE] = key_grad[h, at, :NOPE].astype(bf16)
            expanded_grad[at, base + NOPE : base + NOPE + VDIM] = value_grad[h, at, :].astype(bf16)
            turned = key_grad[h, at, NOPE:].astype(bf16).astype(f32)
            turned = turned if h == 0 else pltpu.roll(turned, ROPE, 1)
            key_rope = key_rope + jnp.where(lane < ROPE, turned, 0.0)
        key_rope = key_rope * cos - swap_halves(key_rope) * sin
        qc_grad[at, MISC_AT:CORE_W] = jnp.where(lane < ROPE, key_rope, 0.0).astype(bf16)

    made = tn(latent[...], expanded_grad[...]).astype(bf16)
    each = RANK // DP
    for d in range(DP):
        for k in range(4):
            at = pl.ds(d * ROWS + k * each, each)
            up_grad[at, :] = made[d * each : (d + 1) * each, k * ROWS : (k + 1) * ROWS]
    up_store = pltpu.make_async_copy(up_grad, grads.at[:, pl.ds(UP_AT, ROWS)], out_sem.at[2])
    up_store.start()
    misc_grad[...] = jnp.zeros_like(misc_grad)
    misc_grad[64:72, :] = norm_rows[...]
    kv_total = jnp.zeros((1, RANK), f32)
    for k in range(SEQ // 256):
        at = pl.ds(k * 256, 256)
        inner = compressed[at, :]
        scale = inverse_rms(inner)
        latent_grad = nt(expanded_grad[at, :], up_w[...])
        kv_total = kv_total + jnp.sum(latent_grad * inner * scale, axis=0, keepdims=True)
        qc_grad[at, QW : QW + RANK] = norm_back(inner, scale, kv_gain, latent_grad).astype(bf16)
    for d in range(DP):
        misc_grad[66:67, d * ROWS : d * ROWS + each] = kv_total[:, d * each : (d + 1) * each]
    gate_up_op.step(3)
    proj_op.step(4)

    def put(n):
        at = pl.ds(pl.multiple_of(n * TILE, TILE), TILE)
        return pltpu.make_async_copy(made_h.at[n % 2], hidden_part.at[:, at], out_sem.at[n % 2])

    @pl.loop(0, D // TILE)
    def _(n):
        at = pl.ds(pl.multiple_of(n * TILE, TILE), TILE)

        @pl.when(n >= 2)
        def _():
            put(n - 2).wait()

        grad = nt(qc_grad[...], weights[at, :CORE_W])
        made_h[n % 2] = grad.astype(bf16)
        put(n).start()
        grad = grad * tok[:, at].astype(f32) * scale_one[...]
        misc_grad[64:65, at] = jnp.sum(grad, axis=0, keepdims=True)

    put(2).wait()
    put(3).wait()
    proj_op.step(5)
    out_op.step(5)

    def half(n, k):
        rows, at = pl.ds(k * SEQ, SEQ), pl.ds(n * TILE, TILE)
        return pltpu.make_async_copy(proj_all.at[rows, at], made_h.at[k], out_sem.at[k])

    half(0, 0).start()
    half(0, 1).start()
    for n in range(D // TILE):
        total = 0.0
        for k in range(2):
            half(n, k).wait()
            total = total + tn(head_cols[pl.ds(k * SEQ, SEQ), :], made_h[k])
            if n < D // TILE - 1:
                half(n + 1, k).start()
        rows, at = pl.ds(n // 2 * ROWS, ROWS), pl.ds(n % 2 * TILE, TILE)
        out_grad[rows, at] = total.astype(bf16)

    def store(n):
        at = pl.ds(pl.multiple_of(n * TILE, TILE), TILE)
        return pltpu.make_async_copy(
            made_w.at[n % 2], grads.at[at, pl.ds(0, CORE_W)], out_sem.at[n % 2]
        )

    @pl.loop(0, D // TILE)
    def _(n):
        at = pl.ds(pl.multiple_of(n * TILE, TILE), TILE)

        @pl.when(n >= 2)
        def _():
            store(n - 2).wait()

        made = tn(hidden[:, at], qc_grad[...])
        made_w[n % 2, :, :MISC_AT] = made[:, :MISC_AT].astype(bf16)
        made_w[n % 2, :, MISC_AT:] = (made[:, MISC_AT:] + misc_grad[:, at].T).astype(bf16)
        store(n).start()

    store(2).wait()
    store(3).wait()
    up_store.wait()
    gate_up_op.step(4)
    down_op.step(4)
    gate_up_op.step(5)
    down_op.step(5)


def attention_grad(*arrays):
    any_spec, vmem = pl.BlockSpec(memory_space=pl.ANY), pl.BlockSpec(memory_space=pltpu.VMEM)
    scratch = [
        ((SEQ, D), bf16),
        ((D, PACK), bf16),
        ((SEQ, D), bf16),
        ((SEQ, RANK), f32),
        ((SEQ, RANK), bf16),
        ((HEADS_HERE, SEQ, 2 * NOPE), bf16),
        ((HEADS_HERE, SEQ, 2 * NOPE), bf16),
        ((HEADS_HERE, SEQ, VDIM), bf16),
        ((GROUP, ROWS), bf16),
        ((ROWS, D), f32),
        ((HEADS_HERE, SEQ, ROWS), f32),
        ((RANK, KVW), bf16),
        ((SEQ, OW), bf16),
        ((HEADS_HERE, SEQ, 2 * NOPE), f32),
        ((HEADS_HERE, SEQ, VDIM), f32),
        ((SEQ, ROWS), f32),
        ((SEQ, KVW), bf16),
        ((SEQ, CORE_W), bf16),
        ((SEQ, 1), f32),
        ((ROWS, D), f32),
        ((D, ROWS), bf16),
        ((2, TILE, CORE_W), bf16),
        ((2, SEQ, TILE), bf16),
    ]
    return pl.pallas_call(
        attention_grad_kernel,
        name="attention_grad",
        out_shape=[
            jax.ShapeDtypeStruct((SEQ, D), bf16),
            jax.ShapeDtypeStruct((DP * GU_PART, ROWS), bf16),
            jax.ShapeDtypeStruct((SP * DP * GU_PART, ROWS), bf16),
            jax.ShapeDtypeStruct((FULL, D), bf16),
            jax.ShapeDtypeStruct((D, PACK), bf16),
            jax.ShapeDtypeStruct((GROUP, D), bf16),
            jax.ShapeDtypeStruct((2 * ROWS, D // 2), bf16),
        ],
        in_specs=[any_spec] * 15 + [vmem] * 3,
        out_specs=[any_spec] * 6 + [vmem],
        scratch_shapes=[pltpu.VMEM(*shape) for shape in scratch]
        + [pltpu.SemaphoreType.DMA((10,)), pltpu.SemaphoreType.DMA((3,))]
        + [entry for op in attention_grad_ops() for entry in op.scratch()],
        compiler_params=pltpu.CompilerParams(
            collective_id=4, has_side_effects=True, vmem_limit_bytes=61 * 2**20
        ),
        cost_estimate=pl.CostEstimate(
            flops=6 * SEQ * D * CORE_W, bytes_accessed=60 * 2**20, transcendentals=SEQ * SEQ
        ),
    )(*arrays)


def per_device(
    tokens,
    cotangent,
    chosen,
    attn_gain,
    w_query,
    w_kv_down,
    kv_gain,
    w_kv_up,
    w_out,
    ffn_gain,
    w_router,
    shared_gate,
    shared_up,
    shared_down,
    expert_gate,
    expert_up,
    expert_down,
):
    own_sp = lax.axis_index("sp")
    picks = jnp.any(chosen[:, :, None] == jnp.arange(EXPERTS, dtype=jnp.int32), axis=1).astype(bf16)
    own_query = lax.dynamic_slice_in_dim(w_query, own_sp * QW, QW, 1)
    own_up = lax.dynamic_slice_in_dim(w_kv_up, own_sp * KVW, KVW, 1)
    pack = jnp.concatenate(
        [
            own_query[:, :NOPE],
            own_query[:, QK : QK + NOPE],
            own_query[:, NOPE:QK],
            own_query[:, QK + NOPE :],
            w_kv_down,
            picks,
            attn_gain[:, None],
            ffn_gain[:, None],
            jnp.pad(kv_gain, (0, ROWS - kv_gain.shape[0]))[:, None],
            jnp.zeros((ROWS, 9), bf16),
            w_router,
            jnp.zeros((ROWS, 44), bf16),
            own_up.reshape(RANK // DP, 4, ROWS).transpose(1, 0, 2).reshape(ROWS, ROWS),
        ],
        axis=1,
    )
    cosine, sine = rope_tables()
    (
        resid_two,
        hidden_two,
        cot_all,
        _,
        gate_up,
        down,
        tok_all,
        weights,
        hidden_one,
        compressed,
        latent,
        queries,
        keys,
        values,
        head_out,
        out_w,
        misc,
        log_totals,
    ) = attention(
        tokens,
        pack,
        cotangent,
        shared_gate,
        expert_gate,
        shared_up,
        expert_up,
        shared_down,
        expert_down,
        w_out,
        cosine,
        sine,
    )
    gain_one, gain_two = misc[GAIN_ONE], misc[GAIN_TWO]
    latent_gain = misc[GAIN_KV].reshape(DP, ROWS)[:, : RANK // DP].reshape(RANK)
    router_t = misc[ROUTER_LANE : ROUTER_LANE + 16].astype(bf16)
    router_w = router_t[:EXPERTS]
    picks_all = weights[:, MISC_AT:CORE_W]
    scale_two = inverse_rms(resid_two)

    hidden_grad, mixed_part, gate_up_grad, down_grad = experts(
        hidden_two, gate_up, router_t, down, cot_all, picks_all
    )
    prob_grad = hidden_grad[:, D + PICK_LANE : D + PICK_LANE + EXPERTS]
    hidden_grad = hidden_grad[:, :D]

    logits = nt(hidden_two, router_w)
    router = jax.nn.softmax(logits, axis=-1)
    prob_grad = prob_grad * picks.astype(f32)
    logit_grad = (
        router * (prob_grad - jnp.sum(router * prob_grad, axis=-1, keepdims=True))
    ).astype(bf16)
    hidden_grad = hidden_grad + nn(logit_grad, router_w)
    router_grad = tn(logit_grad, hidden_two)
    gain_two_grad = jnp.sum(hidden_grad * resid_two * scale_two, axis=0)
    upstream = cotangent.astype(f32)
    resid_two_grad = upstream + norm_back(resid_two, scale_two, gain_two, hidden_grad)
    proj_grad = resid_two_grad.astype(bf16)

    head_tok_grad = nt(proj_grad, out_w).astype(bf16)
    norm_rows = jnp.concatenate(
        [
            jnp.zeros((1, D), f32),
            gain_two_grad[None],
            jnp.zeros((1, D), f32),
            router_grad,
            jnp.zeros((1, D), f32),
        ]
    )
    hidden_one_grad, _, gu_total, dn_total, grads, _, out_grad = attention_grad(
        proj_grad,
        tok_all,
        weights,
        hidden_one,
        compressed,
        latent,
        queries,
        keys,
        values,
        head_out,
        head_tok_grad,
        misc,
        log_totals,
        gate_up_grad,
        down_grad,
        cosine,
        sine,
        norm_rows,
    )

    _, hidden_one_grad, mixed, grads, _, out_total = exchange(
        "sum_grads",
        6,
        [
            Scatter("dp", ROWS, PACK, bf16, spare=True),
            Scatter("sp", ROWS, D),
            Scatter("dp", ROWS, D, spare=True),
            Gather("sp", ROWS, PACK),
            Scatter("sp", 2 * ROWS // SP, D // 2, bf16),
            Gather("sp", 2 * ROWS // SP, D // 2),
        ],
        [grads, hidden_one_grad, mixed_part, out_grad],
        plan=[(0, 0), (1, 0), (4, 0), (2, 0), (0, 1), (4, 1), (1, 1), (0, 2), (0, 3), (4, 2), (4, 3)]
        + [(1, 2), (0, 4), (3, 0), (4, 4), (5, 0), (1, 3), (2, 1), (3, 1), (3, 2), (5, 1), (5, 2)]
        + [(2, 2), (2, 3), (1, 4), (3, 3), (5, 3), (2, 4), (3, 4), (5, 4)]
        + [(op, 5) for op in range(6)],
        chained=[(3, 0), (5, 4)],
    )
    gu_total = gu_total.reshape(SP, DP, GU_PART, ROWS)
    grads = grads.reshape(SP, ROWS, PACK)
    mixed = (resid_two + mixed).astype(bf16)
    resid_one = tokens.astype(f32)
    own_scale = inverse_rms(resid_one)
    tokens_grad = resid_two_grad + norm_back(resid_one, own_scale, gain_one, hidden_one_grad)
    tokens_grad = tokens_grad.astype(bf16)

    def side_by_side(block, width):
        return block.astype(f32).transpose(1, 0, 2).reshape(-1, SP * width)

    query_total = grads[:, :, :QW]
    query_total = jnp.concatenate(
        [
            query_total[:, :, :NOPE],
            query_total[:, :, 2 * NOPE : 2 * NOPE + ROPE],
            query_total[:, :, NOPE : 2 * NOPE],
            query_total[:, :, 2 * NOPE + ROPE :],
        ],
        axis=2,
    )
    query_total = side_by_side(query_total, QW)
    tail = jnp.sum(grads[:, :, QW:CORE_W].astype(f32), axis=0)
    down_total, tail = tail[:, : RANK + ROPE], tail[:, RANK + ROPE :]
    out_total = jnp.concatenate([out_total[:ROWS], out_total[ROWS:]], axis=1).astype(f32)
    up_total = grads[:, :, UP_AT:].reshape(SP, 4, RANK // DP, ROWS).transpose(0, 2, 1, 3)
    up_total = side_by_side(up_total.reshape(SP, RANK // DP, KVW), KVW)

    gu_total = gu_total.transpose(0, 2, 1, 3).reshape(2, SETS, ROOM, DP, ROWS)[:, :, :SLICE]
    gu_total = gu_total.transpose(0, 4, 1, 3, 2).reshape(2, ROWS, SETS, FE).astype(f32)
    dn_total = dn_total[:HALF].reshape(SETS, ROOM, D)[:, :SLICE].transpose(1, 0, 2).astype(f32)
    return (
        mixed,
        tokens_grad,
        tail[:, 0],
        query_total,
        down_total,
        tail[: RANK // DP, 2],
        up_total,
        out_total,
        tail[:, 1],
        tail[:, 3:7],
        gu_total[0, :, :NS],
        gu_total[1, :, :NS],
        dn_total[:, :NS],
        gu_total[0, :, NS:],
        gu_total[1, :, NS:],
        dn_total[:, NS:],
    )


def solution(mesh):
    rows = P(("dp", "sp"), None)
    vec, mat, cube = P("dp"), P("dp", None), P("dp", None, None)
    return jax.shard_map(
        per_device,
        mesh=mesh,
        in_specs=(rows, rows, rows, vec, mat, mat, vec, mat, mat, vec, mat) + (cube,) * 6,
        out_specs=(rows, rows, vec, mat, mat, vec, mat, mat, vec, mat) + (cube,) * 6,
        check_vma=False,
    )
```

```python
import functools

import jax
import jax.numpy as jnp
import numpy as np
from jax import lax
from jax.experimental import pallas as pl
from jax.experimental.pallas import tpu as pltpu
from jax.sharding import PartitionSpec as P

D = 2048
HEADS = 16
NOPE = 128
ROPE = 64
QK = NOPE + ROPE
VDIM = 128
RANK = 512
FE = 1408
NS = 2
EXPERTS = 4
TOP = 2
SETS = NS + EXPERTS
DP = 16
SP = 8
ROWS = 128
SEQ = SP * ROWS
GROUP = DP * ROWS
HEADS_HERE = HEADS // SP
QW = HEADS_HERE * QK
KVW = HEADS_HERE * (NOPE + VDIM)
OW = HEADS_HERE * VDIM
SLICE = FE // DP
CORE_W = 1024
UP_AT = CORE_W
MISC_AT = CORE_W - ROWS
PICK_LANE, GAIN_ONE, GAIN_TWO, GAIN_KV, ROUTER_LANE = 64, 68, 69, 70, 80
ROOM = 96
HALF = SETS * ROOM
FULL = 640
CHUNK = 2 * ROWS
TILE = 512
SCALE = QK ** (-0.5)
PACK = QW + RANK + ROPE + ROPE + ROWS
GU_PART = 2 * HALF // SP
RELAY = 2 * HALF // SP
UNITS = ROOM // SP
DN_PART = FULL // SP

epsilon = 1e-06
bf16 = jnp.bfloat16
f32 = jnp.float32


def mm(left, right, dims):
    return lax.dot_general(left, right, ((dims[0], dims[1]), ((), ())), preferred_element_type=f32)


def nn(left, right):
    return mm(left, right, ((1,), (0,)))


def nt(left, right):
    return mm(left, right, ((1,), (1,)))


def tn(left, right):
    return mm(left, right, ((0,), (0,)))


def rope_tables():
    inverse = 10000.0 ** (-np.arange(ROPE // 2, dtype=np.float64) * 2.0 / ROPE)
    angles = np.arange(SEQ, dtype=np.float64)[:, None] * inverse[None, :]
    cosine, sine = np.cos(angles), np.sin(angles)
    cosine = np.concatenate([cosine] * 4, axis=1)
    sine = np.concatenate([-sine, sine] * 2, axis=1)
    return jnp.asarray(cosine, f32), jnp.asarray(sine, f32)


def norm_back(values, scale, gain, grad):
    scaled = gain * grad
    total = jnp.sum(scaled * values, axis=-1, keepdims=True) / values.shape[-1]
    return scale * scaled - values * (scale * scale * scale) * total


def inverse_rms(values):
    return lax.rsqrt(jnp.mean(values * values, axis=-1, keepdims=True) + epsilon)


class Seat:
    def __init__(self, axis):
        own_dp, own_sp = lax.axis_index("dp"), lax.axis_index("sp")
        self.axis = axis
        if axis == "sp":
            self.pair, self.ring, self.core, self.cores = own_sp // 4, own_sp % 4, 0, 1
            self.own, self.size = own_sp, SP
            self.device = lambda index: (own_dp, index)
        else:
            self.ring, self.pair, self.core, self.cores = own_dp // 4, (own_dp // 2) % 2, own_dp % 2, 2
            self.own, self.size = own_dp, DP
            self.device = lambda index: (index, own_sp)

    def index(self, pair, ring, core=0):
        pair, ring = (self.pair + pair) % 2, (self.ring + ring) % 4
        if self.axis == "sp":
            return pair * 4 + ring
        return (ring * 2 + pair) * 2 + (self.core + core) % 2


def remote(src, dst, send_sem, recv_sem, device):
    return pltpu.make_async_remote_copy(
        src_ref=src,
        dst_ref=dst,
        send_sem=send_sem,
        recv_sem=recv_sem,
        device_id=device,
        device_id_type=pl.DeviceIdType.MESH,
    )


def block_of(ref, start, size):
    return ref.at[pl.ds(pl.multiple_of(start, 16), size)]


def middle(rows):
    return (rows // 2 + 15) // 16 * 16


NEAR = ((0, 1), (0, -1), (1, 0))
SHARE = ((0, 0), (0, -1), (0, 1), (1, 0), (0, 2), (1, -1), (1, 1), (1, 2))
ORDER = ((1, 2), (1, 1), (1, -1), (0, 2), (1, 0), (0, 1), (0, -1), (0, 0))


class Gather:
    def __init__(self, axis, rows, width, spare=False):
        self.axis, self.rows, self.width, self.spare = axis, rows, width, spare
        self.count = SP if axis == "sp" else DP

    def in_spec(self):
        return pl.BlockSpec(memory_space=pl.ANY)

    def out(self):
        return (
            jax.ShapeDtypeStruct((self.count * self.rows, self.width), bf16),
            pl.BlockSpec(memory_space=pl.ANY),
        )

    def scratch(self):
        return [pltpu.SemaphoreType.DMA((17,)), pltpu.SemaphoreType.DMA((17,)), pltpu.SemaphoreType.DMA]

    def partners(self, seat):
        near = [seat.index(*n) for n in NEAR]
        return near + ([seat.index(0, 0, 1)] if seat.cores == 2 else [])

    def bind(self, src, out, scratch):
        self.src, self.dst = src, out
        self.send_sem, self.recv_sem, self.local_sem = scratch
        self.seat = Seat(self.axis)

    def view(self, place, half=None):
        start = self.seat.index(*place) * self.rows
        if half is None:
            return block_of(self.dst, start, self.rows)
        cut = middle(self.rows)
        return block_of(self.dst, start + half * cut, (cut, self.rows - cut)[half])

    def table(self, number):
        if number in (0, 1, 2, 8):
            return self.src, self.view((0, 0)), {0: (0, 1), 1: (0, -1), 2: (1, 0), 8: (0, 0, 1)}[number]
        if 8 <= number < 16:
            here = self.view(SHARE[number - 8])
            return here, here, (0, 0, 1)
        place, half, to = {
            7: ((1, -1), 0, (0, 1)),
            16: ((1, 1), 1, (0, -1)),
        }[number] if self.spare and number in (7, 16) else {
            3: ((0, -1), 0, (0, 1)),
            4: ((0, 1), 1, (0, -1)),
            5: ((1, 0), None, (0, 1)),
            6: ((1, 0), None, (0, -1)),
            7: ((0, 2), None, (1, 0)),
        }[number]
        here = self.view(place, half)
        return here, here, to

    def copy(self, number):
        src, dst, to = self.table(number)
        return remote(
            src,
            dst,
            self.send_sem.at[number],
            self.recv_sem.at[number],
            self.seat.device(self.seat.index(*to)),
        )

    def go(self, *numbers):
        for number in numbers:
            self.copy(number).start()

    def share(self, *numbers):
        if self.seat.cores == 2:
            self.go(*[8 + number for number in numbers])

    def arrived(self, *numbers):
        for number in numbers:
            self.copy(number).wait_recv()

    def local(self):
        return pltpu.make_async_copy(self.src, self.view((0, 0)), self.local_sem)

    def step(self, number, shared=True):
        if number == 0:
            self.local().start()
            self.go(0, 1, 2)
            self.share(0)
        elif number == 1:
            self.arrived(0, 1)
            self.go(3, 4)
            self.share(1, 2)
        elif number == 2:
            self.arrived(2)
            self.go(5, 6)
            self.share(3)
        elif number == 3:
            self.arrived(3, 4)
            if not self.spare:
                self.go(7)
            self.share(4)
        elif number == 4:
            self.arrived(5, 6)
            if self.spare:
                self.go(7, 16)
                self.share(5, 6)
                self.arrived(7, 16)
                self.share(7)
            else:
                self.arrived(7)
                self.share(5, 6, 7)
        else:
            numbers = list(range(8)) + [16] * self.spare
            if self.seat.cores == 2:
                numbers = numbers + list(range(8, 16))
                if shared:
                    self.arrived(*range(8, 16))
            for number in numbers:
                self.copy(number).wait_send()
            if shared:
                self.local().wait()


class Scatter:
    def __init__(self, axis, rows, width, kind=f32, spare=False, load=False):
        self.axis, self.rows, self.width, self.kind, self.spare = axis, rows, width, kind, spare
        self.load = load
        self.count = SP if axis == "sp" else DP

    def in_spec(self):
        return pl.BlockSpec(memory_space=pl.ANY if self.load else pltpu.VMEM)

    def out(self):
        return (
            jax.ShapeDtypeStruct((self.rows, self.width), self.kind),
            pl.BlockSpec(memory_space=pltpu.VMEM),
        )

    def scratch(self):
        block, cut = (self.rows, self.width), middle(self.rows)
        first, second = (cut, self.width), (self.rows - cut, self.width)
        shapes = [block, block, block, first, second, block, block, block]
        shapes = shapes + [(8 if self.axis == "dp" else 5,) + block]
        kept = [pltpu.VMEM((self.count * self.rows, self.width), bf16), pltpu.SemaphoreType.DMA]
        return [pltpu.SemaphoreType.DMA((17,)), pltpu.SemaphoreType.DMA((17,))] + [
            pltpu.VMEM(shape, bf16) for shape in shapes
        ] + kept * self.load

    partners = Gather.partners
    copy = Gather.copy
    go = Gather.go
    arrived = Gather.arrived

    def sizes(self):
        rows, cut = self.rows, middle(self.rows)
        return [rows] * 3 + [cut, rows - cut] + [rows] * 3

    def bind(self, src, out, scratch):
        self.src, self.dst = src, out
        self.send_sem, self.recv_sem = scratch[:2]
        self.got, self.made = scratch[2:10], scratch[10]
        self.seat = Seat(self.axis)
        if self.load:
            self.loading = pltpu.make_async_copy(src, scratch[11], scratch[12])
            self.loading.start()
            self.src = scratch[11]

    def given(self, *place):
        return block_of(self.src, self.seat.index(*place) * self.rows, self.rows)

    def slot(self, place):
        if self.axis == "dp":
            return self.made.at[ORDER.index(place)]
        kept = ((1, 0), (0, 1), (0, -1)) + (((1, 1), (1, -1)) if self.spare else ((0, 2),))
        k = kept.index(place)
        return self.made[k] if isinstance(self.made, list) else self.made.at[k]

    def part(self, place):
        return self.slot(place) if self.axis == "dp" else self.given(*place)

    def ready(self, *places):
        if self.axis == "dp":
            for place in places:
                self.arrived(8 + ORDER.index(place))
                self.add(self.slot(place), [self.slot(place), self.given(*place)])

    def add(self, dst, terms):
        rows = dst.shape[0]
        step = 16

        @pl.loop(0, rows // step)
        def _(i):
            at = pl.ds(pl.multiple_of(i * step, step), step)
            total = terms[0][at, :].astype(f32)
            for term in terms[1:]:
                total = total + term[at, :].astype(f32)
            dst[at, :] = total.astype(dst.dtype)

    def add_half(self, place, half, term):
        made, part = self.halves(self.slot(place)), self.halves(self.part(place))
        self.add(made[half], [part[half], term])
        if self.axis == "sp":
            self.add(made[1 - half], [part[1 - half]])

    def halves(self, ref):
        cut = middle(self.rows)
        return ref.at[pl.ds(0, cut)], ref.at[pl.ds(cut, self.rows - cut)]

    def table(self, number):
        if 8 <= number < 16:
            return self.given(*ORDER[number - 8], 1), self.made.at[number - 8], (0, 0, 1)
        if self.spare and number in (0, 1, 2, 3, 4, 16):
            if number in (1, 2):
                return self.slot((1, 3 - 2 * number)), self.got[number], (0, 3 - 2 * number)
            half = 0 if number in (0, 3) else 1
            src = self.halves(self.part((1, 2) if number in (0, 16) else (0, 2)))[half]
            dst = self.halves(self.got[0])[half] if number in (0, 16) else self.got[number]
            return src, dst, (0, 1 - 2 * half)
        src, to = {
            0: (lambda: self.part((1, 2)), (1, 0)),
            1: (lambda: self.part((1, 1)), (0, 1)),
            2: (lambda: self.part((1, -1)), (0, -1)),
            3: (lambda: self.halves(self.slot((0, 2)))[0], (0, 1)),
            4: (lambda: self.halves(self.slot((0, 2)))[1], (0, -1)),
            5: (lambda: self.slot((1, 0)), (1, 0)),
            6: (lambda: self.slot((0, 1)), (0, 1)),
            7: (lambda: self.slot((0, -1)), (0, -1)),
        }[number]
        return src(), self.got[number], to

    def step(self, number):
        if number == 0:
            if self.load:
                self.loading.wait()
            if self.axis == "dp":
                self.go(*range(8, 16))
            self.ready((1, 2))
            if self.spare:
                self.go(0, 16)
                self.ready((0, 2))
                self.go(3, 4)
                self.ready((1, 1), (1, -1))
                return
            self.go(0)
            self.ready((1, 1))
            self.go(1)
            self.ready((1, -1))
            self.go(2)
        elif number == 1 and self.spare:
            self.arrived(0, 16)
            for place, half in (((1, 1), 0), ((1, -1), 1)):
                self.add_half(place, half, self.halves(self.got[0])[half])
                self.go(1 + half)
        elif number == 1:
            self.ready((0, 2))
            self.arrived(0)
            self.add(self.slot((0, 2)), [self.part((0, 2)), self.got[0]])
            self.go(3, 4)
        elif number == 2:
            self.ready((1, 0))
            self.arrived(1, 2)
            self.add(self.slot((1, 0)), [self.part((1, 0)), self.got[1], self.got[2]])
            self.go(5)
        elif number == 3:
            self.ready((0, 1), (0, -1))
            self.arrived(3, 4)
            for place, half in (((0, 1), 0), ((0, -1), 1)):
                self.add_half(place, half, self.got[3 + half])
                self.go(6 + half)
        elif number == 4:
            self.ready((0, 0))
            self.arrived(5, 6, 7)
            self.add(self.dst, [self.part((0, 0)), self.got[5], self.got[6], self.got[7]])
        else:
            numbers = list(range(16 if self.axis == "dp" else 8)) + [16] * self.spare
            for number in numbers:
                self.copy(number).wait_send()


class Swap:
    def __init__(self, axis, shape, take, put, kind="any"):
        self.axis, self.shape, self.take, self.put = axis, shape, take, put
        self.count = SP if axis == "sp" else DP

    def in_spec(self):
        return pl.BlockSpec(memory_space=pl.ANY)

    def out(self):
        return jax.ShapeDtypeStruct(self.shape, bf16), pl.BlockSpec(memory_space=pl.ANY)

    def scratch(self):
        sems = pltpu.SemaphoreType.DMA((self.count,))
        return [sems, sems, pltpu.SemaphoreType.DMA]

    def partners(self, seat):
        return [(seat.own + k) % seat.size for k in range(1, seat.size)]

    def bind(self, src, out, scratch):
        self.src, self.dst = src, out
        self.send_sem, self.recv_sem, self.local_sem = scratch
        self.seat = Seat(self.axis)

    def copy(self, k):
        to = (self.seat.own + k) % self.seat.size
        return remote(
            self.take(self.src, to),
            self.put(self.dst, self.seat.own),
            self.send_sem.at[k],
            self.recv_sem.at[k],
            self.seat.device(to),
        )

    def local(self):
        own = self.seat.own
        return pltpu.make_async_copy(self.take(self.src, own), self.put(self.dst, own), self.local_sem)

    def step(self, number):
        if number == 0:
            self.local().start()

            @pl.loop(1, self.seat.size)
            def _(k):
                self.copy(k).start()

        elif number == 5:

            @pl.loop(1, self.seat.size)
            def _(k):
                self.copy(k).wait_recv()
                self.copy(k).wait_send()

            self.local().wait()


def meet(ops):
    barrier = pltpu.get_barrier_semaphore()
    total = 0
    for axis in ("sp", "dp"):
        mine = [op for op in ops if op.axis == axis]
        if not mine:
            continue
        seat = Seat(axis)
        widest = max(mine, key=lambda op: len(op.partners(seat)))
        for partner in widest.partners(seat):
            pl.semaphore_signal(
                barrier, inc=1, device_id=seat.device(partner), device_id_type=pl.DeviceIdType.MESH
            )
            total += 1
    pl.semaphore_wait(barrier, total)


def exchange(name, number, ops, arrays, plan=None, chained=()):
    chained = dict(chained)
    plan = plan or [(op, step) for step in range(6) for op in range(len(ops))]
    counts = [len(op.scratch()) for op in ops]
    inputs = [k for k in range(len(ops)) if k not in chained]

    def body(*refs):
        given = dict(zip(inputs, refs[: len(inputs)]))
        outs = refs[len(inputs) : len(inputs) + len(ops)]
        rest = refs[len(inputs) + len(ops) :]
        for k, op in enumerate(ops):
            op.bind(given[k] if k in given else outs[chained[k]], outs[k], rest[: counts[k]])
            rest = rest[counts[k] :]
        meet(ops)
        for op, step in plan:
            ops[op].step(step)

    outs = [op.out() for op in ops]
    return pl.pallas_call(
        body,
        name=name,
        out_shape=[shape for shape, _ in outs],
        in_specs=[ops[k].in_spec() for k in inputs],
        out_specs=[spec for _, spec in outs],
        scratch_shapes=[entry for op in ops for entry in op.scratch()],
        compiler_params=pltpu.CompilerParams(
            collective_id=number, has_side_effects=True, vmem_limit_bytes=56 * 2**20
        ),
    )(*arrays)


def expert_of(column):
    lane = jnp.zeros(column.shape, jnp.int32)
    for e in range(EXPERTS):
        low = (NS + e) * ROOM
        lane = jnp.where((column >= low) & (column < low + ROOM), PICK_LANE + e, lane)
    return lane


def two_terms(values):
    high = values.astype(bf16)
    return high, (values - high.astype(f32)).astype(bf16)


def expert_kernel(
    hidden_own,
    weights,
    router_t,
    down,
    cot_all,
    attention_weights,
    sum_out,
    mixed_out,
    gate_up_sum,
    down_sum,
    hidden,
    gate_up,
    down_w,
    sums,
    stage,
    cot_column,
    acts,
    wide,
    gates_up,
    raw,
    gates,
    dense_terms,
    reached,
    spread,
    collect,
    picks,
    running,
    load_sem,
    in_sem,
    turn_sem,
    gate_up_sems,
    down_sems,
    *rest,
):
    gather, scatter = Gather("dp", ROWS, D), Scatter("dp", ROWS, D + ROWS)
    gather.bind(hidden_own, hidden, rest[:3])
    scatter.bind(sums, sum_out, rest[3:])
    gate_up_op, down_op = Scatter("sp", GU_PART, D, bf16), Scatter("sp", DN_PART, D, bf16)
    views, at = [], 0
    for size in gate_up_op.sizes() + down_op.sizes() + [DN_PART] * 4:
        views.append(hidden.at[pl.ds(at, size)])
        at += size
    gate_up_op.bind(gate_up, gate_up_sum, [gate_up_sems.at[0], gate_up_sems.at[1], *views[:8], running])
    down_op.bind(down_w, down_sum, [down_sems.at[0], down_sems.at[1], *views[8:16], views[16:]])
    loads = [
        pltpu.make_async_copy(down, down_w, load_sem.at[2]),
        pltpu.make_async_copy(weights, sums.at[pl.ds(0, 2 * HALF), pl.ds(0, D)], load_sem.at[0]),
        pltpu.make_async_copy(attention_weights.at[:, pl.ds(MISC_AT, ROWS)], picks, load_sem.at[1]),
    ]
    for load in loads:
        load.start()

    def chunk(i):
        return pl.ds(pl.multiple_of(i * CHUNK, CHUNK), CHUNK)

    def columns(n):
        return pl.ds(pl.multiple_of(n * 256, 256), 256)

    def fetch(i):
        return pltpu.make_async_copy(cot_all.at[chunk(i)], stage.at[i % 2], in_sem.at[i % 2])

    def put(i):
        return pltpu.make_async_copy(stage.at[i % 2], mixed_out.at[chunk(i)], in_sem.at[i % 2])

    def fetch_column(n):
        return pltpu.make_async_copy(cot_all.at[:, columns(n)], cot_column.at[n % 2], in_sem.at[2 + n % 2])

    fetch(0).start()
    fetch_column(0).start()
    meet([gather, gate_up_op])
    gather.step(0)
    gate_up[pl.ds(HALF, 16), :] = router_t[...]
    gate_up[pl.ds(HALF + 16, FULL - HALF - 16), :] = jnp.zeros((FULL - HALF - 16, D), bf16)
    gate_up[pl.ds(FULL + HALF, FULL - HALF), :] = jnp.zeros((FULL - HALF, D), bf16)
    row = lax.broadcasted_iota(jnp.int32, (ROWS, FULL), 0)
    lane_of = expert_of(lax.broadcasted_iota(jnp.int32, (ROWS, FULL), 1))
    hot = (row == lane_of).astype(bf16)
    spread[:ROWS, :] = hot
    spread[ROWS:, :] = hot
    lane = lax.broadcasted_iota(jnp.int32, (FULL, ROWS), 1)
    hot = (lane == expert_of(lax.broadcasted_iota(jnp.int32, (FULL, ROWS), 0))).astype(bf16)
    collect[:FULL, :] = hot
    collect[FULL:, :] = hot
    loads[0].wait()

    @pl.loop(0, 8)
    def _(i):
        @pl.when(i < 7)
        def _():
            fetch(i + 1).start()

        fetch(i).wait()
        raw[chunk(i), :] = nt(stage[i % 2], down_w[...])

    wait_all(loads[1:])
    for k in range(2 * SETS):
        for part in range(SP):
            units = sums[part * RELAY + k * UNITS : part * RELAY + (k + 1) * UNITS, :D]
            at = k // SETS * FULL + k % SETS * ROOM + part * UNITS
            gate_up[at : at + UNITS, :] = units
    gather.local().wait()

    def at_least(i, k):
        return (i + 8 - k) // 8

    def chip_of(i):
        pair = i // 3 - i // 4 + i // 5 - i // 6
        ring = 3 * at_least(i, 1) - 2 * at_least(i, 2) - at_least(i, 3) + 2 * at_least(i, 4)
        ring = ring + at_least(i, 5) - 2 * at_least(i, 6) + at_least(i, 7)
        seat = gather.seat
        return ((seat.ring + ring) % 4) * 2 + (seat.pair + pair) % 2

    @pl.loop(0, 8)
    def _(i):
        for step, when in ((1, 1), (2, 1), (3, 3), (4, 5)):

            @pl.when(i == when)
            def _():
                gather.step(step)

        chip = chip_of(i)
        rows = chunk(chip)
        landed = block_of(hidden, chip * CHUNK + (1 - gather.seat.core) * ROWS, ROWS)
        remote(
            landed,
            landed,
            gather.send_sem.at[8 + i],
            gather.recv_sem.at[8 + i],
            gather.seat.device(gather.seat.index(0, 0, 1)),
        ).wait_recv()
        gates_up[...] = nt(hidden[rows, :], gate_up[...])
        lane = lax.broadcasted_iota(jnp.int32, (CHUNK, ROWS), 1)
        valid = (lane >= PICK_LANE) & (lane < PICK_LANE + EXPERTS)
        logits = jnp.where(valid, gates_up[:, FULL - ROWS : FULL], -1e30)
        top = jnp.max(logits, axis=1, keepdims=True)
        router = jnp.where(valid, jnp.exp(logits - top), 0.0)
        router = router / jnp.sum(router, axis=1, keepdims=True)
        dense_terms[:, :ROWS], dense_terms[:, ROWS:] = two_terms(router * picks[rows, :].astype(f32))
        gates[...] = nn(dense_terms[...], spread[...])

        @pl.loop(0, CHUNK // 32)
        def _(k):
            at = pl.ds(pl.multiple_of(k * 32, 32), 32)
            there = pl.ds(pl.multiple_of(chip * CHUNK + k * 32, 32), 32)
            column = lax.broadcasted_iota(jnp.int32, (32, FULL), 1)
            factor = jnp.where(column < NS * ROOM, 1.0, gates[at, :])
            gate, up, raw_grad = gates_up[at, :FULL], gates_up[at, FULL:], raw[there, :]
            sig = 1.0 / (1.0 + jnp.exp(-gate))
            silu = gate * sig
            act = silu * up
            acts[there, :] = (act.astype(bf16).astype(f32) * factor).astype(bf16)
            reached[at, :FULL], reached[at, FULL:] = two_terms(act * raw_grad)
            act_grad = raw_grad * factor
            wide[there, :FULL] = (act_grad * up * sig * (1.0 + gate * (1.0 - sig))).astype(bf16)
            wide[there, FULL:] = (act_grad * silu).astype(bf16)

        sums[rows, D:] = nn(reached[...], collect[...]).astype(bf16)
        sums[rows, :D] = nn(wide[rows, :], gate_up[...]).astype(bf16)

    def gate_up_grads(first, last):
        @pl.loop(first, last)
        def _(n):
            made = tn(wide[...], hidden[:, columns(n)]).astype(bf16)
            gate_up[:HALF, columns(n)] = made[:HALF]
            gate_up[HALF : 2 * HALF, columns(n)] = made[FULL : FULL + HALF]

    def down_grads(first, last):
        @pl.loop(first, last)
        def _(n):
            @pl.when(n < D // 256 - 1)
            def _():
                fetch_column(n + 1).start()

            fetch_column(n).wait()
            down_w[:, columns(n)] = tn(acts[...], cot_column[n % 2]).astype(bf16)

    def outputs(first, last):
        @pl.loop(first, last)
        def _(i):
            @pl.when(i >= 2)
            def _():
                put(i - 2).wait()

            stage[i % 2] = nn(acts[chunk(i), :], down_w[...]).astype(bf16)
            put(i).start()

    scatter.step(0)
    gate_up_grads(0, 6)
    scatter.step(1)
    gate_up_grads(6, 8)
    gather.step(5, shared=False)
    seat = gate_up_op.seat
    for partner in gate_up_op.partners(seat):
        pl.semaphore_signal(
            turn_sem, inc=1, device_id=seat.device(partner), device_id_type=pl.DeviceIdType.MESH
        )
    scatter.step(2)
    outputs(0, 2)
    pl.semaphore_wait(turn_sem, len(NEAR))
    gate_up_op.step(0)
    outputs(2, 6)
    scatter.step(3)
    outputs(6, 8)
    put(6).wait()
    put(7).wait()
    down_grads(0, 8)
    down_op.step(0)
    gate_up_op.step(1)
    gate_up_op.step(2)
    scatter.step(4)
    gate_up_op.step(3)
    for step in (1, 2, 3):
        down_op.step(step)
    gate_up_op.step(4)
    down_op.step(4)
    gate_up_op.step(5)
    down_op.step(5)
    scatter.step(5)


def experts(*arrays):
    any_spec, vmem = pl.BlockSpec(memory_space=pl.ANY), pl.BlockSpec(memory_space=pltpu.VMEM)
    gather, scatter = Gather("dp", ROWS, D), Scatter("dp", ROWS, D + ROWS)
    flops = 2 * GROUP * D * FULL * 9
    return pl.pallas_call(
        expert_kernel,
        name="experts",
        out_shape=[
            jax.ShapeDtypeStruct((ROWS, D + ROWS), f32),
            jax.ShapeDtypeStruct((GROUP, D), bf16),
            jax.ShapeDtypeStruct((GU_PART, D), bf16),
            jax.ShapeDtypeStruct((DN_PART, D), bf16),
        ],
        in_specs=[any_spec, any_spec, vmem, any_spec, any_spec, any_spec],
        out_specs=[vmem, any_spec, vmem, vmem],
        scratch_shapes=[
            pltpu.VMEM((GROUP, D), bf16),
            pltpu.VMEM((2 * FULL, D), bf16),
            pltpu.VMEM((FULL, D), bf16),
            pltpu.VMEM((GROUP, D + ROWS), bf16),
            pltpu.VMEM((2, CHUNK, D), bf16),
            pltpu.VMEM((2, GROUP, 256), bf16),
            pltpu.VMEM((GROUP, FULL), bf16),
            pltpu.VMEM((GROUP, 2 * FULL), bf16),
            pltpu.VMEM((CHUNK, 2 * FULL), f32),
            pltpu.VMEM((GROUP, FULL), f32),
            pltpu.VMEM((CHUNK, FULL), f32),
            pltpu.VMEM((CHUNK, 2 * ROWS), bf16),
            pltpu.VMEM((CHUNK, 2 * FULL), bf16),
            pltpu.VMEM((2 * ROWS, FULL), bf16),
            pltpu.VMEM((2 * FULL, ROWS), bf16),
            pltpu.VMEM((GROUP, ROWS), bf16),
            pltpu.VMEM((4, GU_PART, D), bf16),
            pltpu.SemaphoreType.DMA((3,)),
            pltpu.SemaphoreType.DMA((4,)),
            pltpu.SemaphoreType.REGULAR,
            pltpu.SemaphoreType.DMA((2, 17)),
            pltpu.SemaphoreType.DMA((2, 17)),
        ]
        + gather.scratch()
        + scatter.scratch(),
        compiler_params=pltpu.CompilerParams(
            collective_id=2, has_side_effects=True, vmem_limit_bytes=61 * 2**20
        ),
        cost_estimate=pl.CostEstimate(flops=flops, bytes_accessed=40 * 2**20, transcendentals=GROUP * FULL),
    )(*arrays)


def wait_all(copies):
    for copy in copies:
        copy.wait()


def swap_halves(values):
    lane = lax.broadcasted_iota(jnp.int32, values.shape, 1) % ROPE
    return jnp.where(lane < ROPE // 2, pltpu.roll(values, 96, 1), pltpu.roll(values, 32, 1))


def causal(scores):
    rows, seen = scores.shape
    row = lax.broadcasted_iota(jnp.int32, (rows, rows), 0)
    column = lax.broadcasted_iota(jnp.int32, (rows, rows), 1)
    last = jnp.where(column <= row, scores[:, seen - rows :], -1e9)
    return last if seen == rows else jnp.concatenate([scores[:, : seen - rows], last], axis=1)


def attention_ops():
    return (
        Gather("sp", ROWS, D, spare=True),
        Gather("dp", ROWS, PACK),
        Gather("dp", ROWS, D, spare=True),
        Gather("dp", ROWS, D, spare=True),
        Swap(
            "dp",
            (RELAY, D),
            lambda ref, j: ref.at[j],
            lambda ref, j: ref.at[:, pl.ds(pl.multiple_of(j * ROWS, ROWS), ROWS)],
        ),
        Gather("sp", RELAY, D),
        Swap(
            "sp",
            (ROWS, D),
            lambda ref, j: ref.at[pl.ds(pl.multiple_of(j * ROWS, ROWS), ROWS)],
            lambda ref, j: ref.at[:, pl.ds(pl.multiple_of(j * OW, OW), OW)],
        ),
    )


def attention_kernel(
    tokens,
    pack,
    cotangent,
    shared_gate,
    expert_gate,
    shared_up,
    expert_up,
    shared_down,
    expert_down,
    out_own,
    cosine,
    sine,
    resid_two,
    hidden_two,
    cot_all,
    gate_up_part,
    gate_up,
    down_out,
    tok_out,
    weights_out,
    hidden_out,
    compressed_out,
    latent_out,
    query_out,
    key_out,
    value_out,
    head_out,
    out_w_out,
    misc_out,
    total_out,
    tok,
    weights,
    hidden,
    qc,
    latent,
    up_w,
    query,
    key,
    value,
    tok_heads,
    out_w,
    misc_t,
    totals,
    heads,
    pieces,
    down,
    gate_shared,
    gate_routed,
    up_shared,
    up_routed,
    down_shared,
    down_routed,
    save_sem,
    load_sem,
    *rest,
):
    ops = attention_ops()
    tok_op, pack_op, out_op, cot_op, piece_op, gate_up_op, head_op = ops
    bound = (
        (tokens, tok),
        (pack, weights),
        (out_own, out_w),
        (cotangent, cot_all),
        (pieces, gate_up_part),
        (gate_up_part, gate_up),
        (heads, tok_heads),
    )
    for op, (src, dst) in zip(ops, bound):
        count = len(op.scratch())
        op.bind(src, dst, rest[:count])
        rest = rest[count:]
    loads = [
        pltpu.make_async_copy(src, dst, load_sem.at[k])
        for k, (src, dst) in enumerate(
            (
                (shared_gate, gate_shared),
                (expert_gate, gate_routed),
                (shared_up, up_shared),
                (expert_up, up_routed),
                (shared_down, down_shared),
                (expert_down, down_routed),
            )
        )
    ]
    for load in loads:
        load.start()
    meet(ops)
    tok_op.step(0)
    pack_op.step(0)
    out_op.step(0)
    for step in (1, 2):
        tok_op.step(step)
        pack_op.step(step)

    wait_all(loads)
    row = lax.broadcasted_iota(jnp.int32, (DP * UNITS, FE), 0)
    column = lax.broadcasted_iota(jnp.int32, (DP * UNITS, FE), 1)
    group, unit = row // UNITS, row - row // UNITS * UNITS + tok_op.seat.own * UNITS
    pick = ((group * SLICE + unit == column) & (unit < SLICE)).astype(bf16)
    for k, (shared, routed) in enumerate(((gate_shared, gate_routed), (up_shared, up_routed))):
        for e in range(SETS):
            piece = shared[:, e, :] if e < NS else routed[:, e - NS, :]
            piece = nt(pick, piece).astype(bf16)
            at = (k * SETS + e) * UNITS
            for d in range(DP):
                pieces[d, at : at + UNITS, :] = piece[d * UNITS : (d + 1) * UNITS]
        if k == 0:
            tok_op.step(3)
            pack_op.step(3)
            out_op.step(1)
            out_op.step(2)
    piece_op.step(0)
    pack_op.step(4)
    pack_op.step(5)
    cot_op.step(0)
    tok_op.local().wait()
    saves = [
        pltpu.make_async_copy(src, dst, save_sem.at[k])
        for k, (src, dst) in enumerate(
            (
                (tok, tok_out),
                (weights, weights_out),
                (hidden, hidden_out),
                (qc.at[:, pl.ds(QW, RANK)], compressed_out),
                (latent, latent_out),
                (query, query_out),
                (key, key_out),
                (value, value_out),
                (tok_heads, head_out),
                (out_w, out_w_out),
                (misc_t, misc_out),
                (totals, total_out),
            )
        )
    ]
    saves[1].start()
    misc_t[...] = weights[:, MISC_AT:CORE_W].astype(f32).T
    up = weights[:, UP_AT:].reshape(DP, 4, RANK // DP, ROWS)
    for k in range(4):
        up_w[:, k * ROWS : (k + 1) * ROWS] = up[:, k].reshape(RANK, ROWS)
    each = RANK // DP
    for d in range(DP):
        misc_t[0:1, d * each : (d + 1) * each] = misc_t[GAIN_KV : GAIN_KV + 1, d * ROWS : d * ROWS + each]
    kv_gain = misc_t[0:1, :RANK]
    saves[10].start()
    gain = misc_t[GAIN_ONE : GAIN_ONE + 1, :]

    def project(*places):
        for place in places:
            start = tok_op.seat.index(*place) * ROWS

            @pl.loop(0, ROWS // 32)
            def _(k):
                at = pl.ds(pl.multiple_of(start + k * 32, 32), 32)
                values = tok[at, :].astype(f32)
                hidden[at, :] = (values * inverse_rms(values) * gain).astype(bf16)

            at = pl.ds(pl.multiple_of(start, ROWS), ROWS)
            qc[at, :] = nn(hidden[at, :], weights[:, :CORE_W])

    project((0, 0), (0, -1), (0, 1), (1, 0), (0, 2))
    tok_op.step(4)
    piece_op.step(5)
    gate_up_op.step(0)
    out_op.step(3)
    project((1, -1), (1, 1), (1, 2))
    tok_op.step(5, shared=False)
    for k in (0, 2, 3):
        saves[k].start()

    @pl.loop(0, SEQ // 256)
    def _(k):
        at = pl.ds(pl.multiple_of(k * 256, 256), 256)
        inner = qc[at, QW : QW + RANK]
        latent[at, :] = (inner * inverse_rms(inner) * kv_gain).astype(bf16)
        ropes, key_rope = qc[at, 2 * NOPE : QW], qc[at, MISC_AT:CORE_W]
        cos, sin = cosine[at, :], sine[at, :]
        ropes = (ropes * cos + swap_halves(ropes) * sin).astype(bf16)
        key_rope = key_rope * cos + swap_halves(key_rope) * sin
        lane = lax.broadcasted_iota(jnp.int32, key_rope.shape, 1)
        key_rope = jnp.where(lane < ROPE, key_rope, 0.0)
        expanded = nn(latent[at, :], up_w[...]).astype(bf16)
        for h in range(HEADS_HERE):
            query[h, at, :NOPE] = qc[at, h * NOPE : (h + 1) * NOPE].astype(bf16)
            query[h, at, NOPE:] = ropes
            turned = key_rope if h == 0 else pltpu.roll(key_rope, ROPE, 1)
            key[h, at, NOPE:] = turned.astype(bf16)
            base = h * (NOPE + VDIM)
            key[h, at, :NOPE] = expanded[:, base : base + NOPE]
            value[h, at, :] = expanded[:, base + NOPE : base + NOPE + VDIM]

    for k in (4, 5, 6, 7):
        saves[k].start()
    gate_up_op.step(1)
    gate_up_op.step(2)
    out_op.step(4)
    cot_op.step(1)
    cot_op.step(2)
    for h in range(HEADS_HERE):
        for i in range(SEQ // 256):
            at, seen = pl.ds(i * 256, 256), (i + 1) * 256
            scores = causal(nt(query[h, at, :], key[h, :seen, :]) * SCALE)
            top = jnp.max(scores, axis=1, keepdims=True)
            parts = jnp.exp(scores - top)
            total = jnp.sum(parts, axis=1, keepdims=True)
            probs = (parts * (1.0 / total)).astype(bf16)
            heads[at, h * VDIM : (h + 1) * VDIM] = nn(probs, value[h, :seen, :]).astype(bf16)
            totals[h, at, :] = jnp.broadcast_to(top + jnp.log(total), (256, ROWS))
        if h == 0:
            gate_up_op.step(3)
    head_op.step(0)
    saves[11].start()
    cot_op.step(3)
    for e in range(SETS):
        part = down_shared[:, e, :] if e < NS else down_routed[:, e - NS, :]
        down[e * ROOM : e * ROOM + SLICE, :] = part
        down[e * ROOM + SLICE : (e + 1) * ROOM, :] = jnp.zeros((ROOM - SLICE, D), bf16)
    down[HALF:, :] = jnp.zeros((FULL - HALF, D), bf16)
    down_save = pltpu.make_async_copy(down, down_out, load_sem.at[0])
    down_save.start()
    gate_up_op.step(4)
    out_op.step(5)
    saves[9].start()
    head_op.step(5)
    saves[8].start()
    own = tok_op.view((0, 0))[...].astype(f32)
    resid = own + nn(tok_heads[...], out_w[...])
    resid_two[...] = resid
    hidden_two[...] = (resid * inverse_rms(resid) * misc_t[GAIN_TWO : GAIN_TWO + 1, :]).astype(bf16)
    cot_op.step(4)
    wait_all(saves + [down_save])
    cot_op.step(5)
    gate_up_op.step(5)


def attention(*arrays):
    any_spec, vmem = pl.BlockSpec(memory_space=pl.ANY), pl.BlockSpec(memory_space=pltpu.VMEM)
    kept = [
        ((SEQ, D), bf16),
        ((D, PACK), bf16),
        ((SEQ, D), bf16),
        ((SEQ, RANK), f32),
        ((SEQ, RANK), bf16),
        ((HEADS_HERE, SEQ, 2 * NOPE), bf16),
        ((HEADS_HERE, SEQ, 2 * NOPE), bf16),
        ((HEADS_HERE, SEQ, VDIM), bf16),
        ((ROWS, D), bf16),
        ((D, D), bf16),
        ((ROWS, D), f32),
        ((HEADS_HERE, SEQ, ROWS), f32),
    ]
    made = [((ROWS, D), f32), ((ROWS, D), bf16), ((GROUP, D), bf16), ((RELAY, D), bf16), ((SP * RELAY, D), bf16), ((FULL, D), bf16)]
    scratch = kept[:3] + [((SEQ, CORE_W), f32), kept[4], ((RANK, KVW), bf16)] + kept[5:]
    scratch = scratch + [((SEQ, OW), bf16), ((DP, RELAY, ROWS), bf16), ((FULL, D), bf16)]
    scratch = scratch + [(array.shape, bf16) for array in arrays[3:9]]
    return pl.pallas_call(
        attention_kernel,
        name="attention",
        out_shape=[jax.ShapeDtypeStruct(*shape) for shape in made + kept],
        in_specs=[any_spec] * 10 + [vmem] * 2,
        out_specs=[vmem] * 2 + [any_spec] * (len(made) + len(kept) - 2),
        scratch_shapes=[pltpu.VMEM(*shape) for shape in scratch]
        + [pltpu.SemaphoreType.DMA((len(kept),)), pltpu.SemaphoreType.DMA((6,))]
        + [entry for op in attention_ops() for entry in op.scratch()],
        compiler_params=pltpu.CompilerParams(
            collective_id=0, has_side_effects=True, vmem_limit_bytes=60 * 2**20
        ),
        cost_estimate=pl.CostEstimate(
            flops=2 * SEQ * D * (CORE_W + OW), bytes_accessed=60 * 2**20, transcendentals=SEQ * SEQ
        ),
    )(*arrays)


def attention_grad_ops():
    return (
        Gather("dp", ROWS, D, spare=True),
        Swap(
            "dp",
            (DP * GU_PART, ROWS),
            lambda ref, j: ref.at[:, pl.ds(pl.multiple_of(j * ROWS, ROWS), ROWS)],
            lambda ref, j: ref.at[pl.ds(pl.multiple_of(j * GU_PART, GU_PART), GU_PART)],
        ),
        Gather("sp", DP * GU_PART, ROWS),
        Gather("sp", DN_PART, D),
        Swap(
            "dp",
            (GROUP, ROWS),
            lambda ref, j: ref.at[:, pl.ds(pl.multiple_of(j * ROWS, ROWS), ROWS)],
            lambda ref, j: ref.at[pl.ds(pl.multiple_of(j * ROWS, ROWS), ROWS)],
        ),
        Swap(
            "sp",
            (SEQ, OW),
            lambda ref, j: ref.at[:, pl.ds(pl.multiple_of(j * OW, OW), OW)],
            lambda ref, j: ref.at[pl.ds(pl.multiple_of(j * ROWS, ROWS), ROWS)],
        ),
    )


def attention_grad_kernel(
    proj_own,
    tok_all,
    weights_all,
    hidden_all,
    compressed_all,
    latent_all,
    query_all,
    key_all,
    value_all,
    head_all,
    out_w_all,
    misc_all,
    total_all,
    gate_up_sum,
    down_sum,
    cosine,
    sine,
    norm_rows,
    hidden_part,
    gate_up_piece,
    gate_up_total,
    down_total,
    grads,
    proj_all,
    out_grad,
    tok,
    weights,
    hidden,
    compressed,
    latent,
    query,
    key,
    value,
    proj,
    out_w,
    head_own,
    head_cols,
    misc_t,
    totals,
    up_w,
    head_grad,
    key_grad,
    value_grad,
    rope_grad,
    expanded_grad,
    qc_grad,
    scale_one,
    misc_grad,
    up_grad,
    made_w,
    made_h,
    load_sem,
    out_sem,
    *rest,
):
    ops = attention_grad_ops()
    proj_op, piece_op, gate_up_op, down_op, out_op, head_op = ops
    bound = (
        (proj_own, proj_all),
        (gate_up_sum, gate_up_piece),
        (gate_up_piece, gate_up_total),
        (down_sum, down_total),
        (head_all, head_cols),
        (head_own, head_grad),
    )
    for op, (src, dst) in zip(ops, bound):
        count = len(op.scratch())
        op.bind(src, dst, rest[:count])
        rest = rest[count:]
    loads = [
        pltpu.make_async_copy(src, dst, load_sem.at[k])
        for k, (src, dst) in enumerate(
            (
                (proj_own, proj),
                (out_w_all, out_w),
                (tok_all, tok),
                (query_all, query),
                (key_all, key),
                (value_all, value),
                (total_all, totals),
                (weights_all, weights),
                (compressed_all, compressed),
                (latent_all, latent),
                (misc_all, misc_t),
                (hidden_all, hidden),
            )
        )
    ]
    for load in loads:
        load.start()
    meet(ops)
    wait_all(loads[:2])
    head_own[...] = nt(proj[...], out_w[...]).astype(bf16)
    head_op.step(0)
    piece_op.step(0)
    down_op.step(0)
    proj_op.step(0)
    out_op.step(0)
    wait_all(loads[2:])

    @pl.loop(0, SEQ // 32)
    def _(k):
        at = pl.ds(pl.multiple_of(k * 32, 32), 32)
        scale_one[at, :] = inverse_rms(tok[at, :].astype(f32))

    up = weights[:, UP_AT:].reshape(DP, 4, RANK // DP, ROWS)
    for k in range(4):
        up_w[:, k * ROWS : (k + 1) * ROWS] = up[:, k].reshape(RANK, ROWS)
    head_op.step(5)
    piece_op.step(5)
    gate_up_op.step(0)
    for h in range(HEADS_HERE):
        for i in reversed(range(SEQ // 256)):
            at, seen = pl.ds(i * 256, 256), (i + 1) * 256
            piece = head_grad[at, h * VDIM : (h + 1) * VDIM]
            scores = causal(nt(query[h, at, :], key[h, :seen, :]) * SCALE)
            probs = jnp.exp(scores - totals[h, at, 0:1])
            dprob = nt(piece, value[h, :seen, :])
            delta = jnp.sum(probs * dprob, axis=1, keepdims=True)
            score_grad = (probs * (dprob - delta) * SCALE).astype(bf16)
            query_grad = nn(score_grad, key[h, :seen, :]).astype(bf16)
            qc_grad[at, h * NOPE : (h + 1) * NOPE] = query_grad[:, :NOPE]
            turned = query_grad[:, NOPE:].astype(f32)
            rope_grad[at, :] = turned if h == 0 else rope_grad[at, :] + turned
            from_query = tn(score_grad, query[h, at, :])
            from_out = tn(probs.astype(bf16), piece)
            if i == SEQ // 256 - 1:
                key_grad[h, :seen, :] = from_query
                value_grad[h, :seen, :] = from_out
            else:
                key_grad[h, :seen, :] += from_query
                value_grad[h, :seen, :] += from_out
        if h == 0:
            down_op.step(1)
            down_op.step(2)
            proj_op.step(1)
            proj_op.step(2)
    down_op.step(3)
    proj_op.step(3)
    kv_gain = misc_t[0:1, :RANK]
    lane = lax.broadcasted_iota(jnp.int32, (128, ROWS), 1)

    @pl.loop(0, SEQ // 128)
    def _(k):
        at = pl.ds(pl.multiple_of(k * 128, 128), 128)
        cos, sin = cosine[at, :], sine[at, :]
        ropes = rope_grad[at, :]
        qc_grad[at, 2 * NOPE : QW] = (ropes * cos - swap_halves(ropes) * sin).astype(bf16)
        key_rope = jnp.zeros((128, ROWS), f32)
        for h in range(HEADS_HERE):
            base = h * (NOPE + VDIM)
            expanded_grad[at, base : base + NOPE] = key_grad[h, at, :NOPE].astype(bf16)
            expanded_grad[at, base + NOPE : base + NOPE + VDIM] = value_grad[h, at, :].astype(bf16)
            turned = key_grad[h, at, NOPE:].astype(bf16).astype(f32)
            turned = turned if h == 0 else pltpu.roll(turned, ROPE, 1)
            key_rope = key_rope + jnp.where(lane < ROPE, turned, 0.0)
        key_rope = key_rope * cos - swap_halves(key_rope) * sin
        qc_grad[at, MISC_AT:CORE_W] = jnp.where(lane < ROPE, key_rope, 0.0).astype(bf16)

    made = tn(latent[...], expanded_grad[...]).astype(bf16)
    each = RANK // DP
    for d in range(DP):
        for k in range(4):
            at = pl.ds(d * ROWS + k * each, each)
            up_grad[at, :] = made[d * each : (d + 1) * each, k * ROWS : (k + 1) * ROWS]
    up_store = pltpu.make_async_copy(up_grad, grads.at[:, pl.ds(UP_AT, ROWS)], out_sem.at[2])
    up_store.start()
    misc_grad[...] = jnp.zeros_like(misc_grad)
    misc_grad[64:72, :] = norm_rows[...]
    kv_total = jnp.zeros((1, RANK), f32)
    for k in range(SEQ // 256):
        at = pl.ds(k * 256, 256)
        inner = compressed[at, :]
        scale = inverse_rms(inner)
        latent_grad = nt(expanded_grad[at, :], up_w[...])
        kv_total = kv_total + jnp.sum(latent_grad * inner * scale, axis=0, keepdims=True)
        qc_grad[at, QW : QW + RANK] = norm_back(inner, scale, kv_gain, latent_grad).astype(bf16)
    for d in range(DP):
        misc_grad[66:67, d * ROWS : d * ROWS + each] = kv_total[:, d * each : (d + 1) * each]
    gate_up_op.step(1)
    gate_up_op.step(2)

    def put(n):
        at = pl.ds(pl.multiple_of(n * TILE, TILE), TILE)
        return pltpu.make_async_copy(made_h.at[n % 2], hidden_part.at[:, at], out_sem.at[n % 2])

    @pl.loop(0, D // TILE)
    def _(n):
        at = pl.ds(pl.multiple_of(n * TILE, TILE), TILE)

        @pl.when(n >= 2)
        def _():
            put(n - 2).wait()

        grad = nt(qc_grad[...], weights[at, :CORE_W])
        made_h[n % 2] = grad.astype(bf16)
        put(n).start()
        grad = grad * tok[:, at].astype(f32) * scale_one[...]
        misc_grad[64:65, at] = jnp.sum(grad, axis=0, keepdims=True)

    put(2).wait()
    put(3).wait()
    gate_up_op.step(3)
    proj_op.step(4)
    down_op.step(4)
    def store(n):
        at = pl.ds(pl.multiple_of(n * TILE, TILE), TILE)
        return pltpu.make_async_copy(
            made_w.at[n % 2], grads.at[at, pl.ds(0, CORE_W)], out_sem.at[n % 2]
        )

    @pl.loop(0, D // TILE)
    def _(n):
        at = pl.ds(pl.multiple_of(n * TILE, TILE), TILE)

        @pl.when(n >= 2)
        def _():
            store(n - 2).wait()

        made = tn(hidden[:, at], qc_grad[...])
        made_w[n % 2, :, :MISC_AT] = made[:, :MISC_AT].astype(bf16)
        made_w[n % 2, :, MISC_AT:] = (made[:, MISC_AT:] + misc_grad[:, at].T).astype(bf16)
        store(n).start()

    store(2).wait()
    store(3).wait()
    up_store.wait()
    proj_op.step(5)
    out_op.step(5)

    def half(n, k):
        rows, at = pl.ds(k * SEQ, SEQ), pl.ds(n * TILE, TILE)
        return pltpu.make_async_copy(proj_all.at[rows, at], made_h.at[k], out_sem.at[k])

    half(0, 0).start()
    half(0, 1).start()
    for n in range(D // TILE):
        total = 0.0
        for k in range(2):
            half(n, k).wait()
            total = total + tn(head_cols[pl.ds(k * SEQ, SEQ), :], made_h[k])
            if n < D // TILE - 1:
                half(n + 1, k).start()
        rows, at = pl.ds(n // 2 * ROWS, ROWS), pl.ds(n % 2 * TILE, TILE)
        out_grad[rows, at] = total.astype(bf16)

    gate_up_op.step(4)
    gate_up_op.step(5)
    down_op.step(5)


def attention_grad(*arrays):
    any_spec, vmem = pl.BlockSpec(memory_space=pl.ANY), pl.BlockSpec(memory_space=pltpu.VMEM)
    scratch = [
        ((SEQ, D), bf16),
        ((D, PACK), bf16),
        ((SEQ, D), bf16),
        ((SEQ, RANK), f32),
        ((SEQ, RANK), bf16),
        ((HEADS_HERE, SEQ, 2 * NOPE), bf16),
        ((HEADS_HERE, SEQ, 2 * NOPE), bf16),
        ((HEADS_HERE, SEQ, VDIM), bf16),
        ((ROWS, D), bf16),
        ((D, D), bf16),
        ((ROWS, D), bf16),
        ((GROUP, ROWS), bf16),
        ((ROWS, D), f32),
        ((HEADS_HERE, SEQ, ROWS), f32),
        ((RANK, KVW), bf16),
        ((SEQ, OW), bf16),
        ((HEADS_HERE, SEQ, 2 * NOPE), f32),
        ((HEADS_HERE, SEQ, VDIM), f32),
        ((SEQ, ROWS), f32),
        ((SEQ, KVW), bf16),
        ((SEQ, CORE_W), bf16),
        ((SEQ, 1), f32),
        ((ROWS, D), f32),
        ((D, ROWS), bf16),
        ((2, TILE, CORE_W), bf16),
        ((2, SEQ, TILE), bf16),
    ]
    return pl.pallas_call(
        attention_grad_kernel,
        name="attention_grad",
        out_shape=[
            jax.ShapeDtypeStruct((SEQ, D), bf16),
            jax.ShapeDtypeStruct((DP * GU_PART, ROWS), bf16),
            jax.ShapeDtypeStruct((SP * DP * GU_PART, ROWS), bf16),
            jax.ShapeDtypeStruct((FULL, D), bf16),
            jax.ShapeDtypeStruct((D, PACK), bf16),
            jax.ShapeDtypeStruct((GROUP, D), bf16),
            jax.ShapeDtypeStruct((2 * ROWS, D // 2), bf16),
        ],
        in_specs=[any_spec] * 15 + [vmem] * 3,
        out_specs=[any_spec] * 6 + [vmem],
        scratch_shapes=[pltpu.VMEM(*shape) for shape in scratch]
        + [pltpu.SemaphoreType.DMA((12,)), pltpu.SemaphoreType.DMA((3,))]
        + [entry for op in attention_grad_ops() for entry in op.scratch()],
        compiler_params=pltpu.CompilerParams(
            collective_id=4, has_side_effects=True, vmem_limit_bytes=61 * 2**20
        ),
        cost_estimate=pl.CostEstimate(
            flops=6 * SEQ * D * CORE_W, bytes_accessed=60 * 2**20, transcendentals=SEQ * SEQ
        ),
    )(*arrays)


def unpack_kernel(
    gate_up, down, gate_shared, up_shared, gate_routed, up_routed, down_shared, down_routed, block, rows, pick, sem
):
    def fetch(k):
        part, skip = divmod(k * ROOM, GU_PART)
        first = min(ROOM, GU_PART - skip)
        pieces = [(part, skip, 0, first)] + ([(part + 1, 0, first, ROOM - first)] if first < ROOM else [])
        return [
            pltpu.make_async_copy(
                gate_up.at[s, :, pl.ds(begin, size)], block.at[k % 2, :, pl.ds(at, size)], sem.at[k % 2, n]
            )
            for n, (s, begin, at, size) in enumerate(pieces)
        ]

    load = pltpu.make_async_copy(down, rows, sem.at[2, 0])
    load.start()
    for copy in fetch(0):
        copy.start()
    row = lax.broadcasted_iota(jnp.int32, pick.shape, 0)
    column = lax.broadcasted_iota(jnp.int32, pick.shape, 1)
    unit = row - row // ROOM * ROOM
    pick[...] = ((row // ROOM * SLICE + unit == column) & (unit < SLICE)).astype(bf16)
    for k in range(2 * SETS):
        if k + 1 < 2 * SETS:
            for copy in fetch(k + 1):
                copy.start()
        for copy in fetch(k):
            copy.wait()
        made = tn(block[k % 2].reshape(DP * ROOM, ROWS), pick[...])
        e = k % SETS
        shared, routed = (gate_shared, gate_routed) if k < SETS else (up_shared, up_routed)
        if e < NS:
            shared[:, e, :] = made
        else:
            routed[:, e - NS, :] = made
    load.wait()
    for e in range(SETS):
        made = rows[e * ROOM : e * ROOM + SLICE, :].astype(f32)
        if e < NS:
            down_shared[:, e, :] = made
        else:
            down_routed[:, e - NS, :] = made


def unpack(gate_up, down):
    any_spec, vmem = pl.BlockSpec(memory_space=pl.ANY), pl.BlockSpec(memory_space=pltpu.VMEM)
    width, height = SLICE, ROWS
    return pl.pallas_call(
        unpack_kernel,
        name="unpack",
        out_shape=[jax.ShapeDtypeStruct((height, n, FE), f32) for n in (NS, NS, EXPERTS, EXPERTS)]
        + [jax.ShapeDtypeStruct((width, n, D), f32) for n in (NS, EXPERTS)],
        in_specs=[any_spec] * 2,
        out_specs=[vmem] * 6,
        scratch_shapes=[
            pltpu.VMEM((2, DP, ROOM, ROWS), bf16),
            pltpu.VMEM((FULL, D), bf16),
            pltpu.VMEM((DP * ROOM, FE), bf16),
            pltpu.SemaphoreType.DMA((3, 2)),
        ],
        compiler_params=pltpu.CompilerParams(vmem_limit_bytes=56 * 2**20),
    )(gate_up, down)


def per_device(
    tokens,
    cotangent,
    chosen,
    attn_gain,
    w_query,
    w_kv_down,
    kv_gain,
    w_kv_up,
    w_out,
    ffn_gain,
    w_router,
    shared_gate,
    shared_up,
    shared_down,
    expert_gate,
    expert_up,
    expert_down,
):
    own_sp = lax.axis_index("sp")
    picks = jnp.any(chosen[:, :, None] == jnp.arange(EXPERTS, dtype=jnp.int32), axis=1).astype(bf16)
    own_query = lax.dynamic_slice_in_dim(w_query, own_sp * QW, QW, 1)
    own_up = lax.dynamic_slice_in_dim(w_kv_up, own_sp * KVW, KVW, 1)
    pack = jnp.concatenate(
        [
            own_query[:, :NOPE],
            own_query[:, QK : QK + NOPE],
            own_query[:, NOPE:QK],
            own_query[:, QK + NOPE :],
            w_kv_down,
            picks,
            attn_gain[:, None],
            ffn_gain[:, None],
            jnp.pad(kv_gain, (0, ROWS - kv_gain.shape[0]))[:, None],
            jnp.zeros((ROWS, 9), bf16),
            w_router,
            jnp.zeros((ROWS, 44), bf16),
            own_up.reshape(RANK // DP, 4, ROWS).transpose(1, 0, 2).reshape(ROWS, ROWS),
        ],
        axis=1,
    )
    cosine, sine = rope_tables()
    (
        resid_two,
        hidden_two,
        cot_all,
        _,
        gate_up,
        down,
        tok_all,
        weights,
        hidden_one,
        compressed,
        latent,
        queries,
        keys,
        values,
        head_out,
        out_w,
        misc,
        log_totals,
    ) = attention(
        tokens,
        pack,
        cotangent,
        shared_gate,
        expert_gate,
        shared_up,
        expert_up,
        shared_down,
        expert_down,
        w_out,
        cosine,
        sine,
    )
    gain_one, gain_two = misc[GAIN_ONE], misc[GAIN_TWO]
    latent_gain = misc[GAIN_KV].reshape(DP, ROWS)[:, : RANK // DP].reshape(RANK)
    router_t = misc[ROUTER_LANE : ROUTER_LANE + 16].astype(bf16)
    router_w = router_t[:EXPERTS]
    scale_two = inverse_rms(resid_two)

    hidden_grad, mixed_part, gate_up_grad, down_grad = experts(
        hidden_two, gate_up, router_t, down, cot_all, weights
    )
    prob_grad = hidden_grad[:, D + PICK_LANE : D + PICK_LANE + EXPERTS]
    hidden_grad = hidden_grad[:, :D]

    logits = nt(hidden_two, router_w)
    router = jax.nn.softmax(logits, axis=-1)
    prob_grad = prob_grad * picks.astype(f32)
    logit_grad = (
        router * (prob_grad - jnp.sum(router * prob_grad, axis=-1, keepdims=True))
    ).astype(bf16)
    hidden_grad = hidden_grad + nn(logit_grad, router_w)
    router_grad = tn(logit_grad, hidden_two)
    gain_two_grad = jnp.sum(hidden_grad * resid_two * scale_two, axis=0)
    upstream = cotangent.astype(f32)
    resid_two_grad = upstream + norm_back(resid_two, scale_two, gain_two, hidden_grad)
    proj_grad = resid_two_grad.astype(bf16)

    norm_rows = jnp.concatenate(
        [
            jnp.zeros((1, D), f32),
            gain_two_grad[None],
            jnp.zeros((1, D), f32),
            router_grad,
            jnp.zeros((1, D), f32),
        ]
    )
    hidden_one_grad, _, gu_total, dn_total, grads, _, out_grad = attention_grad(
        proj_grad,
        tok_all,
        weights,
        hidden_one,
        compressed,
        latent,
        queries,
        keys,
        values,
        head_out,
        out_w,
        misc,
        log_totals,
        gate_up_grad,
        down_grad,
        cosine,
        sine,
        norm_rows,
    )

    _, hidden_one_grad, mixed, grads, _, out_total = exchange(
        "sum_grads",
        6,
        [
            Scatter("dp", ROWS, PACK, bf16, spare=True, load=True),
            Scatter("sp", ROWS, D, load=True),
            Scatter("dp", ROWS, D, spare=True, load=True),
            Gather("sp", ROWS, PACK),
            Scatter("sp", 2 * ROWS // SP, D // 2, bf16),
            Gather("sp", 2 * ROWS // SP, D // 2),
        ],
        [grads, hidden_one_grad, mixed_part, out_grad],
        plan=[(0, 0), (1, 0), (4, 0), (0, 1), (4, 1), (1, 1), (0, 2), (0, 3), (2, 0), (4, 2), (4, 3)]
        + [(1, 2), (0, 4), (3, 0), (4, 4), (5, 0), (1, 3), (2, 1), (3, 1), (3, 2), (5, 1), (5, 2)]
        + [(2, 2), (2, 3), (1, 4), (3, 3), (5, 3), (2, 4), (3, 4), (5, 4)]
        + [(op, 5) for op in range(6)],
        chained=[(3, 0), (5, 4)],
    )
    gate_shared, up_shared, gate_routed, up_routed, down_shared, down_routed = unpack(
        gu_total.reshape(SP, DP, GU_PART, ROWS), dn_total
    )
    grads = grads.reshape(SP, ROWS, PACK)
    mixed = (resid_two + mixed).astype(bf16)
    resid_one = tokens.astype(f32)
    own_scale = inverse_rms(resid_one)
    tokens_grad = resid_two_grad + norm_back(resid_one, own_scale, gain_one, hidden_one_grad)
    tokens_grad = tokens_grad.astype(bf16)

    def side_by_side(block, width):
        return block.astype(f32).transpose(1, 0, 2).reshape(-1, SP * width)

    query_total = grads[:, :, :QW]
    query_total = jnp.concatenate(
        [
            query_total[:, :, :NOPE],
            query_total[:, :, 2 * NOPE : 2 * NOPE + ROPE],
            query_total[:, :, NOPE : 2 * NOPE],
            query_total[:, :, 2 * NOPE + ROPE :],
        ],
        axis=2,
    )
    query_total = side_by_side(query_total, QW)
    tail = jnp.sum(grads[:, :, QW:CORE_W].astype(f32), axis=0)
    down_total, tail = tail[:, : RANK + ROPE], tail[:, RANK + ROPE :]
    out_total = jnp.concatenate([out_total[:ROWS], out_total[ROWS:]], axis=1).astype(f32)
    up_total = grads[:, :, UP_AT:].reshape(SP, 4, RANK // DP, ROWS).transpose(0, 2, 1, 3)
    up_total = side_by_side(up_total.reshape(SP, RANK // DP, KVW), KVW)

    return (
        mixed,
        tokens_grad,
        tail[:, 0],
        query_total,
        down_total,
        tail[: RANK // DP, 2],
        up_total,
        out_total,
        tail[:, 1],
        tail[:, 3:7],
        gate_shared,
        up_shared,
        down_shared,
        gate_routed,
        up_routed,
        down_routed,
    )


def solution(mesh):
    rows = P(("dp", "sp"), None)
    vec, mat, cube = P("dp"), P("dp", None), P("dp", None, None)
    return jax.shard_map(
        per_device,
        mesh=mesh,
        in_specs=(rows, rows, rows, vec, mat, mat, vec, mat, mat, vec, mat) + (cube,) * 6,
        out_specs=(rows, rows, vec, mat, mat, vec, mat, mat, vec, mat) + (cube,) * 6,
        check_vma=False,
    )
```

```python
import functools

import jax
import jax.numpy as jnp
import numpy as np
from jax import lax
from jax.experimental import pallas as pl
from jax.experimental.pallas import tpu as pltpu
from jax.sharding import PartitionSpec as P

D = 2048
HEADS = 16
NOPE = 128
ROPE = 64
QK = NOPE + ROPE
VDIM = 128
RANK = 512
FE = 1408
NS = 2
EXPERTS = 4
TOP = 2
SETS = NS + EXPERTS
DP = 16
SP = 8
ROWS = 128
SEQ = SP * ROWS
GROUP = DP * ROWS
HEADS_HERE = HEADS // SP
QW = HEADS_HERE * QK
KVW = HEADS_HERE * (NOPE + VDIM)
OW = HEADS_HERE * VDIM
SLICE = FE // DP
CORE_W = 1024
UP_AT = CORE_W
MISC_AT = CORE_W - ROWS
PICK_LANE, GAIN_ONE, GAIN_TWO, GAIN_KV, ROUTER_LANE = 64, 68, 69, 70, 80
ROOM = 96
HALF = SETS * ROOM
FULL = 640
CHUNK = 2 * ROWS
TILE = 512
SCALE = QK ** (-0.5)
PACK = QW + RANK + ROPE + ROPE + ROWS
GU_PART = 2 * HALF // SP
RELAY = 2 * HALF // SP
UNITS = ROOM // SP
DN_PART = FULL // SP

epsilon = 1e-06
bf16 = jnp.bfloat16
f32 = jnp.float32


def mm(left, right, dims):
    return lax.dot_general(left, right, ((dims[0], dims[1]), ((), ())), preferred_element_type=f32)


def nn(left, right):
    return mm(left, right, ((1,), (0,)))


def nt(left, right):
    return mm(left, right, ((1,), (1,)))


def tn(left, right):
    return mm(left, right, ((0,), (0,)))


def rope_tables():
    inverse = 10000.0 ** (-np.arange(ROPE // 2, dtype=np.float64) * 2.0 / ROPE)
    angles = np.arange(SEQ, dtype=np.float64)[:, None] * inverse[None, :]
    cosine, sine = np.cos(angles), np.sin(angles)
    cosine = np.concatenate([cosine] * 4, axis=1)
    sine = np.concatenate([-sine, sine] * 2, axis=1)
    return jnp.asarray(cosine, f32), jnp.asarray(sine, f32)


def norm_back(values, scale, gain, grad):
    scaled = gain * grad
    total = jnp.sum(scaled * values, axis=-1, keepdims=True) / values.shape[-1]
    return scale * scaled - values * (scale * scale * scale) * total


def inverse_rms(values):
    return lax.rsqrt(jnp.mean(values * values, axis=-1, keepdims=True) + epsilon)


class Seat:
    def __init__(self, axis):
        own_dp, own_sp = lax.axis_index("dp"), lax.axis_index("sp")
        self.axis = axis
        if axis == "sp":
            self.pair, self.ring, self.core, self.cores = own_sp // 4, own_sp % 4, 0, 1
            self.own, self.size = own_sp, SP
            self.device = lambda index: (own_dp, index)
        else:
            self.ring, self.pair, self.core, self.cores = own_dp // 4, (own_dp // 2) % 2, own_dp % 2, 2
            self.own, self.size = own_dp, DP
            self.device = lambda index: (index, own_sp)

    def index(self, pair, ring, core=0):
        pair, ring = (self.pair + pair) % 2, (self.ring + ring) % 4
        if self.axis == "sp":
            return pair * 4 + ring
        return (ring * 2 + pair) * 2 + (self.core + core) % 2


def remote(src, dst, send_sem, recv_sem, device):
    return pltpu.make_async_remote_copy(
        src_ref=src,
        dst_ref=dst,
        send_sem=send_sem,
        recv_sem=recv_sem,
        device_id=device,
        device_id_type=pl.DeviceIdType.MESH,
    )


def block_of(ref, start, size):
    return ref.at[pl.ds(pl.multiple_of(start, 16), size)]


def middle(rows):
    return (rows // 2 + 15) // 16 * 16


NEAR = ((0, 1), (0, -1), (1, 0))
SHARE = ((0, 0), (0, -1), (0, 1), (1, 0), (0, 2), (1, -1), (1, 1), (1, 2))
ORDER = ((1, 2), (1, 1), (1, -1), (0, 2), (1, 0), (0, 1), (0, -1), (0, 0))


class Gather:
    def __init__(self, axis, rows, width, spare=False):
        self.axis, self.rows, self.width, self.spare = axis, rows, width, spare
        self.count = SP if axis == "sp" else DP

    def in_spec(self):
        return pl.BlockSpec(memory_space=pl.ANY)

    def out(self):
        return (
            jax.ShapeDtypeStruct((self.count * self.rows, self.width), bf16),
            pl.BlockSpec(memory_space=pl.ANY),
        )

    def scratch(self):
        return [pltpu.SemaphoreType.DMA((17,)), pltpu.SemaphoreType.DMA((17,)), pltpu.SemaphoreType.DMA]

    def partners(self, seat):
        near = [seat.index(*n) for n in NEAR]
        return near + ([seat.index(0, 0, 1)] if seat.cores == 2 else [])

    def bind(self, src, out, scratch):
        self.src, self.dst = src, out
        self.send_sem, self.recv_sem, self.local_sem = scratch
        self.seat = Seat(self.axis)

    def view(self, place, half=None):
        start = self.seat.index(*place) * self.rows
        if half is None:
            return block_of(self.dst, start, self.rows)
        cut = middle(self.rows)
        return block_of(self.dst, start + half * cut, (cut, self.rows - cut)[half])

    def table(self, number):
        if number in (0, 1, 2, 8):
            return self.src, self.view((0, 0)), {0: (0, 1), 1: (0, -1), 2: (1, 0), 8: (0, 0, 1)}[number]
        if 8 <= number < 16:
            here = self.view(SHARE[number - 8])
            return here, here, (0, 0, 1)
        place, half, to = {
            7: ((1, -1), 0, (0, 1)),
            16: ((1, 1), 1, (0, -1)),
        }[number] if self.spare and number in (7, 16) else {
            3: ((0, -1), 0, (0, 1)),
            4: ((0, 1), 1, (0, -1)),
            5: ((1, 0), None, (0, 1)),
            6: ((1, 0), None, (0, -1)),
            7: ((0, 2), None, (1, 0)),
        }[number]
        here = self.view(place, half)
        return here, here, to

    def copy(self, number):
        src, dst, to = self.table(number)
        return remote(
            src,
            dst,
            self.send_sem.at[number],
            self.recv_sem.at[number],
            self.seat.device(self.seat.index(*to)),
        )

    def go(self, *numbers):
        for number in numbers:
            self.copy(number).start()

    def share(self, *numbers):
        if self.seat.cores == 2:
            self.go(*[8 + number for number in numbers])

    def arrived(self, *numbers):
        for number in numbers:
            self.copy(number).wait_recv()

    def local(self):
        return pltpu.make_async_copy(self.src, self.view((0, 0)), self.local_sem)

    def step(self, number, shared=True):
        if number == 0:
            self.local().start()
            self.go(0, 1, 2)
            self.share(0)
        elif number == 1:
            self.arrived(0, 1)
            self.go(3, 4)
            self.share(1, 2)
        elif number == 2:
            self.arrived(2)
            self.go(5, 6)
            self.share(3)
        elif number == 3:
            self.arrived(3, 4)
            if not self.spare:
                self.go(7)
            self.share(4)
        elif number == 4:
            self.arrived(5, 6)
            if self.spare:
                self.go(7, 16)
                self.share(5, 6)
                self.arrived(7, 16)
                self.share(7)
            else:
                self.arrived(7)
                self.share(5, 6, 7)
        else:
            numbers = list(range(8)) + [16] * self.spare
            if self.seat.cores == 2:
                numbers = numbers + list(range(8, 16))
                if shared:
                    self.arrived(*range(8, 16))
            for number in numbers:
                self.copy(number).wait_send()
            if shared:
                self.local().wait()


class Scatter:
    def __init__(self, axis, rows, width, kind=f32, spare=False, load=False):
        self.axis, self.rows, self.width, self.kind, self.spare = axis, rows, width, kind, spare
        self.load = load
        self.count = SP if axis == "sp" else DP

    def in_spec(self):
        return pl.BlockSpec(memory_space=pl.ANY if self.load else pltpu.VMEM)

    def out(self):
        return (
            jax.ShapeDtypeStruct((self.rows, self.width), self.kind),
            pl.BlockSpec(memory_space=pltpu.VMEM),
        )

    def scratch(self):
        block, cut = (self.rows, self.width), middle(self.rows)
        first, second = (cut, self.width), (self.rows - cut, self.width)
        shapes = [block, block, block, first, second, block, block, block]
        shapes = shapes + [(8 if self.axis == "dp" else 5,) + block]
        kept = [pltpu.VMEM((self.count * self.rows, self.width), bf16), pltpu.SemaphoreType.DMA]
        return [pltpu.SemaphoreType.DMA((17,)), pltpu.SemaphoreType.DMA((17,))] + [
            pltpu.VMEM(shape, bf16) for shape in shapes
        ] + kept * self.load

    partners = Gather.partners
    copy = Gather.copy
    go = Gather.go
    arrived = Gather.arrived

    def sizes(self):
        rows, cut = self.rows, middle(self.rows)
        return [rows] * 3 + [cut, rows - cut] + [rows] * 3

    def bind(self, src, out, scratch):
        self.src, self.dst = src, out
        self.send_sem, self.recv_sem = scratch[:2]
        self.got, self.made = scratch[2:10], scratch[10]
        self.seat = Seat(self.axis)
        if self.load:
            self.loading = pltpu.make_async_copy(src, scratch[11], scratch[12])
            self.loading.start()
            self.src = scratch[11]

    def given(self, *place):
        return block_of(self.src, self.seat.index(*place) * self.rows, self.rows)

    def slot(self, place):
        if self.axis == "dp":
            return self.made.at[ORDER.index(place)]
        kept = ((1, 0), (0, 1), (0, -1)) + (((1, 1), (1, -1)) if self.spare else ((0, 2),))
        k = kept.index(place)
        return self.made[k] if isinstance(self.made, list) else self.made.at[k]

    def part(self, place):
        return self.slot(place) if self.axis == "dp" else self.given(*place)

    def ready(self, *places):
        if self.axis == "dp":
            for place in places:
                self.arrived(8 + ORDER.index(place))
                self.add(self.slot(place), [self.slot(place), self.given(*place)])

    def add(self, dst, terms):
        rows = dst.shape[0]
        step = 16

        @pl.loop(0, rows // step)
        def _(i):
            at = pl.ds(pl.multiple_of(i * step, step), step)
            total = terms[0][at, :].astype(f32)
            for term in terms[1:]:
                total = total + term[at, :].astype(f32)
            dst[at, :] = total.astype(dst.dtype)

    def add_half(self, place, half, term):
        made, part = self.halves(self.slot(place)), self.halves(self.part(place))
        self.add(made[half], [part[half], term])
        if self.axis == "sp":
            self.add(made[1 - half], [part[1 - half]])

    def halves(self, ref):
        cut = middle(self.rows)
        return ref.at[pl.ds(0, cut)], ref.at[pl.ds(cut, self.rows - cut)]

    def table(self, number):
        if 8 <= number < 16:
            return self.given(*ORDER[number - 8], 1), self.made.at[number - 8], (0, 0, 1)
        if self.spare and number in (0, 1, 2, 3, 4, 16):
            if number in (1, 2):
                return self.slot((1, 3 - 2 * number)), self.got[number], (0, 3 - 2 * number)
            half = 0 if number in (0, 3) else 1
            src = self.halves(self.part((1, 2) if number in (0, 16) else (0, 2)))[half]
            dst = self.halves(self.got[0])[half] if number in (0, 16) else self.got[number]
            return src, dst, (0, 1 - 2 * half)
        src, to = {
            0: (lambda: self.part((1, 2)), (1, 0)),
            1: (lambda: self.part((1, 1)), (0, 1)),
            2: (lambda: self.part((1, -1)), (0, -1)),
            3: (lambda: self.halves(self.slot((0, 2)))[0], (0, 1)),
            4: (lambda: self.halves(self.slot((0, 2)))[1], (0, -1)),
            5: (lambda: self.slot((1, 0)), (1, 0)),
            6: (lambda: self.slot((0, 1)), (0, 1)),
            7: (lambda: self.slot((0, -1)), (0, -1)),
        }[number]
        return src(), self.got[number], to

    def step(self, number):
        if number == 0:
            if self.load:
                self.loading.wait()
            if self.axis == "dp":
                self.go(*range(8, 16))
            self.ready((1, 2))
            if self.spare:
                self.go(0, 16)
                self.ready((0, 2))
                self.go(3, 4)
                self.ready((1, 1), (1, -1))
                return
            self.go(0)
            self.ready((1, 1))
            self.go(1)
            self.ready((1, -1))
            self.go(2)
        elif number == 1 and self.spare:
            self.arrived(0, 16)
            for place, half in (((1, 1), 0), ((1, -1), 1)):
                self.add_half(place, half, self.halves(self.got[0])[half])
                self.go(1 + half)
        elif number == 1:
            self.ready((0, 2))
            self.arrived(0)
            self.add(self.slot((0, 2)), [self.part((0, 2)), self.got[0]])
            self.go(3, 4)
        elif number == 2:
            self.ready((1, 0))
            self.arrived(1, 2)
            self.add(self.slot((1, 0)), [self.part((1, 0)), self.got[1], self.got[2]])
            self.go(5)
        elif number == 3:
            self.ready((0, 1), (0, -1))
            self.arrived(3, 4)
            for place, half in (((0, 1), 0), ((0, -1), 1)):
                self.add_half(place, half, self.got[3 + half])
                self.go(6 + half)
        elif number == 4:
            self.ready((0, 0))
            self.arrived(5, 6, 7)
            self.add(self.dst, [self.part((0, 0)), self.got[5], self.got[6], self.got[7]])
        else:
            numbers = list(range(16 if self.axis == "dp" else 8)) + [16] * self.spare
            for number in numbers:
                self.copy(number).wait_send()


class Swap:
    def __init__(self, axis, shape, take, put, kind="any"):
        self.axis, self.shape, self.take, self.put = axis, shape, take, put
        self.count = SP if axis == "sp" else DP

    def in_spec(self):
        return pl.BlockSpec(memory_space=pl.ANY)

    def out(self):
        return jax.ShapeDtypeStruct(self.shape, bf16), pl.BlockSpec(memory_space=pl.ANY)

    def scratch(self):
        sems = pltpu.SemaphoreType.DMA((self.count,))
        return [sems, sems, pltpu.SemaphoreType.DMA]

    def partners(self, seat):
        return [(seat.own + k) % seat.size for k in range(1, seat.size)]

    def bind(self, src, out, scratch):
        self.src, self.dst = src, out
        self.send_sem, self.recv_sem, self.local_sem = scratch
        self.seat = Seat(self.axis)

    def copy(self, k):
        to = (self.seat.own + k) % self.seat.size
        return remote(
            self.take(self.src, to),
            self.put(self.dst, self.seat.own),
            self.send_sem.at[k],
            self.recv_sem.at[k],
            self.seat.device(to),
        )

    def local(self):
        own = self.seat.own
        return pltpu.make_async_copy(self.take(self.src, own), self.put(self.dst, own), self.local_sem)

    def step(self, number):
        if number == 0:
            self.local().start()

            @pl.loop(1, self.seat.size)
            def _(k):
                self.copy(k).start()

        elif number == 5:

            @pl.loop(1, self.seat.size)
            def _(k):
                self.copy(k).wait_recv()
                self.copy(k).wait_send()

            self.local().wait()


def meet(ops):
    barrier = pltpu.get_barrier_semaphore()
    total = 0
    for axis in ("sp", "dp"):
        mine = [op for op in ops if op.axis == axis]
        if not mine:
            continue
        seat = Seat(axis)
        widest = max(mine, key=lambda op: len(op.partners(seat)))
        for partner in widest.partners(seat):
            pl.semaphore_signal(
                barrier, inc=1, device_id=seat.device(partner), device_id_type=pl.DeviceIdType.MESH
            )
            total += 1
    pl.semaphore_wait(barrier, total)


def exchange(name, number, ops, arrays, plan=None, chained=()):
    chained = dict(chained)
    plan = plan or [(op, step) for step in range(6) for op in range(len(ops))]
    counts = [len(op.scratch()) for op in ops]
    inputs = [k for k in range(len(ops)) if k not in chained]

    def body(*refs):
        given = dict(zip(inputs, refs[: len(inputs)]))
        outs = refs[len(inputs) : len(inputs) + len(ops)]
        rest = refs[len(inputs) + len(ops) :]
        for k, op in enumerate(ops):
            op.bind(given[k] if k in given else outs[chained[k]], outs[k], rest[: counts[k]])
            rest = rest[counts[k] :]
        meet(ops)
        for op, step in plan:
            ops[op].step(step)

    outs = [op.out() for op in ops]
    return pl.pallas_call(
        body,
        name=name,
        out_shape=[shape for shape, _ in outs],
        in_specs=[ops[k].in_spec() for k in inputs],
        out_specs=[spec for _, spec in outs],
        scratch_shapes=[entry for op in ops for entry in op.scratch()],
        compiler_params=pltpu.CompilerParams(
            collective_id=number, has_side_effects=True, vmem_limit_bytes=56 * 2**20
        ),
    )(*arrays)


def expert_of(column):
    lane = jnp.zeros(column.shape, jnp.int32)
    for e in range(EXPERTS):
        low = (NS + e) * ROOM
        lane = jnp.where((column >= low) & (column < low + ROOM), PICK_LANE + e, lane)
    return lane


def two_terms(values):
    high = values.astype(bf16)
    return high, (values - high.astype(f32)).astype(bf16)


def expert_kernel(
    hidden_own,
    weights,
    router_t,
    down,
    cot_all,
    attention_weights,
    sum_out,
    mixed_out,
    gate_up_sum,
    down_sum,
    hidden,
    gate_up,
    down_w,
    sums,
    stage,
    cot_column,
    acts,
    wide,
    gates_up,
    raw,
    gates,
    dense_terms,
    reached,
    spread,
    collect,
    picks,
    running,
    load_sem,
    in_sem,
    turn_sem,
    gate_up_sems,
    down_sems,
    *rest,
):
    gather, scatter = Gather("dp", ROWS, D), Scatter("dp", ROWS, D + ROWS)
    gather.bind(hidden_own, hidden, rest[:3])
    scatter.bind(sums, sum_out, rest[3:])
    gate_up_op, down_op = Scatter("sp", GU_PART, D, bf16), Scatter("sp", DN_PART, D, bf16)
    views, at = [], 0
    for size in gate_up_op.sizes() + down_op.sizes() + [DN_PART] * 4:
        views.append(hidden.at[pl.ds(at, size)])
        at += size
    gate_up_op.bind(gate_up, gate_up_sum, [gate_up_sems.at[0], gate_up_sems.at[1], *views[:8], running])
    down_op.bind(down_w, down_sum, [down_sems.at[0], down_sems.at[1], *views[8:16], views[16:]])
    loads = [
        pltpu.make_async_copy(down, down_w, load_sem.at[2]),
        pltpu.make_async_copy(weights, sums.at[pl.ds(0, 2 * HALF), pl.ds(0, D)], load_sem.at[0]),
        pltpu.make_async_copy(attention_weights.at[:, pl.ds(MISC_AT, ROWS)], picks, load_sem.at[1]),
    ]
    for load in loads:
        load.start()

    def chunk(i):
        return pl.ds(pl.multiple_of(i * CHUNK, CHUNK), CHUNK)

    def columns(n):
        return pl.ds(pl.multiple_of(n * 256, 256), 256)

    def fetch(i):
        return pltpu.make_async_copy(cot_all.at[chunk(i)], stage.at[i % 2], in_sem.at[i % 2])

    def put(i):
        return pltpu.make_async_copy(stage.at[i % 2], mixed_out.at[chunk(i)], in_sem.at[i % 2])

    def fetch_column(n):
        return pltpu.make_async_copy(cot_all.at[:, columns(n)], cot_column.at[n % 2], in_sem.at[2 + n % 2])

    fetch(0).start()
    fetch_column(0).start()
    meet([gather, gate_up_op])
    gather.step(0)
    gate_up[pl.ds(HALF, 16), :] = router_t[...]
    gate_up[pl.ds(HALF + 16, FULL - HALF - 16), :] = jnp.zeros((FULL - HALF - 16, D), bf16)
    gate_up[pl.ds(FULL + HALF, FULL - HALF), :] = jnp.zeros((FULL - HALF, D), bf16)
    row = lax.broadcasted_iota(jnp.int32, (ROWS, FULL), 0)
    lane_of = expert_of(lax.broadcasted_iota(jnp.int32, (ROWS, FULL), 1))
    hot = (row == lane_of).astype(bf16)
    spread[:ROWS, :] = hot
    spread[ROWS:, :] = hot
    lane = lax.broadcasted_iota(jnp.int32, (FULL, ROWS), 1)
    hot = (lane == expert_of(lax.broadcasted_iota(jnp.int32, (FULL, ROWS), 0))).astype(bf16)
    collect[:FULL, :] = hot
    collect[FULL:, :] = hot
    loads[0].wait()

    @pl.loop(0, 8)
    def _(i):
        @pl.when(i < 7)
        def _():
            fetch(i + 1).start()

        fetch(i).wait()
        raw[chunk(i), :] = nt(stage[i % 2], down_w[...])

    wait_all(loads[1:])
    for k in range(2 * SETS):
        for part in range(SP):
            units = sums[part * RELAY + k * UNITS : part * RELAY + (k + 1) * UNITS, :D]
            at = k // SETS * FULL + k % SETS * ROOM + part * UNITS
            gate_up[at : at + UNITS, :] = units
    gather.local().wait()

    def at_least(i, k):
        return (i + 8 - k) // 8

    def chip_of(i):
        pair = i // 3 - i // 4 + i // 5 - i // 6
        ring = 3 * at_least(i, 1) - 2 * at_least(i, 2) - at_least(i, 3) + 2 * at_least(i, 4)
        ring = ring + at_least(i, 5) - 2 * at_least(i, 6) + at_least(i, 7)
        seat = gather.seat
        return ((seat.ring + ring) % 4) * 2 + (seat.pair + pair) % 2

    @pl.loop(0, 8)
    def _(i):
        for step, when in ((1, 1), (2, 1), (3, 3), (4, 5)):

            @pl.when(i == when)
            def _():
                gather.step(step)

        chip = chip_of(i)
        rows = chunk(chip)
        landed = block_of(hidden, chip * CHUNK + (1 - gather.seat.core) * ROWS, ROWS)
        remote(
            landed,
            landed,
            gather.send_sem.at[8 + i],
            gather.recv_sem.at[8 + i],
            gather.seat.device(gather.seat.index(0, 0, 1)),
        ).wait_recv()
        gates_up[...] = nt(hidden[rows, :], gate_up[...])
        lane = lax.broadcasted_iota(jnp.int32, (CHUNK, ROWS), 1)
        valid = (lane >= PICK_LANE) & (lane < PICK_LANE + EXPERTS)
        logits = jnp.where(valid, gates_up[:, FULL - ROWS : FULL], -1e30)
        top = jnp.max(logits, axis=1, keepdims=True)
        router = jnp.where(valid, jnp.exp(logits - top), 0.0)
        router = router / jnp.sum(router, axis=1, keepdims=True)
        dense_terms[:, :ROWS], dense_terms[:, ROWS:] = two_terms(router * picks[rows, :].astype(f32))
        gates[...] = nn(dense_terms[...], spread[...])

        @pl.loop(0, CHUNK // 32)
        def _(k):
            at = pl.ds(pl.multiple_of(k * 32, 32), 32)
            there = pl.ds(pl.multiple_of(chip * CHUNK + k * 32, 32), 32)
            column = lax.broadcasted_iota(jnp.int32, (32, FULL), 1)
            factor = jnp.where(column < NS * ROOM, 1.0, gates[at, :])
            gate, up, raw_grad = gates_up[at, :FULL], gates_up[at, FULL:], raw[there, :]
            sig = 1.0 / (1.0 + jnp.exp(-gate))
            silu = gate * sig
            act = silu * up
            acts[there, :] = (act.astype(bf16).astype(f32) * factor).astype(bf16)
            reached[at, :FULL], reached[at, FULL:] = two_terms(act * raw_grad)
            act_grad = raw_grad * factor
            wide[there, :FULL] = (act_grad * up * sig * (1.0 + gate * (1.0 - sig))).astype(bf16)
            wide[there, FULL:] = (act_grad * silu).astype(bf16)

        sums[rows, D:] = nn(reached[...], collect[...]).astype(bf16)
        sums[rows, :D] = nn(wide[rows, :], gate_up[...]).astype(bf16)

    def gate_up_grads(first, last):
        @pl.loop(first, last)
        def _(n):
            made = tn(wide[...], hidden[:, columns(n)]).astype(bf16)
            gate_up[:HALF, columns(n)] = made[:HALF]
            gate_up[HALF : 2 * HALF, columns(n)] = made[FULL : FULL + HALF]

    def down_grads(first, last):
        @pl.loop(first, last)
        def _(n):
            @pl.when(n < D // 256 - 1)
            def _():
                fetch_column(n + 1).start()

            fetch_column(n).wait()
            down_w[:, columns(n)] = tn(acts[...], cot_column[n % 2]).astype(bf16)

    def outputs(first, last):
        @pl.loop(first, last)
        def _(i):
            @pl.when(i >= 2)
            def _():
                put(i - 2).wait()

            stage[i % 2] = nn(acts[chunk(i), :], down_w[...]).astype(bf16)
            put(i).start()

    scatter.step(0)
    gate_up_grads(0, 6)
    scatter.step(1)
    gate_up_grads(6, 8)
    gather.step(5, shared=False)
    seat = gate_up_op.seat
    for partner in gate_up_op.partners(seat):
        pl.semaphore_signal(
            turn_sem, inc=1, device_id=seat.device(partner), device_id_type=pl.DeviceIdType.MESH
        )
    scatter.step(2)
    outputs(0, 2)
    pl.semaphore_wait(turn_sem, len(NEAR))
    gate_up_op.step(0)
    outputs(2, 6)
    scatter.step(3)
    outputs(6, 8)
    put(6).wait()
    put(7).wait()
    down_grads(0, 8)
    down_op.step(0)
    gate_up_op.step(1)
    gate_up_op.step(2)
    scatter.step(4)
    gate_up_op.step(3)
    for step in (1, 2, 3):
        down_op.step(step)
    gate_up_op.step(4)
    down_op.step(4)
    gate_up_op.step(5)
    down_op.step(5)
    scatter.step(5)


def experts(*arrays):
    any_spec, vmem = pl.BlockSpec(memory_space=pl.ANY), pl.BlockSpec(memory_space=pltpu.VMEM)
    gather, scatter = Gather("dp", ROWS, D), Scatter("dp", ROWS, D + ROWS)
    flops = 2 * GROUP * D * FULL * 9
    return pl.pallas_call(
        expert_kernel,
        name="experts",
        out_shape=[
            jax.ShapeDtypeStruct((ROWS, D + ROWS), f32),
            jax.ShapeDtypeStruct((GROUP, D), bf16),
            jax.ShapeDtypeStruct((GU_PART, D), bf16),
            jax.ShapeDtypeStruct((DN_PART, D), bf16),
        ],
        in_specs=[any_spec, any_spec, vmem, any_spec, any_spec, any_spec],
        out_specs=[vmem, any_spec, vmem, vmem],
        scratch_shapes=[
            pltpu.VMEM((GROUP, D), bf16),
            pltpu.VMEM((2 * FULL, D), bf16),
            pltpu.VMEM((FULL, D), bf16),
            pltpu.VMEM((GROUP, D + ROWS), bf16),
            pltpu.VMEM((2, CHUNK, D), bf16),
            pltpu.VMEM((2, GROUP, 256), bf16),
            pltpu.VMEM((GROUP, FULL), bf16),
            pltpu.VMEM((GROUP, 2 * FULL), bf16),
            pltpu.VMEM((CHUNK, 2 * FULL), f32),
            pltpu.VMEM((GROUP, FULL), f32),
            pltpu.VMEM((CHUNK, FULL), f32),
            pltpu.VMEM((CHUNK, 2 * ROWS), bf16),
            pltpu.VMEM((CHUNK, 2 * FULL), bf16),
            pltpu.VMEM((2 * ROWS, FULL), bf16),
            pltpu.VMEM((2 * FULL, ROWS), bf16),
            pltpu.VMEM((GROUP, ROWS), bf16),
            pltpu.VMEM((4, GU_PART, D), bf16),
            pltpu.SemaphoreType.DMA((3,)),
            pltpu.SemaphoreType.DMA((4,)),
            pltpu.SemaphoreType.REGULAR,
            pltpu.SemaphoreType.DMA((2, 17)),
            pltpu.SemaphoreType.DMA((2, 17)),
        ]
        + gather.scratch()
        + scatter.scratch(),
        compiler_params=pltpu.CompilerParams(
            collective_id=2, has_side_effects=True, vmem_limit_bytes=61 * 2**20
        ),
        cost_estimate=pl.CostEstimate(flops=flops, bytes_accessed=40 * 2**20, transcendentals=GROUP * FULL),
    )(*arrays)


def wait_all(copies):
    for copy in copies:
        copy.wait()


def swap_halves(values):
    lane = lax.broadcasted_iota(jnp.int32, values.shape, 1) % ROPE
    return jnp.where(lane < ROPE // 2, pltpu.roll(values, 96, 1), pltpu.roll(values, 32, 1))


def causal(scores):
    rows, seen = scores.shape
    row = lax.broadcasted_iota(jnp.int32, (rows, rows), 0)
    column = lax.broadcasted_iota(jnp.int32, (rows, rows), 1)
    last = jnp.where(column <= row, scores[:, seen - rows :], -1e9)
    return last if seen == rows else jnp.concatenate([scores[:, : seen - rows], last], axis=1)


def attention_ops():
    return (
        Gather("sp", ROWS, D, spare=True),
        Gather("dp", ROWS, PACK),
        Gather("dp", ROWS, D, spare=True),
        Gather("dp", ROWS, D, spare=True),
        Swap(
            "dp",
            (RELAY, D),
            lambda ref, j: ref.at[j],
            lambda ref, j: ref.at[:, pl.ds(pl.multiple_of(j * ROWS, ROWS), ROWS)],
        ),
        Gather("sp", RELAY, D),
        Swap(
            "sp",
            (ROWS, D),
            lambda ref, j: ref.at[pl.ds(pl.multiple_of(j * ROWS, ROWS), ROWS)],
            lambda ref, j: ref.at[:, pl.ds(pl.multiple_of(j * OW, OW), OW)],
        ),
    )


def attention_kernel(
    tokens,
    pack,
    cotangent,
    shared_gate,
    expert_gate,
    shared_up,
    expert_up,
    shared_down,
    expert_down,
    out_own,
    cosine,
    sine,
    resid_two,
    hidden_two,
    cot_all,
    gate_up_part,
    gate_up,
    down_out,
    tok_out,
    weights_out,
    hidden_out,
    compressed_out,
    latent_out,
    query_out,
    key_out,
    value_out,
    head_out,
    out_w_out,
    misc_out,
    total_out,
    tok,
    weights,
    hidden,
    qc,
    latent,
    up_w,
    query,
    key,
    value,
    tok_heads,
    out_w,
    misc_t,
    totals,
    heads,
    pieces,
    down,
    gate_shared,
    gate_routed,
    up_shared,
    up_routed,
    down_shared,
    down_routed,
    save_sem,
    load_sem,
    *rest,
):
    ops = attention_ops()
    tok_op, pack_op, out_op, cot_op, piece_op, gate_up_op, head_op = ops
    bound = (
        (tokens, tok),
        (pack, weights),
        (out_own, out_w),
        (cotangent, cot_all),
        (pieces, gate_up_part),
        (gate_up_part, gate_up),
        (heads, tok_heads),
    )
    for op, (src, dst) in zip(ops, bound):
        count = len(op.scratch())
        op.bind(src, dst, rest[:count])
        rest = rest[count:]
    loads = [
        pltpu.make_async_copy(src, dst, load_sem.at[k])
        for k, (src, dst) in enumerate(
            (
                (shared_gate, gate_shared),
                (expert_gate, gate_routed),
                (shared_up, up_shared),
                (expert_up, up_routed),
                (shared_down, down_shared),
                (expert_down, down_routed),
            )
        )
    ]
    for load in loads:
        load.start()
    meet(ops)
    tok_op.step(0)
    pack_op.step(0)
    out_op.step(0)
    for step in (1, 2):
        tok_op.step(step)
        pack_op.step(step)

    wait_all(loads)
    row = lax.broadcasted_iota(jnp.int32, (DP * UNITS, FE), 0)
    column = lax.broadcasted_iota(jnp.int32, (DP * UNITS, FE), 1)
    group, unit = row // UNITS, row - row // UNITS * UNITS + tok_op.seat.own * UNITS
    pick = ((group * SLICE + unit == column) & (unit < SLICE)).astype(bf16)
    for k, (shared, routed) in enumerate(((gate_shared, gate_routed), (up_shared, up_routed))):
        for e in range(SETS):
            piece = shared[:, e, :] if e < NS else routed[:, e - NS, :]
            piece = nt(pick, piece).astype(bf16)
            at = (k * SETS + e) * UNITS
            for d in range(DP):
                pieces[d, at : at + UNITS, :] = piece[d * UNITS : (d + 1) * UNITS]
        if k == 0:
            tok_op.step(3)
            pack_op.step(3)
            out_op.step(1)
            out_op.step(2)
    piece_op.step(0)
    pack_op.step(4)
    pack_op.step(5)
    cot_op.step(0)
    tok_op.local().wait()
    saves = [
        pltpu.make_async_copy(src, dst, save_sem.at[k])
        for k, (src, dst) in enumerate(
            (
                (tok, tok_out),
                (weights, weights_out),
                (hidden, hidden_out),
                (qc.at[:, pl.ds(QW, RANK)], compressed_out),
                (latent, latent_out),
                (query, query_out),
                (key, key_out),
                (value, value_out),
                (tok_heads, head_out),
                (out_w, out_w_out),
                (misc_t, misc_out),
                (totals, total_out),
            )
        )
    ]
    saves[1].start()
    misc_t[...] = weights[:, MISC_AT:CORE_W].astype(f32).T
    up = weights[:, UP_AT:].reshape(DP, 4, RANK // DP, ROWS)
    for k in range(4):
        up_w[:, k * ROWS : (k + 1) * ROWS] = up[:, k].reshape(RANK, ROWS)
    each = RANK // DP
    for d in range(DP):
        misc_t[0:1, d * each : (d + 1) * each] = misc_t[GAIN_KV : GAIN_KV + 1, d * ROWS : d * ROWS + each]
    kv_gain = misc_t[0:1, :RANK]
    saves[10].start()
    gain = misc_t[GAIN_ONE : GAIN_ONE + 1, :]

    def project(*places):
        for place in places:
            start = tok_op.seat.index(*place) * ROWS

            @pl.loop(0, ROWS // 32)
            def _(k):
                at = pl.ds(pl.multiple_of(start + k * 32, 32), 32)
                values = tok[at, :].astype(f32)
                hidden[at, :] = (values * inverse_rms(values) * gain).astype(bf16)

            at = pl.ds(pl.multiple_of(start, ROWS), ROWS)
            qc[at, :] = nn(hidden[at, :], weights[:, :CORE_W])

    project((0, 0), (0, -1), (0, 1), (1, 0), (0, 2))
    tok_op.step(4)
    piece_op.step(5)
    gate_up_op.step(0)
    out_op.step(3)
    project((1, -1), (1, 1), (1, 2))
    tok_op.step(5, shared=False)
    for k in (0, 2, 3):
        saves[k].start()

    @pl.loop(0, SEQ // 256)
    def _(k):
        at = pl.ds(pl.multiple_of(k * 256, 256), 256)
        inner = qc[at, QW : QW + RANK]
        latent[at, :] = (inner * inverse_rms(inner) * kv_gain).astype(bf16)
        ropes, key_rope = qc[at, 2 * NOPE : QW], qc[at, MISC_AT:CORE_W]
        cos, sin = cosine[at, :], sine[at, :]
        ropes = (ropes * cos + swap_halves(ropes) * sin).astype(bf16)
        key_rope = key_rope * cos + swap_halves(key_rope) * sin
        lane = lax.broadcasted_iota(jnp.int32, key_rope.shape, 1)
        key_rope = jnp.where(lane < ROPE, key_rope, 0.0)
        expanded = nn(latent[at, :], up_w[...]).astype(bf16)
        for h in range(HEADS_HERE):
            query[h, at, :NOPE] = qc[at, h * NOPE : (h + 1) * NOPE].astype(bf16)
            query[h, at, NOPE:] = ropes
            turned = key_rope if h == 0 else pltpu.roll(key_rope, ROPE, 1)
            key[h, at, NOPE:] = turned.astype(bf16)
            base = h * (NOPE + VDIM)
            key[h, at, :NOPE] = expanded[:, base : base + NOPE]
            value[h, at, :] = expanded[:, base + NOPE : base + NOPE + VDIM]

    for k in (4, 5, 6, 7):
        saves[k].start()
    gate_up_op.step(1)
    gate_up_op.step(2)
    cot_op.step(1)
    cot_op.step(2)
    for h in range(HEADS_HERE):
        for i in range(SEQ // 256):
            at, seen = pl.ds(i * 256, 256), (i + 1) * 256
            scores = causal(nt(query[h, at, :], key[h, :seen, :]) * SCALE)
            top = jnp.max(scores, axis=1, keepdims=True)
            parts = jnp.exp(scores - top)
            total = jnp.sum(parts, axis=1, keepdims=True)
            probs = (parts * (1.0 / total)).astype(bf16)
            heads[at, h * VDIM : (h + 1) * VDIM] = nn(probs, value[h, :seen, :]).astype(bf16)
            totals[h, at, :] = jnp.broadcast_to(top + jnp.log(total), (256, ROWS))
        if h == 0:
            out_op.step(4)
            gate_up_op.step(3)
    head_op.step(0)
    saves[11].start()
    cot_op.step(3)
    for e in range(SETS):
        part = down_shared[:, e, :] if e < NS else down_routed[:, e - NS, :]
        down[e * ROOM : e * ROOM + SLICE, :] = part
        down[e * ROOM + SLICE : (e + 1) * ROOM, :] = jnp.zeros((ROOM - SLICE, D), bf16)
    down[HALF:, :] = jnp.zeros((FULL - HALF, D), bf16)
    down_save = pltpu.make_async_copy(down, down_out, load_sem.at[0])
    down_save.start()
    gate_up_op.step(4)
    out_op.step(5)
    saves[9].start()
    head_op.step(5)
    saves[8].start()
    own = tok_op.view((0, 0))[...].astype(f32)
    resid = own + nn(tok_heads[...], out_w[...])
    resid_two[...] = resid
    hidden_two[...] = (resid * inverse_rms(resid) * misc_t[GAIN_TWO : GAIN_TWO + 1, :]).astype(bf16)
    cot_op.step(4)
    wait_all(saves + [down_save])
    cot_op.step(5)
    gate_up_op.step(5)


def attention(*arrays):
    any_spec, vmem = pl.BlockSpec(memory_space=pl.ANY), pl.BlockSpec(memory_space=pltpu.VMEM)
    kept = [
        ((SEQ, D), bf16),
        ((D, PACK), bf16),
        ((SEQ, D), bf16),
        ((SEQ, RANK), f32),
        ((SEQ, RANK), bf16),
        ((HEADS_HERE, SEQ, 2 * NOPE), bf16),
        ((HEADS_HERE, SEQ, 2 * NOPE), bf16),
        ((HEADS_HERE, SEQ, VDIM), bf16),
        ((ROWS, D), bf16),
        ((D, D), bf16),
        ((ROWS, D), f32),
        ((HEADS_HERE, SEQ, ROWS), f32),
    ]
    made = [((ROWS, D), f32), ((ROWS, D), bf16), ((GROUP, D), bf16), ((RELAY, D), bf16), ((SP * RELAY, D), bf16), ((FULL, D), bf16)]
    scratch = kept[:3] + [((SEQ, CORE_W), f32), kept[4], ((RANK, KVW), bf16)] + kept[5:]
    scratch = scratch + [((SEQ, OW), bf16), ((DP, RELAY, ROWS), bf16), ((FULL, D), bf16)]
    scratch = scratch + [(array.shape, bf16) for array in arrays[3:9]]
    return pl.pallas_call(
        attention_kernel,
        name="attention",
        out_shape=[jax.ShapeDtypeStruct(*shape) for shape in made + kept],
        in_specs=[any_spec] * 10 + [vmem] * 2,
        out_specs=[vmem] * 2 + [any_spec] * (len(made) + len(kept) - 2),
        scratch_shapes=[pltpu.VMEM(*shape) for shape in scratch]
        + [pltpu.SemaphoreType.DMA((len(kept),)), pltpu.SemaphoreType.DMA((6,))]
        + [entry for op in attention_ops() for entry in op.scratch()],
        compiler_params=pltpu.CompilerParams(
            collective_id=0, has_side_effects=True, vmem_limit_bytes=60 * 2**20
        ),
        cost_estimate=pl.CostEstimate(
            flops=2 * SEQ * D * (CORE_W + OW), bytes_accessed=60 * 2**20, transcendentals=SEQ * SEQ
        ),
    )(*arrays)


def attention_grad_ops():
    return (
        Gather("dp", ROWS, D, spare=True),
        Swap(
            "dp",
            (DP * GU_PART, ROWS),
            lambda ref, j: ref.at[:, pl.ds(pl.multiple_of(j * ROWS, ROWS), ROWS)],
            lambda ref, j: ref.at[pl.ds(pl.multiple_of(j * GU_PART, GU_PART), GU_PART)],
        ),
        Gather("sp", DP * GU_PART, ROWS),
        Gather("sp", DN_PART, D),
        Swap(
            "dp",
            (GROUP, ROWS),
            lambda ref, j: ref.at[:, pl.ds(pl.multiple_of(j * ROWS, ROWS), ROWS)],
            lambda ref, j: ref.at[pl.ds(pl.multiple_of(j * ROWS, ROWS), ROWS)],
        ),
        Swap(
            "sp",
            (SEQ, OW),
            lambda ref, j: ref.at[:, pl.ds(pl.multiple_of(j * OW, OW), OW)],
            lambda ref, j: ref.at[pl.ds(pl.multiple_of(j * ROWS, ROWS), ROWS)],
        ),
    )


def attention_grad_kernel(
    proj_own,
    tok_all,
    weights_all,
    hidden_all,
    compressed_all,
    latent_all,
    query_all,
    key_all,
    value_all,
    head_all,
    out_w_all,
    misc_all,
    total_all,
    gate_up_sum,
    down_sum,
    cosine,
    sine,
    norm_rows,
    hidden_part,
    gate_up_piece,
    gate_up_total,
    down_total,
    grads,
    proj_all,
    out_grad,
    tok,
    weights,
    hidden,
    compressed,
    latent,
    query,
    key,
    value,
    proj,
    out_w,
    head_own,
    head_cols,
    misc_t,
    totals,
    up_w,
    head_grad,
    key_grad,
    value_grad,
    rope_grad,
    expanded_grad,
    qc_grad,
    scale_one,
    misc_grad,
    up_grad,
    made_w,
    made_h,
    load_sem,
    out_sem,
    *rest,
):
    ops = attention_grad_ops()
    proj_op, piece_op, gate_up_op, down_op, out_op, head_op = ops
    bound = (
        (proj_own, proj_all),
        (gate_up_sum, gate_up_piece),
        (gate_up_piece, gate_up_total),
        (down_sum, down_total),
        (head_all, head_cols),
        (head_own, head_grad),
    )
    for op, (src, dst) in zip(ops, bound):
        count = len(op.scratch())
        op.bind(src, dst, rest[:count])
        rest = rest[count:]
    loads = [
        pltpu.make_async_copy(src, dst, load_sem.at[k])
        for k, (src, dst) in enumerate(
            (
                (proj_own, proj),
                (out_w_all, out_w),
                (tok_all, tok),
                (query_all, query),
                (key_all, key),
                (value_all, value),
                (total_all, totals),
                (weights_all, weights),
                (compressed_all, compressed),
                (latent_all, latent),
                (misc_all, misc_t),
                (hidden_all, hidden),
            )
        )
    ]
    for load in loads:
        load.start()
    meet(ops)
    wait_all(loads[:2])
    head_own[...] = nt(proj[...], out_w[...]).astype(bf16)
    head_op.step(0)
    piece_op.step(0)
    down_op.step(0)
    proj_op.step(0)
    out_op.step(0)
    wait_all(loads[2:])

    @pl.loop(0, SEQ // 32)
    def _(k):
        at = pl.ds(pl.multiple_of(k * 32, 32), 32)
        scale_one[at, :] = inverse_rms(tok[at, :].astype(f32))

    up = weights[:, UP_AT:].reshape(DP, 4, RANK // DP, ROWS)
    for k in range(4):
        up_w[:, k * ROWS : (k + 1) * ROWS] = up[:, k].reshape(RANK, ROWS)
    head_op.step(5)
    piece_op.step(5)
    gate_up_op.step(0)
    for h in range(HEADS_HERE):
        for i in reversed(range(SEQ // 256)):
            at, seen = pl.ds(i * 256, 256), (i + 1) * 256
            piece = head_grad[at, h * VDIM : (h + 1) * VDIM]
            scores = causal(nt(query[h, at, :], key[h, :seen, :]) * SCALE)
            probs = jnp.exp(scores - totals[h, at, 0:1])
            dprob = nt(piece, value[h, :seen, :])
            delta = jnp.sum(probs * dprob, axis=1, keepdims=True)
            score_grad = (probs * (dprob - delta) * SCALE).astype(bf16)
            query_grad = nn(score_grad, key[h, :seen, :]).astype(bf16)
            qc_grad[at, h * NOPE : (h + 1) * NOPE] = query_grad[:, :NOPE]
            turned = query_grad[:, NOPE:].astype(f32)
            rope_grad[at, :] = turned if h == 0 else rope_grad[at, :] + turned
            from_query = tn(score_grad, query[h, at, :])
            from_out = tn(probs.astype(bf16), piece)
            if i == SEQ // 256 - 1:
                key_grad[h, :seen, :] = from_query
                value_grad[h, :seen, :] = from_out
            else:
                key_grad[h, :seen, :] += from_query
                value_grad[h, :seen, :] += from_out
        if h == 0:
            down_op.step(1)
            down_op.step(2)
            proj_op.step(1)
            proj_op.step(2)
    down_op.step(3)
    proj_op.step(3)
    kv_gain = misc_t[0:1, :RANK]
    lane = lax.broadcasted_iota(jnp.int32, (128, ROWS), 1)

    @pl.loop(0, SEQ // 128)
    def _(k):
        at = pl.ds(pl.multiple_of(k * 128, 128), 128)
        cos, sin = cosine[at, :], sine[at, :]
        ropes = rope_grad[at, :]
        qc_grad[at, 2 * NOPE : QW] = (ropes * cos - swap_halves(ropes) * sin).astype(bf16)
        key_rope = jnp.zeros((128, ROWS), f32)
        for h in range(HEADS_HERE):
            base = h * (NOPE + VDIM)
            expanded_grad[at, base : base + NOPE] = key_grad[h, at, :NOPE].astype(bf16)
            expanded_grad[at, base + NOPE : base + NOPE + VDIM] = value_grad[h, at, :].astype(bf16)
            turned = key_grad[h, at, NOPE:].astype(bf16).astype(f32)
            turned = turned if h == 0 else pltpu.roll(turned, ROPE, 1)
            key_rope = key_rope + jnp.where(lane < ROPE, turned, 0.0)
        key_rope = key_rope * cos - swap_halves(key_rope) * sin
        qc_grad[at, MISC_AT:CORE_W] = jnp.where(lane < ROPE, key_rope, 0.0).astype(bf16)

    made = tn(latent[...], expanded_grad[...]).astype(bf16)
    each = RANK // DP
    for d in range(DP):
        for k in range(4):
            at = pl.ds(d * ROWS + k * each, each)
            up_grad[at, :] = made[d * each : (d + 1) * each, k * ROWS : (k + 1) * ROWS]
    up_store = pltpu.make_async_copy(up_grad, grads.at[:, pl.ds(UP_AT, ROWS)], out_sem.at[2])
    up_store.start()
    misc_grad[...] = jnp.zeros_like(misc_grad)
    misc_grad[64:72, :] = norm_rows[...]
    kv_total = jnp.zeros((1, RANK), f32)
    for k in range(SEQ // 256):
        at = pl.ds(k * 256, 256)
        inner = compressed[at, :]
        scale = inverse_rms(inner)
        latent_grad = nt(expanded_grad[at, :], up_w[...])
        kv_total = kv_total + jnp.sum(latent_grad * inner * scale, axis=0, keepdims=True)
        qc_grad[at, QW : QW + RANK] = norm_back(inner, scale, kv_gain, latent_grad).astype(bf16)
    for d in range(DP):
        misc_grad[66:67, d * ROWS : d * ROWS + each] = kv_total[:, d * each : (d + 1) * each]
    gate_up_op.step(1)
    gate_up_op.step(2)

    def put(n):
        at = pl.ds(pl.multiple_of(n * TILE, TILE), TILE)
        return pltpu.make_async_copy(made_h.at[n % 2], hidden_part.at[:, at], out_sem.at[n % 2])

    @pl.loop(0, D // TILE)
    def _(n):
        at = pl.ds(pl.multiple_of(n * TILE, TILE), TILE)

        @pl.when(n >= 2)
        def _():
            put(n - 2).wait()

        grad = nt(qc_grad[...], weights[at, :CORE_W])
        made_h[n % 2] = grad.astype(bf16)
        put(n).start()
        grad = grad * tok[:, at].astype(f32) * scale_one[...]
        misc_grad[64:65, at] = jnp.sum(grad, axis=0, keepdims=True)

    put(2).wait()
    put(3).wait()
    gate_up_op.step(3)
    proj_op.step(4)
    down_op.step(4)
    def store(n):
        at = pl.ds(pl.multiple_of(n * TILE, TILE), TILE)
        return pltpu.make_async_copy(
            made_w.at[n % 2], grads.at[at, pl.ds(0, CORE_W)], out_sem.at[n % 2]
        )

    @pl.loop(0, D // TILE)
    def _(n):
        at = pl.ds(pl.multiple_of(n * TILE, TILE), TILE)

        @pl.when(n >= 2)
        def _():
            store(n - 2).wait()

        made = tn(hidden[:, at], qc_grad[...])
        made_w[n % 2, :, :MISC_AT] = made[:, :MISC_AT].astype(bf16)
        made_w[n % 2, :, MISC_AT:] = (made[:, MISC_AT:] + misc_grad[:, at].T).astype(bf16)
        store(n).start()

    store(2).wait()
    store(3).wait()
    up_store.wait()
    proj_op.step(5)
    out_op.step(5)

    def half(n, k):
        rows, at = pl.ds(k * SEQ, SEQ), pl.ds(n * TILE, TILE)
        return pltpu.make_async_copy(proj_all.at[rows, at], made_h.at[k], out_sem.at[k])

    half(0, 0).start()
    half(0, 1).start()
    for n in range(D // TILE):
        total = 0.0
        for k in range(2):
            half(n, k).wait()
            total = total + tn(head_cols[pl.ds(k * SEQ, SEQ), :], made_h[k])
            if n < D // TILE - 1:
                half(n + 1, k).start()
        rows, at = pl.ds(n // 2 * ROWS, ROWS), pl.ds(n % 2 * TILE, TILE)
        out_grad[rows, at] = total.astype(bf16)

    gate_up_op.step(4)
    gate_up_op.step(5)
    down_op.step(5)


def attention_grad(*arrays):
    any_spec, vmem = pl.BlockSpec(memory_space=pl.ANY), pl.BlockSpec(memory_space=pltpu.VMEM)
    scratch = [
        ((SEQ, D), bf16),
        ((D, PACK), bf16),
        ((SEQ, D), bf16),
        ((SEQ, RANK), f32),
        ((SEQ, RANK), bf16),
        ((HEADS_HERE, SEQ, 2 * NOPE), bf16),
        ((HEADS_HERE, SEQ, 2 * NOPE), bf16),
        ((HEADS_HERE, SEQ, VDIM), bf16),
        ((ROWS, D), bf16),
        ((D, D), bf16),
        ((ROWS, D), bf16),
        ((GROUP, ROWS), bf16),
        ((ROWS, D), f32),
        ((HEADS_HERE, SEQ, ROWS), f32),
        ((RANK, KVW), bf16),
        ((SEQ, OW), bf16),
        ((HEADS_HERE, SEQ, 2 * NOPE), f32),
        ((HEADS_HERE, SEQ, VDIM), f32),
        ((SEQ, ROWS), f32),
        ((SEQ, KVW), bf16),
        ((SEQ, CORE_W), bf16),
        ((SEQ, 1), f32),
        ((ROWS, D), f32),
        ((D, ROWS), bf16),
        ((2, TILE, CORE_W), bf16),
        ((2, SEQ, TILE), bf16),
    ]
    return pl.pallas_call(
        attention_grad_kernel,
        name="attention_grad",
        out_shape=[
            jax.ShapeDtypeStruct((SEQ, D), bf16),
            jax.ShapeDtypeStruct((DP * GU_PART, ROWS), bf16),
            jax.ShapeDtypeStruct((SP * DP * GU_PART, ROWS), bf16),
            jax.ShapeDtypeStruct((FULL, D), bf16),
            jax.ShapeDtypeStruct((D, PACK), bf16),
            jax.ShapeDtypeStruct((GROUP, D), bf16),
            jax.ShapeDtypeStruct((2 * ROWS, D // 2), bf16),
        ],
        in_specs=[any_spec] * 15 + [vmem] * 3,
        out_specs=[any_spec] * 6 + [vmem],
        scratch_shapes=[pltpu.VMEM(*shape) for shape in scratch]
        + [pltpu.SemaphoreType.DMA((12,)), pltpu.SemaphoreType.DMA((3,))]
        + [entry for op in attention_grad_ops() for entry in op.scratch()],
        compiler_params=pltpu.CompilerParams(
            collective_id=4, has_side_effects=True, vmem_limit_bytes=61 * 2**20
        ),
        cost_estimate=pl.CostEstimate(
            flops=6 * SEQ * D * CORE_W, bytes_accessed=60 * 2**20, transcendentals=SEQ * SEQ
        ),
    )(*arrays)


def unpack_kernel(
    gate_up, down, gate_shared, up_shared, gate_routed, up_routed, down_shared, down_routed, block, rows, pick, sem
):
    def fetch(k):
        part, skip = divmod(k * ROOM, GU_PART)
        first = min(ROOM, GU_PART - skip)
        pieces = [(part, skip, 0, first)] + ([(part + 1, 0, first, ROOM - first)] if first < ROOM else [])
        return [
            pltpu.make_async_copy(
                gate_up.at[s, :, pl.ds(begin, size)], block.at[k % 2, :, pl.ds(at, size)], sem.at[k % 2, n]
            )
            for n, (s, begin, at, size) in enumerate(pieces)
        ]

    load = pltpu.make_async_copy(down, rows, sem.at[2, 0])
    load.start()
    for copy in fetch(0):
        copy.start()
    row = lax.broadcasted_iota(jnp.int32, pick.shape, 0)
    column = lax.broadcasted_iota(jnp.int32, pick.shape, 1)
    unit = row - row // ROOM * ROOM
    pick[...] = ((row // ROOM * SLICE + unit == column) & (unit < SLICE)).astype(bf16)
    for k in range(2 * SETS):
        if k + 1 < 2 * SETS:
            for copy in fetch(k + 1):
                copy.start()
        for copy in fetch(k):
            copy.wait()
        made = tn(block[k % 2].reshape(DP * ROOM, ROWS), pick[...])
        e = k % SETS
        shared, routed = (gate_shared, gate_routed) if k < SETS else (up_shared, up_routed)
        if e < NS:
            shared[:, e, :] = made
        else:
            routed[:, e - NS, :] = made
    load.wait()
    for e in range(SETS):
        made = rows[e * ROOM : e * ROOM + SLICE, :].astype(f32)
        if e < NS:
            down_shared[:, e, :] = made
        else:
            down_routed[:, e - NS, :] = made


def unpack(gate_up, down):
    any_spec, vmem = pl.BlockSpec(memory_space=pl.ANY), pl.BlockSpec(memory_space=pltpu.VMEM)
    width, height = SLICE, ROWS
    return pl.pallas_call(
        unpack_kernel,
        name="unpack",
        out_shape=[jax.ShapeDtypeStruct((height, n, FE), f32) for n in (NS, NS, EXPERTS, EXPERTS)]
        + [jax.ShapeDtypeStruct((width, n, D), f32) for n in (NS, EXPERTS)],
        in_specs=[any_spec] * 2,
        out_specs=[vmem] * 6,
        scratch_shapes=[
            pltpu.VMEM((2, DP, ROOM, ROWS), bf16),
            pltpu.VMEM((FULL, D), bf16),
            pltpu.VMEM((DP * ROOM, FE), bf16),
            pltpu.SemaphoreType.DMA((3, 2)),
        ],
        compiler_params=pltpu.CompilerParams(vmem_limit_bytes=56 * 2**20),
    )(gate_up, down)


def per_device(
    tokens,
    cotangent,
    chosen,
    attn_gain,
    w_query,
    w_kv_down,
    kv_gain,
    w_kv_up,
    w_out,
    ffn_gain,
    w_router,
    shared_gate,
    shared_up,
    shared_down,
    expert_gate,
    expert_up,
    expert_down,
):
    own_sp = lax.axis_index("sp")
    picks = jnp.any(chosen[:, :, None] == jnp.arange(EXPERTS, dtype=jnp.int32), axis=1).astype(bf16)
    own_query = lax.dynamic_slice_in_dim(w_query, own_sp * QW, QW, 1)
    own_up = lax.dynamic_slice_in_dim(w_kv_up, own_sp * KVW, KVW, 1)
    pack = jnp.concatenate(
        [
            own_query[:, :NOPE],
            own_query[:, QK : QK + NOPE],
            own_query[:, NOPE:QK],
            own_query[:, QK + NOPE :],
            w_kv_down,
            picks,
            attn_gain[:, None],
            ffn_gain[:, None],
            jnp.pad(kv_gain, (0, ROWS - kv_gain.shape[0]))[:, None],
            jnp.zeros((ROWS, 9), bf16),
            w_router,
            jnp.zeros((ROWS, 44), bf16),
            own_up.reshape(RANK // DP, 4, ROWS).transpose(1, 0, 2).reshape(ROWS, ROWS),
        ],
        axis=1,
    )
    cosine, sine = rope_tables()
    (
        resid_two,
        hidden_two,
        cot_all,
        _,
        gate_up,
        down,
        tok_all,
        weights,
        hidden_one,
        compressed,
        latent,
        queries,
        keys,
        values,
        head_out,
        out_w,
        misc,
        log_totals,
    ) = attention(
        tokens,
        pack,
        cotangent,
        shared_gate,
        expert_gate,
        shared_up,
        expert_up,
        shared_down,
        expert_down,
        w_out,
        cosine,
        sine,
    )
    gain_one, gain_two = misc[GAIN_ONE], misc[GAIN_TWO]
    latent_gain = misc[GAIN_KV].reshape(DP, ROWS)[:, : RANK // DP].reshape(RANK)
    router_t = misc[ROUTER_LANE : ROUTER_LANE + 16].astype(bf16)
    router_w = router_t[:EXPERTS]
    scale_two = inverse_rms(resid_two)

    hidden_grad, mixed_part, gate_up_grad, down_grad = experts(
        hidden_two, gate_up, router_t, down, cot_all, weights
    )
    prob_grad = hidden_grad[:, D + PICK_LANE : D + PICK_LANE + EXPERTS]
    hidden_grad = hidden_grad[:, :D]

    logits = nt(hidden_two, router_w)
    router = jax.nn.softmax(logits, axis=-1)
    prob_grad = prob_grad * picks.astype(f32)
    logit_grad = (
        router * (prob_grad - jnp.sum(router * prob_grad, axis=-1, keepdims=True))
    ).astype(bf16)
    hidden_grad = hidden_grad + nn(logit_grad, router_w)
    router_grad = tn(logit_grad, hidden_two)
    gain_two_grad = jnp.sum(hidden_grad * resid_two * scale_two, axis=0)
    upstream = cotangent.astype(f32)
    resid_two_grad = upstream + norm_back(resid_two, scale_two, gain_two, hidden_grad)
    proj_grad = resid_two_grad.astype(bf16)

    norm_rows = jnp.concatenate(
        [
            jnp.zeros((1, D), f32),
            gain_two_grad[None],
            jnp.zeros((1, D), f32),
            router_grad,
            jnp.zeros((1, D), f32),
        ]
    )
    hidden_one_grad, _, gu_total, dn_total, grads, _, out_grad = attention_grad(
        proj_grad,
        tok_all,
        weights,
        hidden_one,
        compressed,
        latent,
        queries,
        keys,
        values,
        head_out,
        out_w,
        misc,
        log_totals,
        gate_up_grad,
        down_grad,
        cosine,
        sine,
        norm_rows,
    )

    _, hidden_one_grad, mixed, grads, _, out_total = exchange(
        "sum_grads",
        6,
        [
            Scatter("dp", ROWS, PACK, bf16, spare=True, load=True),
            Scatter("sp", ROWS, D, load=True),
            Scatter("dp", ROWS, D, spare=True, load=True),
            Gather("sp", ROWS, PACK),
            Scatter("sp", 2 * ROWS // SP, D // 2, bf16),
            Gather("sp", 2 * ROWS // SP, D // 2),
        ],
        [grads, hidden_one_grad, mixed_part, out_grad],
        plan=[(0, 0), (1, 0), (4, 0), (0, 1), (4, 1), (1, 1), (0, 2), (0, 3), (2, 0), (4, 2), (4, 3)]
        + [(1, 2), (0, 4), (3, 0), (4, 4), (5, 0), (1, 3), (2, 1), (3, 1), (3, 2), (5, 1), (5, 2)]
        + [(2, 2), (2, 3), (1, 4), (3, 3), (5, 3), (2, 4), (3, 4), (5, 4)]
        + [(op, 5) for op in range(6)],
        chained=[(3, 0), (5, 4)],
    )
    gate_shared, up_shared, gate_routed, up_routed, down_shared, down_routed = unpack(
        gu_total.reshape(SP, DP, GU_PART, ROWS), dn_total
    )
    grads = grads.reshape(SP, ROWS, PACK)
    mixed = (resid_two + mixed).astype(bf16)
    resid_one = tokens.astype(f32)
    own_scale = inverse_rms(resid_one)
    tokens_grad = resid_two_grad + norm_back(resid_one, own_scale, gain_one, hidden_one_grad)
    tokens_grad = tokens_grad.astype(bf16)

    def side_by_side(block, width):
        return block.astype(f32).transpose(1, 0, 2).reshape(-1, SP * width)

    query_total = grads[:, :, :QW]
    query_total = jnp.concatenate(
        [
            query_total[:, :, :NOPE],
            query_total[:, :, 2 * NOPE : 2 * NOPE + ROPE],
            query_total[:, :, NOPE : 2 * NOPE],
            query_total[:, :, 2 * NOPE + ROPE :],
        ],
        axis=2,
    )
    query_total = side_by_side(query_total, QW)
    tail = jnp.sum(grads[:, :, QW:CORE_W].astype(f32), axis=0)
    down_total, tail = tail[:, : RANK + ROPE], tail[:, RANK + ROPE :]
    out_total = jnp.concatenate([out_total[:ROWS], out_total[ROWS:]], axis=1).astype(f32)
    up_total = grads[:, :, UP_AT:].reshape(SP, 4, RANK // DP, ROWS).transpose(0, 2, 1, 3)
    up_total = side_by_side(up_total.reshape(SP, RANK // DP, KVW), KVW)

    return (
        mixed,
        tokens_grad,
        tail[:, 0],
        query_total,
        down_total,
        tail[: RANK // DP, 2],
        up_total,
        out_total,
        tail[:, 1],
        tail[:, 3:7],
        gate_shared,
        up_shared,
        down_shared,
        gate_routed,
        up_routed,
        down_routed,
    )


def solution(mesh):
    rows = P(("dp", "sp"), None)
    vec, mat, cube = P("dp"), P("dp", None), P("dp", None, None)
    return jax.shard_map(
        per_device,
        mesh=mesh,
        in_specs=(rows, rows, rows, vec, mat, mat, vec, mat, mat, vec, mat) + (cube,) * 6,
        out_specs=(rows, rows, vec, mat, mat, vec, mat, mat, vec, mat) + (cube,) * 6,
        check_vma=False,
    )
```
